128 devices in a mesh: tok: 32 (over y, x_lo, z), rep: 4 (over x_hi, core).
Axes of the slice: x: 4 (x_hi: 2, x_lo: 2; x = x_hi * 2 + x_lo), y: 4, z: 4, core: 2. Of those that a mesh axis runs over, the one named last changes fastest.
Arguments:
- tokens: bfloat16 [65536, 768], P(('rep', 'tok')), parts along dimension 0, may hold values from -6 to 6
- attn_gain: bfloat16 [768], replicated, may hold values from 0.25 to 1.75
- qkv_weight: bfloat16 [768, 2304], replicated, may hold values from -0.21875 to 0.21875
- head_temp: float32 [12], replicated, may hold values from 2 to 600, as said below
- out_weight: bfloat16 [768, 768], replicated, may hold values from -0.21875 to 0.21875
- kv_weight: bfloat16 [768, 1536], replicated, may hold values from -0.21875 to 0.21875
- rate_weight: float32 [768, 2], replicated, may hold values from -0.21875 to 0.21875
- fast_weights: bfloat16 [768, 2304], replicated, may hold values from -0.3125 to 0.3125
- target: bfloat16 [32768, 768], P(('rep', 'tok')), parts along dimension 0, may hold values from -6 to 6
- query_weight: bfloat16 [768, 768], replicated, may hold values from -0.21875 to 0.21875
- merge_weight: bfloat16 [768, 768], replicated, may hold values from -0.21875 to 0.21875
- image_lengths: int32 [64], P('rep'), parts along dimension 0, may hold values from 512 to 1024, as said below
- target_counts: int32 [128], P(('rep', 'tok')), parts along dimension 0, may hold values from 64 to 256, as said below
Outputs:
- tokens_out: bfloat16 [65536, 768], P(('rep', 'tok')), parts along dimension 0
- fast_updated: bfloat16 [3072, 2304], P(('rep', 'tok')), parts along dimension 0
- target_out: bfloat16 [32768, 768], P(('rep', 'tok')), parts along dimension 0
The draws below stay inside these ranges and needn't reach their ends.
There are 4 independent parts, one for each index of `rep`. The reference program is written for one: setup_inputs(seed, part) draws one part's arguments, and reference() takes and returns one part's arrays. A program takes and returns all parts, laid end to end along the dimension named above; an argument that names none is the same for every part. Nothing has to cross between parts.
Inputs may be any that keep to these rules, and one draw needn't show every extreme that they name: `image_lengths`: every image has at least half of its 1024 slots valid, and some image of every scene is full. `target_counts`: some device of every scene uses all 256 slots. `head_temp`: positive score scales.
All inputs are finite; a program needn't handle non-finite values.
Results may differ from the reference program's by a relative error of at most 0.025.
The reference program's roundings to bfloat16 on the way count: a program that leaves them out, or rounds other values in their place, can miss the bound.
Values may be sent and summed in bfloat16 or wider, within the bound.
No kernel may reach another device: no remote copies, remote signals or barrier semaphores. Data moves between devices by JAX's collectives and lax.ppermute only.
A program may use at most 192 MiB of HBM per device.

```python
import math
import jax
import jax.numpy as jnp
from jax import lax

D = 768
HEADS = 12
HD = 64
FHEADS = 2
DH = 384
FH = 768
TGT_DEV = 256
SHARDS = 32
TOKENS = 16384
IMG_TOK = 1024
IMAGES = 16
TGT_TOK = 8192


def draw_head_temp(key, part):
    first = jax.random.fold_in(jax.random.fold_in(key, 7), 0)
    low = jnp.exp(jax.random.uniform(first, (HEADS,), jnp.float32, math.log(2.0), math.log(20.0)))
    return low


def draw_image_lengths(key, part):
    first, second = jax.random.split(jax.random.fold_in(key, 11))
    spans = jax.random.randint(first, (IMAGES,), IMG_TOK // 2, IMG_TOK + 1, dtype=jnp.int32)
    chosen = jax.random.randint(second, (), 0, IMAGES, dtype=jnp.int32)
    return jnp.where(jnp.arange(IMAGES, dtype=jnp.int32) == chosen, IMG_TOK, spans).astype(jnp.int32)


def draw_target_counts(key, part):
    first, second = jax.random.split(jax.random.fold_in(key, 13))
    counts = jax.random.randint(first, (SHARDS,), TGT_DEV // 4, TGT_DEV + 1, dtype=jnp.int32)
    chosen = jax.random.randint(second, (), 0, SHARDS, dtype=jnp.int32)
    return jnp.where(jnp.arange(SHARDS, dtype=jnp.int32) == chosen, TGT_DEV, counts).astype(jnp.int32)


def block_levels(rng, shape, shards, low, high):
    gain, own = 1.0, jax.random.fold_in(rng, 6)
    for axis_at, blocks in shards:
        draws = jnp.exp(jax.random.uniform(jax.random.fold_in(own, axis_at), (blocks,), jnp.float32, low / len(shards), high / len(shards)))
        gain = gain * jnp.repeat(draws, shape[axis_at] // blocks).reshape([-1 if axis == axis_at else 1 for axis in range(len(shape))])
    return gain


def scatter_about(key, shape, spread, bound, pieces=(), held_as=jnp.bfloat16):
    level = block_levels(key, shape, pieces, -0.22, 0.18) if pieces else 1.0
    entries = jax.random.normal(key, shape, jnp.float32) * spread * level
    return jnp.minimum(jnp.maximum(entries, -bound), bound).astype(held_as)


def setup_inputs(seed: int = 0, part: int = 0) -> dict:
    splits = jax.random.split(jax.random.key(seed), 14)
    part_keys = jax.random.split(jax.random.fold_in(splits[13], part), 14)
    tokens = scatter_about(part_keys[0], (TOKENS, D), 1.0, 6.0, ((0, 32),))
    attn_gain = jnp.clip(1.0 + 0.15 * jax.random.normal(splits[1], (D,), jnp.float32), 0.25, 1.75).astype(jnp.bfloat16)
    qkv_weight = scatter_about(splits[2], (D, 3 * D), D ** -0.5, 0.21875)
    head_temp = draw_head_temp(jax.random.fold_in(splits[13], 71), part)
    out_weight = scatter_about(splits[4], (D, D), D ** -0.5, 0.21875)
    kv_weight = scatter_about(splits[5], (D, 2 * D), D ** -0.5, 0.21875)
    rate_weight = scatter_about(splits[6], (D, FHEADS), D ** -0.5, 0.21875, (), jnp.float32)
    fast_weights = scatter_about(splits[7], (FH, 3 * D), DH ** -0.5, 0.3125)
    target = scatter_about(part_keys[8], (TGT_TOK, D), 1.0, 6.0, ((0, 32),))
    query_weight = scatter_about(splits[9], (D, D), D ** -0.5, 0.21875)
    merge_weight = scatter_about(splits[10], (D, D), D ** -0.5, 0.21875)
    image_lengths = draw_image_lengths(jax.random.fold_in(jax.random.fold_in(splits[13], part), 71), part)
    target_counts = draw_target_counts(jax.random.fold_in(jax.random.fold_in(splits[13], part), 71), part)
    return {"tokens": tokens, "attn_gain": attn_gain, "qkv_weight": qkv_weight, "head_temp": head_temp, "out_weight": out_weight, "kv_weight": kv_weight, "rate_weight": rate_weight, "fast_weights": fast_weights, "target": target, "query_weight": query_weight, "merge_weight": merge_weight, "image_lengths": image_lengths, "target_counts": target_counts}


eps = 1e-06
rate_base = 4.0

def unit_rows(values):
    values = values.astype(jnp.float32)
    return values * lax.rsqrt(lax.optimization_barrier(jnp.mean(values * values, axis=-1, keepdims=True)) + eps)

def image_attention(inputs):
    block, length, temps = inputs
    query = unit_rows(block[:, 0]).astype(jnp.bfloat16)
    keyset = unit_rows(block[:, 1]).astype(jnp.bfloat16)
    valueset = block[:, 2]
    scores = jnp.einsum('qhd,khd->hqk', query.astype(jnp.float32), keyset.astype(jnp.float32))
    scores = scores * (temps / HD)[:, None, None]
    valid = jnp.arange(IMG_TOK, dtype=jnp.int32) < length
    scores = jnp.where(valid[None, None, :], scores, -1e+30)
    top = lax.optimization_barrier(jnp.max(scores, axis=-1, keepdims=True))
    expo = jnp.exp(scores - top)
    weights = (expo / lax.optimization_barrier(jnp.sum(expo, axis=-1, keepdims=True))).astype(jnp.bfloat16)
    result = jnp.einsum('hqk,khd->qhd', weights.astype(jnp.float32), valueset.astype(jnp.float32))
    return result.astype(jnp.bfloat16)

def reference(tokens, attn_gain, qkv_weight, head_temp, out_weight, kv_weight, rate_weight, fast_weights, target, query_weight, merge_weight, image_lengths, target_counts):
    inputs = tokens.astype(jnp.float32)
    normed = (unit_rows(inputs) * attn_gain.astype(jnp.float32)).astype(jnp.bfloat16)
    qkv = jnp.dot(normed, qkv_weight, preferred_element_type=jnp.float32).astype(jnp.bfloat16)
    qkv = qkv.reshape(IMAGES, IMG_TOK, 3, HEADS, HD)
    temps = jnp.broadcast_to(head_temp, (IMAGES, HEADS))
    attn = lax.map(image_attention, (qkv, image_lengths, temps)).reshape(TOKENS, D)
    tokens_out = (inputs + jnp.dot(attn, out_weight, preferred_element_type=jnp.float32)).astype(jnp.bfloat16)
    kv = jnp.dot(tokens_out, kv_weight, preferred_element_type=jnp.float32)
    position = jnp.arange(TOKENS, dtype=jnp.int32)
    valid = position % IMG_TOK < image_lengths[position // IMG_TOK]
    logit = jnp.dot(tokens_out.astype(jnp.float32), rate_weight, precision=lax.Precision.HIGHEST)
    rate = jax.nn.softplus(logit + 1.0) * (rate_base / TOKENS) * valid[:, None].astype(jnp.float32)
    blocks = []
    for head in range(FHEADS):
        keys = unit_rows(kv[:, head * DH:(head + 1) * DH]).astype(jnp.bfloat16)
        values = kv[:, D + head * DH:D + (head + 1) * DH]
        base = 3 * head * DH
        gate_w = fast_weights[:, base:base + DH]
        up_w = fast_weights[:, base + DH:base + 2 * DH]
        down_w = fast_weights[:, base + 2 * DH:base + 3 * DH]
        act_a = jnp.dot(keys, gate_w.T, preferred_element_type=jnp.float32)
        act_b = jnp.dot(keys, up_w.T, preferred_element_type=jnp.float32)
        hidden = (jax.nn.silu(act_a) * act_b).astype(jnp.bfloat16)
        push = (-rate[:, head:head + 1] * values).astype(jnp.bfloat16)
        back_h = jnp.dot(push, down_w.T, preferred_element_type=jnp.float32)
        sigma = jax.nn.sigmoid(act_a)
        grad_a = (back_h * act_b * sigma * (1.0 + act_a * (1.0 - sigma))).astype(jnp.bfloat16)
        grad_b = (back_h * jax.nn.silu(act_a)).astype(jnp.bfloat16)
        blocks.append(jnp.dot(grad_a.T, keys, preferred_element_type=jnp.float32))
        blocks.append(jnp.dot(grad_b.T, keys, preferred_element_type=jnp.float32))
        blocks.append(jnp.dot(hidden.T, push, preferred_element_type=jnp.float32))
    grad = jnp.concatenate(blocks, axis=1)
    start_w = fast_weights.astype(jnp.float32).reshape(FH, 3 * FHEADS, DH)
    update = start_w - grad.reshape(FH, 3 * FHEADS, DH)
    fresh = update * jnp.sqrt(lax.optimization_barrier(jnp.mean(start_w * start_w, axis=-1, keepdims=True)) + eps) * lax.rsqrt(lax.optimization_barrier(jnp.mean(update * update, axis=-1, keepdims=True)) + eps)
    fast_updated = fresh.reshape(FH, 3 * D).astype(jnp.bfloat16)
    tq = jnp.dot(target, query_weight, preferred_element_type=jnp.float32)
    outs = []
    for head in range(FHEADS):
        qfast = unit_rows(tq[:, head * DH:(head + 1) * DH]).astype(jnp.bfloat16)
        base = 3 * head * DH
        act_a = jnp.dot(qfast, fast_updated[:, base:base + DH].T, preferred_element_type=jnp.float32)
        act_b = jnp.dot(qfast, fast_updated[:, base + DH:base + 2 * DH].T, preferred_element_type=jnp.float32)
        hidden_t = (jax.nn.silu(act_a) * act_b).astype(jnp.bfloat16)
        fout = jnp.dot(hidden_t, fast_updated[:, base + 2 * DH:base + 3 * DH], preferred_element_type=jnp.float32)
        outs.append(unit_rows(fout).astype(jnp.bfloat16))
    fout = jnp.concatenate(outs, axis=1)
    merged = target.astype(jnp.float32) + jnp.dot(fout, merge_weight, preferred_element_type=jnp.float32)
    slot = jnp.arange(TGT_TOK, dtype=jnp.int32)
    used = slot % TGT_DEV < target_counts[slot // TGT_DEV]
    target_out = jnp.where(used[:, None], merged, 0.0).astype(jnp.bfloat16)
    return (tokens_out, fast_updated, target_out)
```

```python
import functools
import math

import jax
import jax.numpy as jnp
from jax import lax
from jax.experimental import pallas as pl
from jax.experimental.pallas import tpu as pltpu
from jax.sharding import PartitionSpec as P

eps = 1e-06
rate_base = 4.0
safe_temp = 60.0
bf16 = jnp.bfloat16
f32 = jnp.float32

pair_mask = 1
reduce_orders = ((3, 4, 8, 24), (8, 24, 3, 4))


def swap(value, mask):
    pairs = [(source, source ^ mask) for source in range(lax.axis_size("tok"))]
    return lax.ppermute(value, "tok", pairs)


def params(mib, *semantics):
    return pltpu.CompilerParams(vmem_limit_bytes=mib * 2**20)


def nn(a, b):
    return lax.dot_general(a, b, (((1,), (0,)), ((), ())), preferred_element_type=f32)


def nt(a, b):
    return lax.dot_general(a, b, (((1,), (1,)), ((), ())), preferred_element_type=f32)


def whole(shape):
    return pl.BlockSpec(shape, lambda *_: (0,) * len(shape))


smem = pl.BlockSpec(memory_space=pltpu.SMEM)


def gather_kernel(index_ref, rows_ref, out_ref, sems):
    copies = []
    heads, blocks = index_ref.shape
    width = out_ref.shape[-1]
    for head in range(heads):
        for block in range(blocks):
            copies.append(
                pltpu.make_async_copy(
                    rows_ref.at[index_ref[head, block], :, pl.ds(head * width, width)],
                    out_ref.at[head, block],
                    sems.at[head, block],
                )
            )
    for copy in copies:
        copy.start()
    for copy in copies:
        copy.wait()


def gather_rows(index, rows):
    heads, blocks = index.shape
    _, height, width = rows.shape
    return pl.pallas_call(
        gather_kernel,
        out_shape=jax.ShapeDtypeStruct((heads, blocks, height, width // heads), rows.dtype),
        in_specs=[smem, pl.BlockSpec(memory_space=pl.ANY)],
        out_specs=pl.BlockSpec(memory_space=pl.ANY),
        scratch_shapes=[pltpu.SemaphoreType.DMA((heads, blocks))],
        name="gather_rows",
    )(index, rows)


def qkv_kernel(valid_ref, tok_ref, gain_ref, scale_ref, wq_ref, wk_ref, wv_ref, q_ref, k_ref, v_ref, normed):
    @pl.when(pl.program_id(0) == 0)
    def _():
        x = tok_ref[...].astype(f32)
        unit = x * lax.rsqrt(jnp.mean(x * x, axis=-1, keepdims=True) + eps)
        normed[...] = (unit * gain_ref[...].astype(f32)).astype(bf16)

    rows = normed[...]
    count, cols = q_ref.shape[0], wq_ref.shape[1]
    low = lax.broadcasted_iota(jnp.int32, (count, 128), 1) < 64
    same = lax.broadcasted_iota(jnp.int32, (cols, cols), 0) >> 6 == lax.broadcasted_iota(jnp.int32, (cols, cols), 1) >> 6
    ones = jnp.where(same, 1.0, 0.0).astype(bf16)

    def unit_heads(t):
        square = t * t
        high = square.astype(bf16)
        rest = (square - high.astype(f32)).astype(bf16)
        total = nn(high, ones) + nn(rest, ones)
        return (t * lax.rsqrt(total * (1.0 / 64.0) + eps)).astype(bf16).astype(f32)

    query = unit_heads(nn(rows, wq_ref[...]).astype(bf16).astype(f32)) * scale_ref[...]
    q_high = query.astype(bf16).astype(f32)
    q_rest = query - q_high
    key = unit_heads(nn(rows, wk_ref[...]).astype(bf16).astype(f32))
    value = nn(rows, wv_ref[...])
    live = lax.broadcasted_iota(jnp.int32, (count, 128), 0) < valid_ref[0]
    for tile in range(cols // 128):
        part = slice(tile * 128, tile * 128 + 128)
        even = slice(tile * 256, tile * 256 + 128)
        odd = slice(tile * 256 + 128, tile * 256 + 256)
        moved = pltpu.roll(q_rest[:, part], 64, 1)
        q_ref[:, even] = jnp.where(low, q_high[:, part], moved).astype(bf16)
        q_ref[:, odd] = jnp.where(low, moved, q_high[:, part]).astype(bf16)
        moved = pltpu.roll(key[:, part], 64, 1)
        k_ref[:, even] = jnp.where(low, key[:, part], moved).astype(bf16)
        k_ref[:, odd] = jnp.where(low, moved, key[:, part]).astype(bf16)
        shown = jnp.where(live, value[:, part], 0.0)
        one = jnp.where(live, 1.0, 0.0)
        v_ref[:, even] = jnp.where(low, shown, one).astype(bf16)
        v_ref[:, odd] = jnp.where(low, one, shown).astype(bf16)


def project_qkv(valid, tokens, gain, scale, weight):
    count, width = tokens.shape
    cols = 256
    steps = width // cols
    out = jax.ShapeDtypeStruct((count, 2 * width), bf16)
    return pl.pallas_call(
        qkv_kernel,
        grid=(steps,),
        out_shape=(out, out, out),
        in_specs=[
            smem,
            whole((count, width)),
            whole((1, width)),
            pl.BlockSpec((1, cols), lambda i: (0, i)),
            pl.BlockSpec((width, cols), lambda i: (0, i)),
            pl.BlockSpec((width, cols), lambda i: (0, steps + i)),
            pl.BlockSpec((width, cols), lambda i: (0, 2 * steps + i)),
        ],
        out_specs=[pl.BlockSpec((count, 2 * cols), lambda i: (0, i))] * 3,
        scratch_shapes=[pltpu.VMEM((count, width), bf16)],
        compiler_params=params(32),
        name="project_qkv",
    )(valid, tokens, gain, scale, weight, weight, weight)


def attend_kernel(valid_ref, temp_ref, q0_ref, q1_ref, k0_ref, k1_ref, v0_ref, v1_ref, out_ref):
    pair = pl.program_id(0)
    count = q0_ref.shape[0]
    block = 256
    low = lax.broadcasted_iota(jnp.int32, (block, 128), 1) < 64
    spot = lax.broadcasted_iota(jnp.int32, (block, count), 1)

    def fill(weigh):
        for side, q_ref in enumerate((q0_ref, q1_ref)):
            for first in range(0, count, block):
                sums = []
                for head in range(2):
                    lanes = slice(head * 128, head * 128 + 128)
                    q = q_ref[first : first + block, lanes]
                    p0, p1 = weigh(nt(q, k0_ref[:, lanes]), nt(q, k1_ref[:, lanes]))
                    sums.append(nn(p0, v0_ref[:, lanes]) + nn(p1, v1_ref[:, lanes]))
                top = jnp.where(low, sums[0], sums[1])
                bottom = pltpu.roll(jnp.where(low, sums[1], sums[0]), 64, 1)
                start = side * count + first
                out_ref[start : start + block, :] = (top / bottom).astype(bf16)

    plain = jnp.maximum(temp_ref[2 * pair], temp_ref[2 * pair + 1]) <= safe_temp

    @pl.when(plain)
    def _():
        fill(lambda s0, s1: (jnp.exp2(s0).astype(bf16), jnp.exp2(s1).astype(bf16)))

    @pl.when(jnp.logical_not(plain))
    def _():
        def weigh(s0, s1):
            s0 = jnp.where(spot < valid_ref[0], s0, -1e30)
            s1 = jnp.where(spot < valid_ref[1], s1, -1e30)
            top = jnp.max(jnp.maximum(s0, s1), axis=-1, keepdims=True)
            return jnp.exp2(s0 - top).astype(bf16), jnp.exp2(s1 - top).astype(bf16)

        fill(weigh)


def attend(valid, temps, q0, q1, k0, k1, v0, v1):
    count, width = q0.shape
    block = pl.BlockSpec((count, 256), lambda i: (0, i))
    return pl.pallas_call(
        attend_kernel,
        grid=(width // 256,),
        out_shape=jax.ShapeDtypeStruct((2 * count, width // 2), bf16),
        in_specs=[smem, smem] + [block] * 6,
        out_specs=pl.BlockSpec((2 * count, 128), lambda i: (0, i)),
        compiler_params=params(32),
        name="attend",
    )(valid, temps, q0, q1, k0, k1, v0, v1)


def push_kernel(scale, valid_ref, attn_ref, t0_ref, t1_ref, wo_ref, wkv_ref, r0_ref, r1_ref, r2_ref, out_ref, key_ref, push_ref):
    side = pl.program_id(0)
    count, width = t0_ref.shape
    before = jnp.where(side == 0, t0_ref[...], t1_ref[...]).astype(f32)
    after = (before + nn(attn_ref[...], wo_ref[...])).astype(bf16)

    @pl.when(side == 0)
    def _():
        out_ref[...] = after

    kv = nn(after, wkv_ref[...])
    logit = nn(after, r0_ref[...]) + nn(after, r1_ref[...]) + nn(after, r2_ref[...])
    high = logit + 1.0
    soft = jnp.maximum(high, 0.0) + jnp.log1p(jnp.exp(-jnp.abs(high)))
    live = lax.broadcasted_iota(jnp.int32, logit.shape, 0) < valid_ref[side]
    rate = jnp.where(live, soft * scale, 0.0)
    heads = logit.shape[1] // 128
    size = width // heads
    for head in range(heads):
        part = slice(head * size, head * size + size)
        key = kv[:, part]
        inv = lax.rsqrt(jnp.mean(key * key, axis=-1, keepdims=True) + eps)
        key_ref[:, part] = (key * inv).astype(bf16)
        for tile in range(size // 128):
            at = head * size + tile * 128
            value = kv[:, width + at : width + at + 128]
            push_ref[:, at : at + 128] = (-rate[:, head * 128 : head * 128 + 128] * value).astype(bf16)


def make_pushes(scale, valid, attn, t0, t1, wo, wkv, rates):
    count, width = t0.shape
    both = jax.ShapeDtypeStruct((2 * count, width), bf16)
    block = pl.BlockSpec((count, width), lambda i: (i, 0))
    return pl.pallas_call(
        functools.partial(push_kernel, scale),
        grid=(2,),
        out_shape=(jax.ShapeDtypeStruct((count, width), bf16), both, both),
        in_specs=[
            smem,
            block,
            whole((count, width)),
            whole((count, width)),
            whole(wo.shape),
            whole(wkv.shape),
        ]
        + [whole(rates[0].shape)] * 3,
        out_specs=[whole((count, width)), block, block],
        compiler_params=params(40),
        name="make_pushes",
    )(valid, attn, t0, t1, wo, wkv, *rates)


def grad_kernel(w_ref, key_ref, push_ref, out_ref):
    size = key_ref.shape[1]
    key, push = key_ref[...], push_ref[...]
    act_a = nt(w_ref[0, :, :size], key)
    act_b = nt(w_ref[0, :, size : 2 * size], key)
    back = nt(w_ref[0, :, 2 * size :], push)
    sigma = 1.0 / (1.0 + jnp.exp(-act_a))
    silu = act_a * sigma
    hidden = (silu * act_b).astype(bf16)
    grad_a = (back * act_b * sigma * (1.0 + act_a * (1.0 - sigma))).astype(bf16)
    grad_b = (back * silu).astype(bf16)
    out_ref[:, :size] = nn(grad_a, key).astype(out_ref.dtype)
    out_ref[:, size : 2 * size] = nn(grad_b, key).astype(out_ref.dtype)
    out_ref[:, 2 * size :] = nn(hidden, push).astype(out_ref.dtype)


def gradient(weights, keys, pushes, head, half, kind):
    _, rows, cols = weights.shape
    count = keys.shape[0]
    size = cols // 3
    column = pl.BlockSpec((count, size), lambda i: (0, head))
    return pl.pallas_call(
        grad_kernel,
        grid=(1,),
        out_shape=jax.ShapeDtypeStruct((rows // 2, cols), kind),
        in_specs=[pl.BlockSpec((1, rows // 2, cols), lambda i: (head, half, 0)), column, column],
        out_specs=whole((rows // 2, cols)),
        compiler_params=params(32),
        name="gradient",
    )(weights, keys, pushes)


def rescale_kernel(start_ref, mine_ref, theirs_ref, out_ref):
    size = start_ref.shape[1] // 3
    grad = mine_ref[...] + theirs_ref[...].astype(f32)
    for block in range(3):
        part = slice(block * size, block * size + size)
        start = start_ref[:, part].astype(f32)
        update = start - grad[:, part]
        before = jnp.sqrt(jnp.mean(start * start, axis=-1, keepdims=True) + eps)
        after = lax.rsqrt(jnp.mean(update * update, axis=-1, keepdims=True) + eps)
        out_ref[:, part] = (update * before * after).astype(bf16)


def rescale(start, mine, theirs):
    return pl.pallas_call(
        rescale_kernel,
        grid=(1,),
        out_shape=jax.ShapeDtypeStruct(start.shape, bf16),
        in_specs=[whole(start.shape)] * 3,
        out_specs=whole(start.shape),
        compiler_params=params(8),
        name="rescale",
    )(start, mine, theirs)


def query_kernel(t0_ref, t1_ref, w_ref, out_ref):
    side = pl.program_id(0)
    width = t0_ref.shape[1]
    size = width // 2
    tq = nn(jnp.where(side == 0, t0_ref[...], t1_ref[...]), w_ref[...])
    for head in range(2):
        part = slice(head * size, head * size + size)
        q = tq[:, part]
        out_ref[:, part] = (q * lax.rsqrt(jnp.mean(q * q, axis=-1, keepdims=True) + eps)).astype(bf16)


def target_queries(t0, t1, weight):
    count, width = t0.shape
    return pl.pallas_call(
        query_kernel,
        grid=(2,),
        out_shape=jax.ShapeDtypeStruct((2 * count, width), bf16),
        in_specs=[whole((count, width))] * 2 + [whole(weight.shape)],
        out_specs=pl.BlockSpec((count, width), lambda i: (i, 0)),
        compiler_params=params(16),
        name="target_queries",
    )(t0, t1, weight)


def apply_rows(q, w_ref):
    size = q.shape[1]
    act_a = nt(q, w_ref[:, :size])
    act_b = nt(q, w_ref[:, size : 2 * size])
    hidden = (act_a / (1.0 + jnp.exp(-act_a)) * act_b).astype(bf16)
    return nn(hidden, w_ref[:, 2 * size :])


def first_kernel(q_ref, w_ref, out_ref):
    out_ref[...] = apply_rows(q_ref[...], w_ref)


def apply_first(queries, weights, head):
    count = queries.shape[0]
    size = weights.shape[1] // 3
    return pl.pallas_call(
        first_kernel,
        grid=(1,),
        out_shape=jax.ShapeDtypeStruct((count, size), f32),
        in_specs=[pl.BlockSpec((count, size), lambda i: (0, head)), whole(weights.shape)],
        out_specs=whole((count, size)),
        compiler_params=params(16),
        name="apply_first",
    )(queries, weights)


def last_kernel(q_ref, w_ref, sum_ref, mine_ref, theirs_ref):
    count = mine_ref.shape[0]
    total = sum_ref[...] + apply_rows(q_ref[...], w_ref)
    mine_ref[...] = total[:count]
    theirs_ref[...] = total[count:].astype(bf16)


def apply_last(queries, weights, total, head):
    count = queries.shape[0]
    size = weights.shape[1] // 3
    return pl.pallas_call(
        last_kernel,
        grid=(1,),
        out_shape=(
            jax.ShapeDtypeStruct((count // 2, size), f32),
            jax.ShapeDtypeStruct((count // 2, size), bf16),
        ),
        in_specs=[
            pl.BlockSpec((count, size), lambda i: (0, head)),
            whole(weights.shape),
            whole((count, size)),
        ],
        out_specs=[whole((count // 2, size))] * 2,
        compiler_params=params(16),
        name="apply_last",
    )(queries, weights, total)


def merge_kernel(used_ref, target_ref, w_ref, m0_ref, m1_ref, r0_ref, r1_ref, out_ref):
    size = m0_ref.shape[1]
    total = target_ref[...].astype(f32)
    for head, (mine, theirs) in enumerate(((m0_ref, r0_ref), (m1_ref, r1_ref))):
        fout = mine[...] + theirs[...].astype(f32)
        unit = (fout * lax.rsqrt(jnp.mean(fout * fout, axis=-1, keepdims=True) + eps)).astype(bf16)
        total = total + nn(unit, w_ref[head * size : head * size + size, :])
    live = lax.broadcasted_iota(jnp.int32, total.shape, 0) < used_ref[0]
    out_ref[...] = jnp.where(live, total, 0.0).astype(bf16)


def merge(used, target, weight, mine, theirs):
    return pl.pallas_call(
        merge_kernel,
        grid=(1,),
        out_shape=jax.ShapeDtypeStruct(target.shape, bf16),
        in_specs=[smem, whole(target.shape), whole(weight.shape)] + [whole(mine[0].shape)] * 4,
        out_specs=whole(target.shape),
        compiler_params=params(16),
        name="merge",
    )(used, target, weight, *mine, *theirs)


def split_weight(value):
    parts = []
    for _ in range(3):
        part = lax.reduce_precision(value, 8, 7)
        parts.append(part.astype(bf16))
        value = value - part
    return parts


def body(
    tokens,
    attn_gain,
    qkv_weight,
    head_temp,
    out_weight,
    kv_weight,
    rate_weight,
    fast_weights,
    target,
    query_weight,
    merge_weight,
    image_lengths,
    target_counts,
):
    tok_rows, width = tokens.shape
    devices = lax.axis_size("tok")
    place = lax.axis_index("tok")
    parity = place % 2
    head_dim = width // head_temp.shape[0]
    fast_hidden, fast_cols = fast_weights.shape
    fast_heads = rate_weight.shape[1]
    rows = fast_hidden // devices
    image_ids = jnp.arange(image_lengths.shape[0], dtype=jnp.int32)
    length = jnp.sum(jnp.where(image_ids == place // 2, image_lengths, 0))
    valid = jnp.stack([length - parity * tok_rows, length - (1 - parity) * tok_rows]).astype(jnp.int32)

    arrived = swap(tokens, pair_mask)

    scale = jnp.repeat(head_temp * (math.log2(math.e) / head_dim), head_dim)[None, :]
    gain = attn_gain[None, :]
    q0, k0, v0 = project_qkv(valid[:1], tokens, gain, scale, qkv_weight)

    moves = []
    for order in reduce_orders:
        span = [0]
        for mask in reversed(order):
            span = span + [mask ^ at for at in span]
        moves.append(span)
    index = place ^ jnp.array(moves, dtype=jnp.int32)
    start = gather_rows(index, fast_weights.reshape(devices, rows, fast_cols))
    weights = start.reshape(fast_heads, len(moves[0]) * rows, fast_cols // fast_heads)
    rates = [
        jnp.broadcast_to(part[:, :, None], part.shape + (128,)).reshape(width, fast_heads * 128)
        for part in split_weight(rate_weight)
    ]

    arrived, target_sent = lax.optimization_barrier((arrived, target))
    other_target = swap(target_sent, pair_mask)
    q1, k1, v1 = project_qkv(valid[1:], arrived, gain, scale, qkv_weight)
    attn = attend(valid, head_temp, q0, q1, k0, k1, v0, v1)
    tokens_out, keys, pushes = make_pushes(
        rate_base / (tok_rows * devices), valid, attn, tokens, arrived, out_weight, kv_weight, rates
    )

    sent = [gradient(weights, keys, pushes, head, 1, bf16) for head in range(fast_heads)]
    kept = [gradient(weights, keys, pushes, head, 0, f32) for head in range(fast_heads)]
    for step in range(len(reduce_orders[0])):
        got = [swap(sent[head], reduce_orders[head][step]) for head in range(fast_heads)]
        if step < len(reduce_orders[0]) - 1:
            half = kept[0].shape[0] // 2
            total = [kept[head] + got[head].astype(f32) for head in range(fast_heads)]
            kept = [part[:half] for part in total]
            sent = [part[half:].astype(bf16) for part in total]
    fresh = [rescale(start[head, 0], kept[head], got[head]) for head in range(fast_heads)]

    queries = target_queries(target, other_target, query_weight)
    held = list(fresh)
    steps = len(reduce_orders[0])
    for step in range(steps - 1):
        got = [swap(held[head], reduce_orders[head][steps - 1 - step]) for head in range(fast_heads)]
        held = [jnp.concatenate([held[head], got[head]], axis=0) for head in range(fast_heads)]
    got = [swap(held[head], reduce_orders[head][0]) for head in range(fast_heads)]
    mine, theirs = [], []
    totals = [apply_first(queries, held[head], head) for head in range(fast_heads)]
    for head in range(fast_heads):
        own, other = apply_last(queries, got[head], totals[head], head)
        mine.append(own)
        theirs.append(swap(other, pair_mask))
    target_out = merge(target_counts, target, merge_weight, mine, theirs)
    return (tokens_out, jnp.concatenate(fresh, axis=1), target_out)


def solution(mesh):
    placed = (
        P(("rep", "tok"), None),
        P(),
        P(),
        P(),
        P(),
        P(),
        P(),
        P(),
        P(("rep", "tok"), None),
        P(),
        P(),
        P("rep"),
        P(("rep", "tok")),
    )
    return jax.shard_map(
        body,
        mesh=mesh,
        in_specs=placed,
        out_specs=(P(("rep", "tok"), None), P(("rep", "tok"), None), P(("rep", "tok"), None)),
        check_vma=False,
    )
```

```python
import functools
import math

import jax
import jax.numpy as jnp
from jax import lax
from jax.experimental import pallas as pl
from jax.experimental.pallas import tpu as pltpu
from jax.sharding import PartitionSpec as P

eps = 1e-06
rate_base = 4.0
safe_temp = 60.0
bf16 = jnp.bfloat16
f32 = jnp.float32

pair_mask = 1
reduce_orders = ((3, 4, 8, 24), (24, 8, 3, 4))
split = 640


def swap(value, mask):
    pairs = [(source, source ^ mask) for source in range(lax.axis_size("tok"))]
    return lax.ppermute(value, "tok", pairs)


def params(mib):
    return pltpu.CompilerParams(vmem_limit_bytes=mib * 2**20)


def nn(a, b):
    return lax.dot_general(a, b, (((1,), (0,)), ((), ())), preferred_element_type=f32)


def nt(a, b):
    return lax.dot_general(a, b, (((1,), (1,)), ((), ())), preferred_element_type=f32)


def whole(shape):
    return pl.BlockSpec(shape, lambda *_: (0,) * len(shape))


smem = pl.BlockSpec(memory_space=pltpu.SMEM)


def gather_kernel(index_ref, rows_ref, out_ref):
    heads, blocks = index_ref.shape
    width = out_ref.shape[-1]
    for head in range(heads):
        for block in range(blocks):
            out_ref[head, block] = rows_ref[index_ref[head, block], :, head * width : head * width + width]


def gather_rows(index, rows):
    heads, blocks = index.shape
    _, height, width = rows.shape
    shape = (heads, blocks, height, width // heads)
    return pl.pallas_call(
        gather_kernel,
        grid=(1,),
        out_shape=jax.ShapeDtypeStruct(shape, rows.dtype),
        in_specs=[smem, whole(rows.shape)],
        out_specs=whole(shape),
        compiler_params=params(24),
        name="gather_rows",
    )(index, rows)


def qkv_kernel(valid_ref, tok_ref, gain_ref, scale_ref, wq_ref, wk_ref, wv_ref, q_ref, k_ref, v_ref, normed):
    @pl.when(pl.program_id(0) == 0)
    def _():
        x = tok_ref[...].astype(f32)
        unit = x * lax.rsqrt(jnp.mean(x * x, axis=-1, keepdims=True) + eps)
        normed[...] = (unit * gain_ref[...].astype(f32)).astype(bf16)

    rows = normed[...]
    count, cols = q_ref.shape[0], wq_ref.shape[1]
    low = lax.broadcasted_iota(jnp.int32, (count, 128), 1) < 64

    def unit_heads(t):
        square = t * t
        first = jnp.sum(jnp.where(low, square, 0.0), axis=-1, keepdims=True)
        second = jnp.sum(jnp.where(low, 0.0, square), axis=-1, keepdims=True)
        inv = [lax.rsqrt(total * (1.0 / 64.0) + eps) for total in (first, second)]
        return (t * jnp.where(low, inv[0], inv[1])).astype(bf16).astype(f32)

    query = nn(rows, wq_ref[...]).astype(bf16).astype(f32)
    key = nn(rows, wk_ref[...]).astype(bf16).astype(f32)
    value = nn(rows, wv_ref[...])
    live = lax.broadcasted_iota(jnp.int32, (count, 128), 0) < valid_ref[0]
    one = jnp.where(live, 1.0, 0.0)
    for tile in range(cols // 128):
        part = slice(tile * 128, tile * 128 + 128)
        even = slice(tile * 256, tile * 256 + 128)
        odd = slice(tile * 256 + 128, tile * 256 + 256)
        q = unit_heads(query[:, part]) * scale_ref[:, part]
        q_high = q.astype(bf16).astype(f32)
        moved = pltpu.roll(q - q_high, 64, 1)
        q_ref[:, even] = jnp.where(low, q_high, moved).astype(bf16)
        q_ref[:, odd] = jnp.where(low, moved, q_high).astype(bf16)
        k = unit_heads(key[:, part])
        moved = pltpu.roll(k, 64, 1)
        k_ref[:, even] = jnp.where(low, k, moved).astype(bf16)
        k_ref[:, odd] = jnp.where(low, moved, k).astype(bf16)
        shown = jnp.where(live, value[:, part], 0.0)
        v_ref[:, even] = jnp.where(low, shown, one).astype(bf16)
        v_ref[:, odd] = jnp.where(low, one, shown).astype(bf16)


def project_qkv(valid, tokens, gain, scale, weight):
    count, width = tokens.shape
    cols = 256
    steps = width // cols
    out = jax.ShapeDtypeStruct((count, 2 * width), bf16)
    return pl.pallas_call(
        qkv_kernel,
        grid=(steps,),
        out_shape=(out, out, out),
        in_specs=[
            smem,
            whole((count, width)),
            whole((1, width)),
            pl.BlockSpec((1, cols), lambda i: (0, i)),
            pl.BlockSpec((width, cols), lambda i: (0, i)),
            pl.BlockSpec((width, cols), lambda i: (0, steps + i)),
            pl.BlockSpec((width, cols), lambda i: (0, 2 * steps + i)),
        ],
        out_specs=[pl.BlockSpec((count, 2 * cols), lambda i: (0, i))] * 3,
        scratch_shapes=[pltpu.VMEM((count, width), bf16)],
        compiler_params=params(32),
        name="project_qkv",
    )(valid, tokens, gain, scale, weight, weight, weight)


def head_lanes(head):
    return slice(head * 128, head * 128 + 128)


def weighted(q, keys, values, lanes):
    total = None
    for k_ref, v_ref in zip(keys, values):
        part = nn(jnp.exp2(nt(q, k_ref[:, lanes])).astype(bf16), v_ref[:, lanes])
        total = part if total is None else total + part
    return total


def finish(sums, out_ref, start):
    count = sums[0].shape[0]
    low = lax.broadcasted_iota(jnp.int32, (count, 128), 1) < 64
    top = jnp.where(low, sums[0], sums[1])
    bottom = pltpu.roll(jnp.where(low, sums[1], sums[0]), 64, 1)
    out_ref[start : start + count, :] = (top / bottom).astype(bf16)


def is_plain(temp_ref):
    pair = pl.program_id(0)
    return jnp.maximum(temp_ref[2 * pair], temp_ref[2 * pair + 1]) <= safe_temp


def first_stage(temp_ref, q0, k0, v0, a0):
    @pl.when(is_plain(temp_ref))
    def _():
        for head in range(2):
            lanes = head_lanes(head)
            a0[:, lanes] = weighted(q0[:, lanes], [k0], [v0], lanes)


def second_stage(temp_ref, q0, k0, v0, q1, k1, v1, b0, a0, a1):
    @pl.when(is_plain(temp_ref))
    def _():
        for head in range(2):
            lanes = head_lanes(head)
            a0[:, lanes] = b0[:, lanes] + weighted(q0[:, lanes], [k1], [v1], lanes)
            a1[:, lanes] = weighted(q1[:, lanes], [k0, k1], [v0, v1], lanes)


def third_stage(valid_ref, temp_ref, q0, k0, v0, q1, k1, v1, q2, k2, v2, a0, a1, out_ref):
    starts = (0, q0.shape[0], q0.shape[0] + q1.shape[0])
    keys, values = [k0, k1, k2], [v0, v1, v2]

    @pl.when(is_plain(temp_ref))
    def _():
        for q_ref, a_ref, start in zip((q0, q1), (a0, a1), starts):
            finish(
                [
                    a_ref[:, head_lanes(head)] + weighted(q_ref[:, head_lanes(head)], [k2], [v2], head_lanes(head))
                    for head in range(2)
                ],
                out_ref,
                start,
            )
        finish([weighted(q2[:, head_lanes(head)], keys, values, head_lanes(head)) for head in range(2)], out_ref, starts[2])

    @pl.when(jnp.logical_not(is_plain(temp_ref)))
    def _():
        for q_ref, start in zip((q0, q1, q2), starts):
            for first in range(0, q_ref.shape[0], 256):
                sums = []
                for head in range(2):
                    lanes = head_lanes(head)
                    scores = []
                    for at, k_ref in enumerate(keys):
                        score = nt(q_ref[first : first + 256, lanes], k_ref[:, lanes])
                        spot = lax.broadcasted_iota(jnp.int32, score.shape, 1)
                        scores.append(jnp.where(spot < valid_ref[at], score, -1e30))
                    tops = [jnp.max(score, axis=-1, keepdims=True) for score in scores]
                    top = functools.reduce(jnp.maximum, tops)
                    total = 0.0
                    for score, v_ref in zip(scores, values):
                        total = total + nn(jnp.exp2(score - top).astype(bf16), v_ref[:, lanes])
                    sums.append(total)
                finish(sums, out_ref, start + first)


def columns(array):
    return pl.BlockSpec((array.shape[0], 256), lambda i: (0, i))


def stage(kernel, scalars, arrays, outs, name):
    return pl.pallas_call(
        kernel,
        grid=(arrays[0].shape[1] // 256,),
        out_shape=outs,
        in_specs=[smem] * len(scalars) + [columns(array) for array in arrays],
        out_specs=jax.tree.map(
            lambda out: pl.BlockSpec((out.shape[0], 256 * out.shape[1] // arrays[0].shape[1]), lambda i: (0, i)), outs
        ),
        compiler_params=params(40),
        name=name,
    )(*scalars, *arrays)


def push_rows(scale, live, after, wk_ref, wv_ref, r_ref, key_ref, push_ref):
    parts = nn(after, r_ref[...])
    high = parts[:, 0:1] + parts[:, 1:2] + parts[:, 2:3] + 1.0
    soft = jnp.maximum(high, 0.0) + jnp.log1p(jnp.exp(-jnp.abs(high)))
    spot = lax.broadcasted_iota(jnp.int32, high.shape, 0)
    rate = jnp.where(live(spot), soft * scale, 0.0)
    key = nn(after, wk_ref[...])
    key_ref[...] = (key * lax.rsqrt(jnp.mean(key * key, axis=-1, keepdims=True) + eps)).astype(bf16)
    push_ref[...] = (-rate * nn(after, wv_ref[...])).astype(bf16)


def shown_rows(valid_ref, side, count):
    return lambda spot: spot < valid_ref[side]


def out_kernel(scale, valid_ref, attn_ref, t0, t1, t2, wo_ref, wk_ref, wv_ref, r_ref, after_ref, key_ref, push_ref):
    side = pl.program_id(0)
    other = jnp.concatenate([t1[...], t2[...]], axis=0)
    before = jnp.where(side == 0, t0[...], other).astype(f32)
    after = (before + nn(attn_ref[...], wo_ref[...])).astype(bf16)
    after_ref[...] = after
    push_rows(scale, shown_rows(valid_ref, side, 0), after, wk_ref, wv_ref, r_ref, key_ref, push_ref)


def again_kernel(scale, valid_ref, after_ref, wk_ref, wv_ref, r_ref, key_ref, push_ref):
    side = pl.program_id(0)
    push_rows(scale, shown_rows(valid_ref, side, 0), after_ref[...], wk_ref, wv_ref, r_ref, key_ref, push_ref)


def head_weights(width, size, head):
    return [
        pl.BlockSpec((width, size), lambda i: (0, head)),
        pl.BlockSpec((width, size), lambda i: (0, width // size + head)),
        pl.BlockSpec((width, 128), lambda i: (0, head)),
    ]


def first_pushes(scale, valid, attn, t0, t1, t2, wo, wkv, rate):
    count, width = t0.shape
    size = width // (rate.shape[1] // 128)
    block = pl.BlockSpec((count, width), lambda i: (i, 0))
    narrow = pl.BlockSpec((count, size), lambda i: (i, 0))
    both = jax.ShapeDtypeStruct((2 * count, size), bf16)
    return pl.pallas_call(
        functools.partial(out_kernel, scale),
        grid=(2,),
        out_shape=(jax.ShapeDtypeStruct((2 * count, width), bf16), both, both),
        in_specs=[smem, block] + [whole(t.shape) for t in (t0, t1, t2, wo)] + head_weights(width, size, 0),
        out_specs=[block, narrow, narrow],
        compiler_params=params(32),
        name="first_pushes",
    )(valid, attn, t0, t1, t2, wo, wkv, wkv, rate)


def next_pushes(scale, valid, after, wkv, rate, head):
    rows, width = after.shape
    count = rows // 2
    size = width // (rate.shape[1] // 128)
    narrow = pl.BlockSpec((count, size), lambda i: (i, 0))
    both = jax.ShapeDtypeStruct((rows, size), bf16)
    return pl.pallas_call(
        functools.partial(again_kernel, scale),
        grid=(2,),
        out_shape=(both, both),
        in_specs=[smem, pl.BlockSpec((count, width), lambda i: (i, 0))] + head_weights(width, size, head),
        out_specs=[narrow, narrow],
        compiler_params=params(32),
        name="next_pushes",
    )(valid, after, wkv, wkv, rate)


def grad_rows(w, key, push):
    size = key.shape[1]
    act_a = nt(w[:, :size], key)
    act_b = nt(w[:, size : 2 * size], key)
    back = nt(w[:, 2 * size :], push)
    sigma = 1.0 / (1.0 + jnp.exp(-act_a))
    silu = act_a * sigma
    hidden = (silu * act_b).astype(bf16)
    grad_a = (back * act_b * sigma * (1.0 + act_a * (1.0 - sigma))).astype(bf16)
    grad_b = (back * silu).astype(bf16)
    return nn(grad_a, key), nn(grad_b, key), nn(hidden, push)


def sent_kernel(w_ref, key_ref, push_ref, first_ref, second_ref, first_keep, second_keep):
    quarter = first_keep.shape[0]
    size = key_ref.shape[1]
    rest = split - size
    a, b, c = grad_rows(w_ref[0, quarter:, :], key_ref[...], push_ref[...])
    early, middle, late = slice(0, quarter), slice(quarter, 2 * quarter), slice(2 * quarter, 3 * quarter)
    first_ref[:, :size] = a[quarter:].astype(bf16)
    first_ref[:, size:] = b[quarter:, :rest].astype(bf16)
    first_keep[:, :size] = a[early]
    first_keep[:, size:] = b[early, :rest]
    second_ref[:quarter, : size - rest] = b[early, rest:].astype(bf16)
    second_ref[:quarter, size - rest :] = c[early].astype(bf16)
    second_ref[quarter:, : size - rest] = b[late, rest:].astype(bf16)
    second_ref[quarter:, size - rest :] = c[late].astype(bf16)
    second_keep[:, : size - rest] = b[middle, rest:]
    second_keep[:, size - rest :] = c[middle]


def sent_gradient(weights, keys, pushes, head):
    _, rows, cols = weights.shape
    quarter = rows // 4
    shapes = [(2 * quarter, split), (2 * quarter, cols - split), (quarter, split), (quarter, cols - split)]
    kinds = [bf16, bf16, f32, f32]
    return pl.pallas_call(
        sent_kernel,
        grid=(1,),
        out_shape=tuple(jax.ShapeDtypeStruct(shape, kind) for shape, kind in zip(shapes, kinds)),
        in_specs=[pl.BlockSpec((1, rows, cols), lambda i: (head, 0, 0)), whole(keys.shape), whole(pushes.shape)],
        out_specs=[whole(shape) for shape in shapes],
        compiler_params=params(32),
        name="sent_gradient",
    )(weights, keys, pushes)


def kept_kernel(w_ref, key_ref, push_ref, out_ref):
    size = key_ref.shape[1]
    for at, part in enumerate(grad_rows(w_ref[0], key_ref[...], push_ref[...])):
        out_ref[:, at * size : at * size + size] = part


def kept_gradient(weights, keys, pushes, head):
    _, rows, cols = weights.shape
    quarter = rows // 4
    return pl.pallas_call(
        kept_kernel,
        grid=(1,),
        out_shape=jax.ShapeDtypeStruct((quarter, cols), f32),
        in_specs=[pl.BlockSpec((1, quarter, cols), lambda i: (head, 0, 0)), whole(keys.shape), whole(pushes.shape)],
        out_specs=whole((quarter, cols)),
        compiler_params=params(32),
        name="kept_gradient",
    )(weights, keys, pushes)


def join_kernel(kept_ref, a1_ref, b1_ref, a2_ref, b2_ref, sent_ref, keep_ref):
    half = keep_ref.shape[0]
    quarter = kept_ref.shape[0]
    for first, second, part in ((a1_ref, a2_ref, slice(0, split)), (b1_ref, b2_ref, slice(split, kept_ref.shape[1]))):
        total = kept_ref[:, part] + first[:quarter, :].astype(f32) + second[...].astype(f32)
        keep_ref[:, part] = total[:half]
        sent_ref[:, part] = total[half:].astype(bf16)


def join(kept, *got):
    half = (kept.shape[0] // 2, kept.shape[1])
    return pl.pallas_call(
        join_kernel,
        grid=(1,),
        out_shape=(jax.ShapeDtypeStruct(half, bf16), jax.ShapeDtypeStruct(half, f32)),
        in_specs=[whole(kept.shape)] + [whole(part.shape) for part in got],
        out_specs=[whole(half)] * 2,
        compiler_params=params(8),
        name="join",
    )(kept, *got)


def rescale_kernel(start_ref, mine_ref, theirs_ref, out_ref):
    size = start_ref.shape[1] // 3
    grad = mine_ref[...] + theirs_ref[...].astype(f32)
    for block in range(3):
        part = slice(block * size, block * size + size)
        start = start_ref[:, part].astype(f32)
        update = start - grad[:, part]
        before = jnp.sqrt(jnp.mean(start * start, axis=-1, keepdims=True) + eps)
        after = lax.rsqrt(jnp.mean(update * update, axis=-1, keepdims=True) + eps)
        out_ref[:, part] = (update * before * after).astype(bf16)


def rescale(start, mine, theirs):
    return pl.pallas_call(
        rescale_kernel,
        grid=(1,),
        out_shape=jax.ShapeDtypeStruct(start.shape, bf16),
        in_specs=[whole(start.shape)] * 3,
        out_specs=whole(start.shape),
        compiler_params=params(8),
        name="rescale",
    )(start, mine, theirs)


def query_kernel(t0_ref, t1_ref, w_ref, out_ref):
    side = pl.program_id(0)
    width = t0_ref.shape[1]
    size = width // 2
    tq = nn(jnp.where(side == 0, t0_ref[...], t1_ref[...]), w_ref[...])
    for head in range(2):
        part = slice(head * size, head * size + size)
        q = tq[:, part]
        out_ref[:, part] = (q * lax.rsqrt(jnp.mean(q * q, axis=-1, keepdims=True) + eps)).astype(bf16)


def target_queries(t0, t1, weight):
    count, width = t0.shape
    return pl.pallas_call(
        query_kernel,
        grid=(2,),
        out_shape=jax.ShapeDtypeStruct((2 * count, width), bf16),
        in_specs=[whole((count, width))] * 2 + [whole(weight.shape)],
        out_specs=pl.BlockSpec((count, width), lambda i: (i, 0)),
        compiler_params=params(16),
        name="target_queries",
    )(t0, t1, weight)


def apply_kernel(q_ref, h_ref, a3, b3, a4, b4, mine_ref, theirs_ref):
    count = mine_ref.shape[0]
    size = q_ref.shape[1]
    rest = split - size
    quarter = h_ref.shape[0]
    q = q_ref[...]
    total = 0.0
    blocks = (
        (h_ref[:, :split], h_ref[:, split:]),
        (a3[...], b4[:quarter, :]),
        (a4[:quarter, :], b3[...]),
        (a4[quarter:, :], b4[quarter:, :]),
    )
    for first, second in blocks:
        act_a = nt(q, first[:, :size])
        act_b = nt(q[:, :rest], first[:, size:]) + nt(q[:, rest:], second[:, : size - rest])
        hidden = (act_a / (1.0 + jnp.exp(-act_a)) * act_b).astype(bf16)
        total = total + nn(hidden, second[:, size - rest :])
    mine_ref[...] = total[:count]
    theirs_ref[...] = total[count:].astype(bf16)


def apply_weights(queries, parts, head):
    count = queries.shape[0]
    size = (parts[0].shape[1]) // 3
    half = (count // 2, size)
    return pl.pallas_call(
        apply_kernel,
        grid=(1,),
        out_shape=(jax.ShapeDtypeStruct(half, f32), jax.ShapeDtypeStruct(half, bf16)),
        in_specs=[pl.BlockSpec((count, size), lambda i: (0, head))] + [whole(part.shape) for part in parts],
        out_specs=[whole(half)] * 2,
        compiler_params=params(16),
        name="apply_weights",
    )(queries, *parts)


def merge_kernel(used_ref, target_ref, w_ref, m0_ref, m1_ref, r0_ref, r1_ref, out_ref):
    size = m0_ref.shape[1]
    total = target_ref[...].astype(f32)
    for head, (mine, theirs) in enumerate(((m0_ref, r0_ref), (m1_ref, r1_ref))):
        fout = mine[...] + theirs[...].astype(f32)
        unit = (fout * lax.rsqrt(jnp.mean(fout * fout, axis=-1, keepdims=True) + eps)).astype(bf16)
        total = total + nn(unit, w_ref[head * size : head * size + size, :])
    live = lax.broadcasted_iota(jnp.int32, total.shape, 0) < used_ref[0]
    out_ref[...] = jnp.where(live, total, 0.0).astype(bf16)


def merge(used, target, weight, mine, theirs):
    return pl.pallas_call(
        merge_kernel,
        grid=(1,),
        out_shape=jax.ShapeDtypeStruct(target.shape, bf16),
        in_specs=[smem, whole(target.shape), whole(weight.shape)] + [whole(mine[0].shape)] * 4,
        out_specs=whole(target.shape),
        compiler_params=params(16),
        name="merge",
    )(used, target, weight, *mine, *theirs)


def split_weight(value):
    parts = []
    for _ in range(3):
        part = lax.reduce_precision(value, 8, 7)
        parts.append(part.astype(bf16))
        value = value - part
    return parts


def body(
    tokens,
    attn_gain,
    qkv_weight,
    head_temp,
    out_weight,
    kv_weight,
    rate_weight,
    fast_weights,
    target,
    query_weight,
    merge_weight,
    image_lengths,
    target_counts,
):
    tok_rows, width = tokens.shape
    devices = lax.axis_size("tok")
    place = lax.axis_index("tok")
    parity = place % 2
    head_dim = width // head_temp.shape[0]
    fast_hidden, fast_cols = fast_weights.shape
    fast_heads = rate_weight.shape[1]
    rows = fast_hidden // devices
    image_ids = jnp.arange(image_lengths.shape[0], dtype=jnp.int32)
    length = jnp.sum(jnp.where(image_ids == place // 2, image_lengths, 0))
    own = length - parity * tok_rows
    other = length - (1 - parity) * tok_rows
    chunk = tok_rows // 2
    valid = jnp.stack([own, other, other - chunk]).astype(jnp.int32)

    t1 = swap(tokens[:chunk], pair_mask)

    scale = jnp.repeat(head_temp * (math.log2(math.e) / head_dim), head_dim)[None, :]
    gain = attn_gain[None, :]
    q0, k0, v0 = project_qkv(valid[:1], tokens, gain, scale, qkv_weight)
    late, q0 = lax.optimization_barrier((tokens[chunk:], q0))
    t2 = swap(late, pair_mask)

    moves = []
    for order in reduce_orders:
        span = [0]
        for mask in reversed(order):
            span = span + [mask ^ at for at in span]
        moves.append(span)
    index = place ^ jnp.array(moves, dtype=jnp.int32)
    start = gather_rows(index, fast_weights.reshape(devices, rows, fast_cols))
    weights = start.reshape(fast_heads, len(moves[0]) * rows, fast_cols // fast_heads)
    rate = jnp.stack(split_weight(rate_weight), axis=-1)
    rate = jnp.pad(rate, ((0, 0), (0, 0), (0, 125))).reshape(width, fast_heads * 128)

    wide = 2 * width
    sums0 = jax.ShapeDtypeStruct((tok_rows, wide), f32)
    sums1 = jax.ShapeDtypeStruct((chunk, wide), f32)
    a0 = stage(first_stage, [head_temp], [q0, k0, v0], sums0, "attend_first")
    q1, k1, v1 = project_qkv(valid[1:2], t1, gain, scale, qkv_weight)
    a0, a1 = stage(
        second_stage, [head_temp], [q0, k0, v0, q1, k1, v1, a0], (sums0, sums1), "attend_second"
    )
    t2, target_sent = lax.optimization_barrier((t2, target))
    other_target = swap(target_sent, pair_mask)
    q2, k2, v2 = project_qkv(valid[2:], t2, gain, scale, qkv_weight)
    attn = stage(
        third_stage,
        [valid, head_temp],
        [q0, k0, v0, q1, k1, v1, q2, k2, v2, a0, a1],
        jax.ShapeDtypeStruct((2 * tok_rows, width), bf16),
        "attend_third",
    )

    factor = rate_base / (tok_rows * devices)
    after, keys, pushes = first_pushes(factor, valid, attn, tokens, t1, t2, out_weight, kv_weight, rate)
    made = [(keys, pushes)]
    sent = [sent_gradient(weights, keys, pushes, 0)]
    after, other_target = lax.optimization_barrier((after, other_target))
    for head in range(1, fast_heads):
        made.append(next_pushes(factor, valid, after, kv_weight, rate, head))
        sent.append(sent_gradient(weights, *made[head], head))
    kept = [kept_gradient(weights, *made[head], head) for head in range(fast_heads)]

    fresh = []
    for head in range(fast_heads):
        d1, d2, d3, d4 = reduce_orders[head]
        first, second, first_keep, second_keep = sent[head]
        quarter = first_keep.shape[0]
        a1, b1 = swap(first, d1), swap(second, d2)
        a2 = swap((first_keep + a1[quarter:].astype(f32)).astype(bf16), d2)
        b2 = swap((second_keep + b1[quarter:].astype(f32)).astype(bf16), d1)
        away, stay = join(kept[head], a1, b1, a2, b2)
        total = stay + swap(away, d3).astype(f32)
        got = swap(total[rows:].astype(bf16), d4)
        fresh.append(rescale(start[head, 0], total[:rows], got))

    queries = target_queries(target, other_target, query_weight)
    mine, theirs = [], []
    for head in range(fast_heads):
        d1, d2, d3, d4 = reduce_orders[head]
        held = fresh[head]
        for mask in (d4, d3):
            held = jnp.concatenate([held, swap(held, mask)], axis=0)
        first, second = held[:, :split], held[:, split:]
        a3, b3 = swap(first, d2), swap(second, d1)
        a4 = swap(jnp.concatenate([first, a3], axis=0), d1)
        b4 = swap(jnp.concatenate([second, b3], axis=0), d2)
        kept_sum, sent_sum = apply_weights(queries, [held, a3, b3, a4, b4], head)
        mine.append(kept_sum)
        theirs.append(swap(sent_sum, pair_mask))
    target_out = merge(target_counts, target, merge_weight, mine, theirs)
    return (after[:tok_rows], jnp.concatenate(fresh, axis=1), target_out)


def solution(mesh):
    placed = (
        P(("rep", "tok"), None),
        P(),
        P(),
        P(),
        P(),
        P(),
        P(),
        P(),
        P(("rep", "tok"), None),
        P(),
        P(),
        P("rep"),
        P(("rep", "tok")),
    )
    return jax.shard_map(
        body,
        mesh=mesh,
        in_specs=placed,
        out_specs=(P(("rep", "tok"), None), P(("rep", "tok"), None), P(("rep", "tok"), None)),
        check_vma=False,
    )
```

```python
import functools
import math

import jax
import jax.numpy as jnp
from jax import lax
from jax.experimental import pallas as pl
from jax.experimental.pallas import tpu as pltpu
from jax.sharding import PartitionSpec as P

eps = 1e-06
rate_base = 4.0
safe_temp = 60.0
bf16 = jnp.bfloat16
f32 = jnp.float32

pair_mask = 1
reduce_orders = ((3, 4, 8, 24), (24, 3, 4, 8))
gather_orders = ((24, 8, 4, 3), (3, 4, 8, 24))


def swap(value, mask):
    pairs = [(source, source ^ mask) for source in range(lax.axis_size("tok"))]
    return lax.ppermute(value, "tok", pairs)


def params(mib):
    return pltpu.CompilerParams(vmem_limit_bytes=mib * 2**20)


brief = pl.CostEstimate(flops=1, transcendentals=0, bytes_accessed=1)


def nn(a, b):
    return lax.dot_general(a, b, (((1,), (0,)), ((), ())), preferred_element_type=f32)


def nt(a, b):
    return lax.dot_general(a, b, (((1,), (1,)), ((), ())), preferred_element_type=f32)


def whole(shape):
    return pl.BlockSpec(shape, lambda *_: (0,) * len(shape))


smem = pl.BlockSpec(memory_space=pltpu.SMEM)
vmem = pl.BlockSpec(memory_space=pltpu.VMEM)


def gather_kernel(index_ref, rows_ref, out_ref):
    heads, blocks = index_ref.shape
    width = out_ref.shape[-1]
    for head in range(heads):
        for block in range(blocks):
            out_ref[head, block] = rows_ref[index_ref[head, block], :, head * width : head * width + width]


def gather_rows(index, rows):
    heads, blocks = index.shape
    _, height, width = rows.shape
    shape = (heads, blocks, height, width // heads)
    return pl.pallas_call(
        gather_kernel,
        out_shape=jax.ShapeDtypeStruct(shape, rows.dtype),
        in_specs=[smem, vmem],
        out_specs=vmem,
        compiler_params=params(4),
        cost_estimate=brief,
        name="gather_rows",
    )(index, rows)


def qkv_kernel(valid_ref, tok_ref, gain_ref, scale_ref, w_ref, q_ref, k_ref, v_ref, normed):
    x = tok_ref[...].astype(f32)
    unit = x * lax.rsqrt(jnp.mean(x * x, axis=-1, keepdims=True) + eps)
    normed[...] = (unit * gain_ref[...].astype(f32)).astype(bf16)
    count, width = tok_ref.shape
    cols = 256
    low = lax.broadcasted_iota(jnp.int32, (count, 128), 1) < 64
    live = lax.broadcasted_iota(jnp.int32, (count, 128), 0) < valid_ref[0]
    one = jnp.where(live, 1.0, 0.0)

    def unit_heads(t):
        square = t * t
        first = jnp.sum(jnp.where(low, square, 0.0), axis=-1, keepdims=True)
        second = jnp.sum(jnp.where(low, 0.0, square), axis=-1, keepdims=True)
        inv = [lax.rsqrt(total * (1.0 / 64.0) + eps) for total in (first, second)]
        return (t * jnp.where(low, inv[0], inv[1])).astype(bf16).astype(f32)

    for group in range(width // cols):
        rows = normed[...]
        query, key, value = (nn(rows, w_ref[:, at + group * cols : at + group * cols + cols]) for at in (0, width, 2 * width))
        query = query.astype(bf16).astype(f32)
        key = key.astype(bf16).astype(f32)
        for tile in range(cols // 128):
            part = slice(tile * 128, tile * 128 + 128)
            at = group * cols + tile * 128
            even = slice(2 * at, 2 * at + 128)
            odd = slice(2 * at + 128, 2 * at + 256)
            q = unit_heads(query[:, part]) * scale_ref[:, at : at + 128]
            q_high = q.astype(bf16).astype(f32)
            moved = pltpu.roll(q - q_high, 64, 1)
            q_ref[:, even] = jnp.where(low, q_high, moved).astype(bf16)
            q_ref[:, odd] = jnp.where(low, moved, q_high).astype(bf16)
            k = unit_heads(key[:, part])
            moved = pltpu.roll(k, 64, 1)
            k_ref[:, even] = jnp.where(low, k, moved).astype(bf16)
            k_ref[:, odd] = jnp.where(low, moved, k).astype(bf16)
            shown = jnp.where(live, value[:, part], 0.0)
            v_ref[:, even] = jnp.where(low, shown, one).astype(bf16)
            v_ref[:, odd] = jnp.where(low, one, shown).astype(bf16)


def project_qkv(valid, tokens, gain, scale, weight):
    count, width = tokens.shape
    out = jax.ShapeDtypeStruct((count, 2 * width), bf16)
    return pl.pallas_call(
        qkv_kernel,
        out_shape=(out, out, out),
        in_specs=[smem, vmem, vmem, vmem, vmem],
        out_specs=[vmem] * 3,
        scratch_shapes=[pltpu.VMEM((count, width), bf16)],
        compiler_params=params(16),
        cost_estimate=brief,
        name="project_qkv",
    )(valid, tokens, gain, scale, weight)


def weighted(q, keys, values, lanes):
    total = None
    for k_ref, v_ref in zip(keys, values):
        part = nn(jnp.exp2(nt(q, k_ref[:, lanes])).astype(bf16), v_ref[:, lanes])
        total = part if total is None else total + part
    return total


def finish(sums, out_ref, start, pair):
    count = sums[0].shape[0]
    low = lax.broadcasted_iota(jnp.int32, (count, 128), 1) < 64
    top = jnp.where(low, sums[0], sums[1])
    bottom = pltpu.roll(jnp.where(low, sums[1], sums[0]), 64, 1)
    out_ref[start : start + count, pl.ds(pl.multiple_of(pair * 128, 128), 128)] = (top / bottom).astype(bf16)


def pairs_of_heads(temp_ref, width, plain, other=None):
    def step(pair, _):
        lanes = [pl.ds(pl.multiple_of(pair * 256 + head * 128, 128), 128) for head in range(2)]
        safe = jnp.maximum(temp_ref[2 * pair], temp_ref[2 * pair + 1]) <= safe_temp
        pl.when(safe)(functools.partial(plain, pair, lanes))
        if other is not None:
            pl.when(jnp.logical_not(safe))(functools.partial(other, pair, lanes))
        return 0

    lax.fori_loop(0, width // 256, step, 0)


def first_stage(temp_ref, q0, k0, v0, a0):
    def plain(pair, heads):
        for lanes in heads:
            a0[:, lanes] = weighted(q0[:, lanes], [k0], [v0], lanes)

    pairs_of_heads(temp_ref, q0.shape[1], plain)


def last_stage(valid_ref, temp_ref, q0, k0, v0, q1, k1, v1, a0, out_ref):
    count = q0.shape[0]
    keys, values = [k0, k1], [v0, v1]

    def plain(pair, heads):
        finish([a0[:, lanes] + weighted(q0[:, lanes], [k1], [v1], lanes) for lanes in heads], out_ref, 0, pair)
        finish([weighted(q1[:, lanes], keys, values, lanes) for lanes in heads], out_ref, count, pair)

    def other(pair, heads):
        for q_ref, start in zip((q0, q1), (0, count)):
            for first in range(0, count, 256):
                sums = []
                for lanes in heads:
                    scores = []
                    for at, k_ref in enumerate(keys):
                        score = nt(q_ref[first : first + 256, lanes], k_ref[:, lanes])
                        spot = lax.broadcasted_iota(jnp.int32, score.shape, 1)
                        scores.append(jnp.where(spot < valid_ref[at], score, -1e30))
                    tops = [jnp.max(score, axis=-1, keepdims=True) for score in scores]
                    top = functools.reduce(jnp.maximum, tops)
                    total = 0.0
                    for score, v_ref in zip(scores, values):
                        total = total + nn(jnp.exp2(score - top).astype(bf16), v_ref[:, lanes])
                    sums.append(total)
                finish(sums, out_ref, start + first, pair)

    pairs_of_heads(temp_ref, q0.shape[1], plain, other)


def stage(kernel, scalars, arrays, outs, name):
    return pl.pallas_call(
        kernel,
        out_shape=outs,
        in_specs=[smem] * len(scalars) + [vmem] * len(arrays),
        out_specs=jax.tree.map(lambda out: vmem, outs),
        compiler_params=params(16),
        cost_estimate=brief,
        name=name,
    )(*scalars, *arrays)


def push_rows(scale, shown, after, wkv_ref, r_ref, head, key_ref, push_ref, rows):
    size = key_ref.shape[1]
    width = wkv_ref.shape[1] // 2
    parts = nn(after, r_ref[:, head * 128 : head * 128 + 128])
    high = parts[:, 0:1] + parts[:, 1:2] + parts[:, 2:3] + 1.0
    soft = jnp.maximum(high, 0.0) + jnp.log1p(jnp.exp(-jnp.abs(high)))
    spot = lax.broadcasted_iota(jnp.int32, high.shape, 0)
    rate = jnp.where(spot < shown, soft * scale, 0.0)
    key = nn(after, wkv_ref[:, head * size : head * size + size])
    key_ref[rows, :] = (key * lax.rsqrt(jnp.mean(key * key, axis=-1, keepdims=True) + eps)).astype(bf16)
    value = nn(after, wkv_ref[:, width + head * size : width + head * size + size])
    push_ref[rows, :] = (-rate * value).astype(bf16)


def out_kernel(scale, valid_ref, attn_ref, t0, t1, wo_ref, wkv_ref, r_ref, out_ref, after_ref, key_ref, push_ref):
    count = t0.shape[0]
    for side, tok_ref in enumerate((t0, t1)):
        rows = slice(side * count, side * count + count)
        after = (tok_ref[...].astype(f32) + nn(attn_ref[rows, :], wo_ref[...])).astype(bf16)
        after_ref[rows, :] = after
        if side == 0:
            out_ref[...] = after
        push_rows(scale, valid_ref[side], after, wkv_ref, r_ref, 0, key_ref, push_ref, rows)


def again_kernel(scale, head, valid_ref, after_ref, wkv_ref, r_ref, key_ref, push_ref):
    half = after_ref.shape[0] // 2
    for side in range(2):
        rows = slice(side * half, side * half + half)
        push_rows(scale, valid_ref[side], after_ref[rows, :], wkv_ref, r_ref, head, key_ref, push_ref, rows)


def first_pushes(scale, valid, attn, t0, t1, wo, wkv, rate):
    count, width = t0.shape
    both = jax.ShapeDtypeStruct((2 * count, width * 128 // rate.shape[1]), bf16)
    return pl.pallas_call(
        functools.partial(out_kernel, scale),
        out_shape=(
            jax.ShapeDtypeStruct((count, width), bf16),
            jax.ShapeDtypeStruct((2 * count, width), bf16),
            both,
            both,
        ),
        in_specs=[smem] + [vmem] * 6,
        out_specs=[vmem] * 4,
        compiler_params=params(12),
        cost_estimate=brief,
        name="first_pushes",
    )(valid, attn, t0, t1, wo, wkv, rate)


def next_pushes(scale, valid, after, wkv, rate, head):
    rows, width = after.shape
    both = jax.ShapeDtypeStruct((rows, width * 128 // rate.shape[1]), bf16)
    return pl.pallas_call(
        functools.partial(again_kernel, scale, head),
        out_shape=(both, both),
        in_specs=[smem] + [vmem] * 3,
        out_specs=[vmem] * 2,
        compiler_params=params(12),
        cost_estimate=brief,
        name="next_pushes",
    )(valid, after, wkv, rate)


def grad_kernel(head, half, w_ref, key_ref, push_ref, out_ref):
    count, size = out_ref.shape[0], key_ref.shape[1]
    key, push = key_ref[...], push_ref[...]
    w = w_ref[head, half * count : half * count + count, :]
    act_a = nt(w[:, :size], key)
    act_b = nt(w[:, size : 2 * size], key)
    back = nt(w[:, 2 * size :], push)
    sigma = 1.0 / (1.0 + jnp.exp(-act_a))
    silu = act_a * sigma
    hidden = (silu * act_b).astype(bf16)
    grad_a = (back * act_b * sigma * (1.0 + act_a * (1.0 - sigma))).astype(bf16)
    grad_b = (back * silu).astype(bf16)
    out_ref[:, :size] = nn(grad_a, key).astype(out_ref.dtype)
    out_ref[:, size : 2 * size] = nn(grad_b, key).astype(out_ref.dtype)
    out_ref[:, 2 * size :] = nn(hidden, push).astype(out_ref.dtype)


def gradient(weights, keys, pushes, head, half, kind):
    _, rows, cols = weights.shape
    return pl.pallas_call(
        functools.partial(grad_kernel, head, half),
        out_shape=jax.ShapeDtypeStruct((rows // 2, cols), kind),
        in_specs=[vmem] * 3,
        out_specs=vmem,
        compiler_params=params(12),
        cost_estimate=brief,
        name="gradient",
    )(weights, keys, pushes)


def add_kernel(kept_ref, got_ref, sent_ref, keep_ref):
    half = keep_ref.shape[0]
    sent_ref[...] = (kept_ref[half:, :] + got_ref[half:, :].astype(f32)).astype(bf16)
    keep_ref[...] = kept_ref[:half, :] + got_ref[:half, :].astype(f32)


def add_step(kept, got):
    half = (kept.shape[0] // 2, kept.shape[1])
    return pl.pallas_call(
        add_kernel,
        out_shape=(jax.ShapeDtypeStruct(half, bf16), jax.ShapeDtypeStruct(half, f32)),
        in_specs=[vmem] * 2,
        out_specs=[vmem] * 2,
        compiler_params=params(4),
        cost_estimate=brief,
        name="add_step",
    )(kept, got)


def rescale_kernel(start_ref, mine_ref, theirs_ref, out_ref):
    size = start_ref.shape[1] // 3
    grad = mine_ref[...] + theirs_ref[...].astype(f32)
    for block in range(3):
        part = slice(block * size, block * size + size)
        start = start_ref[:, part].astype(f32)
        update = start - grad[:, part]
        before = jnp.sqrt(jnp.mean(start * start, axis=-1, keepdims=True) + eps)
        after = lax.rsqrt(jnp.mean(update * update, axis=-1, keepdims=True) + eps)
        out_ref[:, part] = (update * before * after).astype(bf16)


def rescale(start, mine, theirs):
    return pl.pallas_call(
        rescale_kernel,
        out_shape=jax.ShapeDtypeStruct(start.shape, bf16),
        in_specs=[vmem] * 3,
        out_specs=vmem,
        compiler_params=params(4),
        cost_estimate=brief,
        name="rescale",
    )(start, mine, theirs)


def query_kernel(t0_ref, t1_ref, w_ref, out_ref):
    count, width = t0_ref.shape
    size = width // 2
    for side, t_ref in enumerate((t0_ref, t1_ref)):
        tq = nn(t_ref[...], w_ref[...])
        for head in range(2):
            part = slice(head * size, head * size + size)
            q = tq[:, part]
            unit = q * lax.rsqrt(jnp.mean(q * q, axis=-1, keepdims=True) + eps)
            out_ref[side * count : side * count + count, part] = unit.astype(bf16)


def target_queries(t0, t1, weight):
    count, width = t0.shape
    return pl.pallas_call(
        query_kernel,
        out_shape=jax.ShapeDtypeStruct((2 * count, width), bf16),
        in_specs=[vmem] * 3,
        out_specs=vmem,
        compiler_params=params(8),
        cost_estimate=brief,
        name="target_queries",
    )(t0, t1, weight)


def apply_rows(q, w_ref):
    size = q.shape[1]
    act_a = nt(q, w_ref[:, :size])
    act_b = nt(q, w_ref[:, size : 2 * size])
    hidden = (act_a / (1.0 + jnp.exp(-act_a)) * act_b).astype(bf16)
    return nn(hidden, w_ref[:, 2 * size :])


def first_kernel(head, q_ref, w_ref, out_ref):
    size = out_ref.shape[1]
    out_ref[...] = apply_rows(q_ref[:, head * size : head * size + size], w_ref)


def apply_first(queries, weights, head):
    return pl.pallas_call(
        functools.partial(first_kernel, head),
        out_shape=jax.ShapeDtypeStruct((queries.shape[0], weights.shape[1] // 3), f32),
        in_specs=[vmem] * 2,
        out_specs=vmem,
        compiler_params=params(8),
        cost_estimate=brief,
        name="apply_first",
    )(queries, weights)


def last_kernel(head, q_ref, w_ref, sum_ref, mine_ref, theirs_ref):
    count, size = mine_ref.shape
    total = sum_ref[...] + apply_rows(q_ref[:, head * size : head * size + size], w_ref)
    mine_ref[...] = total[:count]
    theirs_ref[...] = total[count:].astype(bf16)


def apply_last(queries, weights, total, head):
    half = (total.shape[0] // 2, total.shape[1])
    return pl.pallas_call(
        functools.partial(last_kernel, head),
        out_shape=(jax.ShapeDtypeStruct(half, f32), jax.ShapeDtypeStruct(half, bf16)),
        in_specs=[vmem] * 3,
        out_specs=[vmem] * 2,
        compiler_params=params(8),
        cost_estimate=brief,
        name="apply_last",
    )(queries, weights, total)


def merge_kernel(used_ref, target_ref, w_ref, m0_ref, m1_ref, r0_ref, r1_ref, out_ref):
    size = m0_ref.shape[1]
    total = target_ref[...].astype(f32)
    for head, (mine, theirs) in enumerate(((m0_ref, r0_ref), (m1_ref, r1_ref))):
        fout = mine[...] + theirs[...].astype(f32)
        unit = (fout * lax.rsqrt(jnp.mean(fout * fout, axis=-1, keepdims=True) + eps)).astype(bf16)
        total = total + nn(unit, w_ref[head * size : head * size + size, :])
    live = lax.broadcasted_iota(jnp.int32, total.shape, 0) < used_ref[0]
    out_ref[...] = jnp.where(live, total, 0.0).astype(bf16)


def merge(used, target, weight, mine, theirs):
    return pl.pallas_call(
        merge_kernel,
        out_shape=jax.ShapeDtypeStruct(target.shape, bf16),
        in_specs=[smem] + [vmem] * 6,
        out_specs=vmem,
        compiler_params=params(8),
        cost_estimate=brief,
        name="merge",
    )(used, target, weight, *mine, *theirs)


def split_weight(value):
    parts = []
    for _ in range(3):
        part = lax.reduce_precision(value, 8, 7)
        parts.append(part.astype(bf16))
        value = value - part
    return parts


def body(
    tokens,
    attn_gain,
    qkv_weight,
    head_temp,
    out_weight,
    kv_weight,
    rate_weight,
    fast_weights,
    target,
    query_weight,
    merge_weight,
    image_lengths,
    target_counts,
):
    tok_rows, width = tokens.shape
    devices = lax.axis_size("tok")
    place = lax.axis_index("tok")
    parity = place % 2
    head_dim = width // head_temp.shape[0]
    fast_hidden, fast_cols = fast_weights.shape
    fast_heads = rate_weight.shape[1]
    rows = fast_hidden // devices
    image_ids = jnp.arange(image_lengths.shape[0], dtype=jnp.int32)
    length = jnp.sum(jnp.where(image_ids == place // 2, image_lengths, 0))
    valid = jnp.stack([length - parity * tok_rows, length - (1 - parity) * tok_rows]).astype(jnp.int32)

    moves = []
    for order in reduce_orders:
        span = [0]
        for mask in reversed(order):
            span = span + [mask ^ at for at in span]
        moves.append(span)
    index = place ^ jnp.array(moves, dtype=jnp.int32)
    scale = jnp.repeat(head_temp * (math.log2(math.e) / head_dim), head_dim)[None, :]
    gain = attn_gain[None, :]
    sums = jax.ShapeDtypeStruct((tok_rows, 2 * width), f32)
    arrived = swap(tokens, pair_mask)
    q0, k0, v0 = project_qkv(valid[:1], tokens, gain, scale, qkv_weight)
    a0 = stage(first_stage, [head_temp], [q0, k0, v0], sums, "attend_first")

    start = gather_rows(index, fast_weights.reshape(devices, rows, fast_cols))
    weights = start.reshape(fast_heads, len(moves[0]) * rows, fast_cols // fast_heads)
    rate = jnp.stack(split_weight(rate_weight), axis=-1)
    rate = jnp.pad(rate, ((0, 0), (0, 0), (0, 125))).reshape(width, fast_heads * 128)

    arrived, target_sent, a0, weights, rate = lax.optimization_barrier((arrived, target, a0, weights, rate))
    other_target = swap(target_sent, pair_mask)
    q1, k1, v1 = project_qkv(valid[1:], arrived, gain, scale, qkv_weight)
    attn = stage(
        last_stage,
        [valid, head_temp],
        [q0, k0, v0, q1, k1, v1, a0],
        jax.ShapeDtypeStruct((2 * tok_rows, width), bf16),
        "attend_last",
    )

    attn, other_target = lax.optimization_barrier((attn, other_target))
    factor = rate_base / (tok_rows * devices)
    tokens_out, after, keys, pushes = first_pushes(
        factor, valid, attn, tokens, arrived, out_weight, kv_weight, rate
    )
    made = [(keys, pushes)]
    sent = [gradient(weights, keys, pushes, 0, 1, bf16)]
    after, sent[0] = lax.optimization_barrier((after, sent[0]))
    got = [swap(sent[0], reduce_orders[0][0])]
    made.append(next_pushes(factor, valid, after, kv_weight, rate, 1))
    sent.append(gradient(weights, *made[1], 1, 1, bf16))
    made[0], made[1], sent[1] = lax.optimization_barrier((made[0], made[1], sent[1]))
    got.append(swap(sent[1], reduce_orders[1][0]))
    kept = [gradient(weights, *made[head], head, 0, f32) for head in range(fast_heads)]
    queries = target_queries(target, other_target, query_weight)
    fresh = []
    for head in range(fast_heads):
        keep, came = kept[head], got[head]
        for mask in reduce_orders[head][1:]:
            away, keep = add_step(keep, came)
            if head == 0 and mask == reduce_orders[head][-1]:
                keep, queries = lax.optimization_barrier((keep, queries))
            came = swap(away, mask)
        fresh.append(rescale(start[head, 0], keep, came))

    mine, theirs = [], []
    for head in range(fast_heads):
        held = fresh[head]
        for mask in gather_orders[head][:-1]:
            held = jnp.concatenate([held, swap(held, mask)], axis=0)
        last = swap(held, gather_orders[head][-1])
        total = apply_first(queries, held, head)
        kept_sum, sent_sum = apply_last(queries, last, total, head)
        mine.append(kept_sum)
        theirs.append(swap(sent_sum, pair_mask))
    target_out = merge(target_counts, target, merge_weight, mine, theirs)
    return (tokens_out, jnp.concatenate(fresh, axis=1), target_out)


def solution(mesh):
    placed = (
        P(("rep", "tok"), None),
        P(),
        P(),
        P(),
        P(),
        P(),
        P(),
        P(),
        P(("rep", "tok"), None),
        P(),
        P(),
        P("rep"),
        P(("rep", "tok")),
    )
    return jax.shard_map(
        body,
        mesh=mesh,
        in_specs=placed,
        out_specs=(P(("rep", "tok"), None), P(("rep", "tok"), None), P(("rep", "tok"), None)),
        check_vma=False,
    )
```

```python
import functools
import math

import jax
import jax.numpy as jnp
from jax import lax
from jax.experimental import pallas as pl
from jax.experimental.pallas import tpu as pltpu
from jax.sharding import PartitionSpec as P

eps = 1e-06
rate_base = 4.0
safe_temp = 60.0
bf16 = jnp.bfloat16
f32 = jnp.float32

image_mask = 1
halve_masks = ((3, 4), (4, 3))
ring_masks = (24, 8, 16)
double_masks = ((1, 3), (4, 1))
share_masks = (4, 3)


def swap(value, mask):
    pairs = [(source, source ^ mask) for source in range(lax.axis_size("tok"))]
    return lax.ppermute(value, "tok", pairs)


def params(mib):
    return pltpu.CompilerParams(vmem_limit_bytes=mib * 2**20)


brief = pl.CostEstimate(flops=1, transcendentals=0, bytes_accessed=1)


def nn(a, b):
    return lax.dot_general(a, b, (((1,), (0,)), ((), ())), preferred_element_type=f32)


def nt(a, b):
    return lax.dot_general(a, b, (((1,), (1,)), ((), ())), preferred_element_type=f32)


def whole(shape):
    return pl.BlockSpec(shape, lambda *_: (0,) * len(shape))


smem = pl.BlockSpec(memory_space=pltpu.SMEM)
vmem = pl.BlockSpec(memory_space=pltpu.VMEM)


def gather_kernel(index_ref, rows_ref, out_ref):
    head = pl.program_id(0)
    for block in range(index_ref.shape[1]):
        out_ref[head, block] = rows_ref[index_ref[head, block]]


def gather_rows(index, rows):
    heads, blocks = index.shape
    count, height, width = rows.shape
    cols = width // heads
    return pl.pallas_call(
        gather_kernel,
        grid=(heads,),
        out_shape=jax.ShapeDtypeStruct((heads, blocks, height, cols), rows.dtype),
        in_specs=[smem, pl.BlockSpec((count, height, cols), lambda i: (0, 0, i))],
        out_specs=vmem,
        compiler_params=params(12),
        cost_estimate=brief,
        name="gather_rows",
    )(index, rows)


def qkv_kernel(side, valid_ref, temp_ref, tok_ref, gain_ref, wq_ref, wk_ref, wv_ref, q_ref, k_ref, v_ref, normed):
    group = pl.program_id(0)

    @pl.when(group == 0)
    def _():
        x = tok_ref[...].astype(f32)
        unit = x * lax.rsqrt(jnp.mean(x * x, axis=-1, keepdims=True) + eps)
        normed[...] = (unit * gain_ref[...].astype(f32)).astype(bf16)

    count, cols = normed.shape[0], wq_ref.shape[1]
    low = lax.broadcasted_iota(jnp.int32, (count, 128), 1) < 64
    live = lax.broadcasted_iota(jnp.int32, (count, 128), 0) < valid_ref[side]
    one = jnp.where(live, 1.0, 0.0)

    def unit_heads(t):
        square = t * t
        first = jnp.sum(jnp.where(low, square, 0.0), axis=-1, keepdims=True)
        second = jnp.sum(jnp.where(low, 0.0, square), axis=-1, keepdims=True)
        inv = [lax.rsqrt(total * (1.0 / 64.0) + eps) for total in (first, second)]
        return (t * jnp.where(low, inv[0], inv[1])).astype(bf16).astype(f32)

    rows = normed[...]
    query = nn(rows, wq_ref[...]).astype(bf16).astype(f32)
    key = nn(rows, wk_ref[...]).astype(bf16).astype(f32)
    value = nn(rows, wv_ref[...])
    for tile in range(cols // 128):
        part = slice(tile * 128, tile * 128 + 128)
        head = group * (cols // 64) + 2 * tile
        even = pl.ds(pl.multiple_of(group * (2 * cols) + tile * 256, 128), 128)
        odd = pl.ds(pl.multiple_of(group * (2 * cols) + tile * 256 + 128, 128), 128)
        scale = jnp.where(low, temp_ref[head], temp_ref[head + 1]) * (math.log2(math.e) / 64.0)
        q = unit_heads(query[:, part]) * scale
        q_high = q.astype(bf16).astype(f32)
        moved = pltpu.roll(q - q_high, 64, 1)
        q_ref[:, even] = jnp.where(low, q_high, moved).astype(bf16)
        q_ref[:, odd] = jnp.where(low, moved, q_high).astype(bf16)
        k = unit_heads(key[:, part])
        moved = pltpu.roll(k, 64, 1)
        k_ref[:, even] = jnp.where(low, k, moved).astype(bf16)
        k_ref[:, odd] = jnp.where(low, moved, k).astype(bf16)
        shown = jnp.where(live, value[:, part], 0.0)
        v_ref[:, even] = jnp.where(low, shown, one).astype(bf16)
        v_ref[:, odd] = jnp.where(low, one, shown).astype(bf16)


def project_qkv(side, valid, temps, tokens, gain, weight):
    count, width = tokens.shape
    cols = 256
    steps = width // cols
    out = jax.ShapeDtypeStruct((count, 2 * width), bf16)
    return pl.pallas_call(
        functools.partial(qkv_kernel, side),
        grid=(steps,),
        out_shape=(out, out, out),
        in_specs=[
            smem,
            smem,
            whole((count, width)),
            whole((1, width)),
            pl.BlockSpec((width, cols), lambda i: (0, i)),
            pl.BlockSpec((width, cols), lambda i: (0, steps + i)),
            pl.BlockSpec((width, cols), lambda i: (0, 2 * steps + i)),
        ],
        out_specs=[vmem] * 3,
        scratch_shapes=[pltpu.VMEM((count, width), bf16)],
        compiler_params=params(16),
        cost_estimate=brief,
        name="project_qkv",
    )(valid, temps, tokens, gain, weight, weight, weight)


def weighted(q, keys, values, lanes):
    total = None
    for k_ref, v_ref in zip(keys, values):
        part = nn(jnp.exp2(nt(q, k_ref[:, lanes])).astype(bf16), v_ref[:, lanes])
        total = part if total is None else total + part
    return total


def finish(sums, out_ref, start, pair):
    count = sums[0].shape[0]
    low = lax.broadcasted_iota(jnp.int32, (count, 128), 1) < 64
    top = jnp.where(low, sums[0], sums[1])
    bottom = pltpu.roll(jnp.where(low, sums[1], sums[0]), 64, 1)
    out_ref[start : start + count, pl.ds(pl.multiple_of(pair * 128, 128), 128)] = (top / bottom).astype(bf16)


def pairs_of_heads(temp_ref, width, plain, other=None):
    def step(pair, _):
        lanes = [pl.ds(pl.multiple_of(pair * 256 + head * 128, 128), 128) for head in range(2)]
        safe = jnp.maximum(temp_ref[2 * pair], temp_ref[2 * pair + 1]) <= safe_temp
        pl.when(safe)(functools.partial(plain, pair, lanes))
        if other is not None:
            pl.when(jnp.logical_not(safe))(functools.partial(other, pair, lanes))
        return 0

    lax.fori_loop(0, width // 256, step, 0)


def first_stage(temp_ref, q0, k0, v0, a0):
    def plain(pair, heads):
        for lanes in heads:
            a0[:, lanes] = weighted(q0[:, lanes], [k0], [v0], lanes)

    pairs_of_heads(temp_ref, q0.shape[1], plain)


def last_stage(valid_ref, temp_ref, q0, k0, v0, q1, k1, v1, a0, out_ref):
    count = q0.shape[0]
    keys, values = [k0, k1], [v0, v1]

    def plain(pair, heads):
        finish([a0[:, lanes] + weighted(q0[:, lanes], [k1], [v1], lanes) for lanes in heads], out_ref, 0, pair)
        finish([weighted(q1[:, lanes], keys, values, lanes) for lanes in heads], out_ref, count, pair)

    def other(pair, heads):
        for q_ref, start in zip((q0, q1), (0, count)):
            for first in range(0, count, 256):
                sums = []
                for lanes in heads:
                    scores = []
                    for at, k_ref in enumerate(keys):
                        score = nt(q_ref[first : first + 256, lanes], k_ref[:, lanes])
                        spot = lax.broadcasted_iota(jnp.int32, score.shape, 1)
                        scores.append(jnp.where(spot < valid_ref[at], score, -1e30))
                    tops = [jnp.max(score, axis=-1, keepdims=True) for score in scores]
                    top = functools.reduce(jnp.maximum, tops)
                    total = 0.0
                    for score, v_ref in zip(scores, values):
                        total = total + nn(jnp.exp2(score - top).astype(bf16), v_ref[:, lanes])
                    sums.append(total)
                finish(sums, out_ref, start + first, pair)

    pairs_of_heads(temp_ref, q0.shape[1], plain, other)


def stage(kernel, scalars, arrays, outs, name):
    return pl.pallas_call(
        kernel,
        out_shape=outs,
        in_specs=[smem] * len(scalars) + [vmem] * len(arrays),
        out_specs=jax.tree.map(lambda out: vmem, outs),
        compiler_params=params(16),
        cost_estimate=brief,
        name=name,
    )(*scalars, *arrays)


def push_rows(scale, shown, after, wkv_ref, r_ref, head, key_ref, push_ref, rows):
    size = key_ref.shape[1]
    width = wkv_ref.shape[1] // 2
    exact, pieces = r_ref[...], []
    for _ in range(3):
        pieces.append(exact.astype(bf16).astype(f32))
        exact = exact - pieces[-1]
    heads = exact.shape[0]
    parts = nt(after, jnp.concatenate(pieces, axis=0).astype(bf16))
    high = sum(parts[:, at * heads + head : at * heads + head + 1] for at in range(3)) + 1.0
    soft = jnp.maximum(high, 0.0) + jnp.log1p(jnp.exp(-jnp.abs(high)))
    spot = lax.broadcasted_iota(jnp.int32, high.shape, 0)
    rate = jnp.where(spot < shown, soft * scale, 0.0)
    key = nn(after, wkv_ref[:, head * size : head * size + size])
    key_ref[rows, :] = (key * lax.rsqrt(jnp.mean(key * key, axis=-1, keepdims=True) + eps)).astype(bf16)
    value = nn(after, wkv_ref[:, width + head * size : width + head * size + size])
    push_ref[rows, :] = (-rate * value).astype(bf16)


def out_kernel(scale, valid_ref, attn_ref, t0, t1, wo_ref, wkv_ref, r_ref, out_ref, after_ref, key_ref, push_ref):
    count = t0.shape[0]
    for side, tok_ref in enumerate((t0, t1)):
        rows = slice(side * count, side * count + count)
        after = (tok_ref[...].astype(f32) + nn(attn_ref[rows, :], wo_ref[...])).astype(bf16)
        after_ref[rows, :] = after
        if side == 0:
            out_ref[...] = after
        push_rows(scale, valid_ref[side], after, wkv_ref, r_ref, 0, key_ref, push_ref, rows)


def again_kernel(scale, head, valid_ref, after_ref, wkv_ref, r_ref, key_ref, push_ref):
    half = after_ref.shape[0] // 2
    for side in range(2):
        rows = slice(side * half, side * half + half)
        push_rows(scale, valid_ref[side], after_ref[rows, :], wkv_ref, r_ref, head, key_ref, push_ref, rows)


def first_pushes(scale, valid, attn, t0, t1, wo, wkv, rate):
    count, width = t0.shape
    both = jax.ShapeDtypeStruct((2 * count, width // rate.shape[0]), bf16)
    return pl.pallas_call(
        functools.partial(out_kernel, scale),
        out_shape=(
            jax.ShapeDtypeStruct((count, width), bf16),
            jax.ShapeDtypeStruct((2 * count, width), bf16),
            both,
            both,
        ),
        in_specs=[smem] + [vmem] * 6,
        out_specs=[vmem] * 4,
        compiler_params=params(12),
        cost_estimate=brief,
        name="first_pushes",
    )(valid, attn, t0, t1, wo, wkv, rate)


def next_pushes(scale, valid, after, wkv, rate, head):
    rows, width = after.shape
    both = jax.ShapeDtypeStruct((rows, width // rate.shape[0]), bf16)
    return pl.pallas_call(
        functools.partial(again_kernel, scale, head),
        out_shape=(both, both),
        in_specs=[smem] + [vmem] * 3,
        out_specs=[vmem] * 2,
        compiler_params=params(12),
        cost_estimate=brief,
        name="next_pushes",
    )(valid, after, wkv, rate)


def grad_kernel(head, half, w_ref, key_ref, push_ref, out_ref):
    count, size = out_ref.shape[0], key_ref.shape[1]
    key, push = key_ref[...], push_ref[...]
    w = w_ref[head, half * count : half * count + count, :]
    act_a = nt(w[:, :size], key)
    act_b = nt(w[:, size : 2 * size], key)
    back = nt(w[:, 2 * size :], push)
    sigma = 1.0 / (1.0 + jnp.exp(-act_a))
    silu = act_a * sigma
    hidden = (silu * act_b).astype(bf16)
    grad_a = (back * act_b * sigma * (1.0 + act_a * (1.0 - sigma))).astype(bf16)
    grad_b = (back * silu).astype(bf16)
    out_ref[:, :size] = nn(grad_a, key).astype(out_ref.dtype)
    out_ref[:, size : 2 * size] = nn(grad_b, key).astype(out_ref.dtype)
    out_ref[:, 2 * size :] = nn(hidden, push).astype(out_ref.dtype)


def gradient(weights, keys, pushes, head, half, kind):
    _, rows, cols = weights.shape
    return pl.pallas_call(
        functools.partial(grad_kernel, head, half),
        out_shape=jax.ShapeDtypeStruct((rows // 2, cols), kind),
        in_specs=[vmem] * 3,
        out_specs=vmem,
        compiler_params=params(12),
        cost_estimate=brief,
        name="gradient",
    )(weights, keys, pushes)


def add_kernel(kept_ref, got_ref, sent_ref, keep_ref):
    half = keep_ref.shape[0]
    sent_ref[...] = (kept_ref[half:, :] + got_ref[half:, :].astype(f32)).astype(bf16)
    keep_ref[...] = kept_ref[:half, :] + got_ref[:half, :].astype(f32)


def add_step(kept, got):
    half = (kept.shape[0] // 2, kept.shape[1])
    return pl.pallas_call(
        add_kernel,
        out_shape=(jax.ShapeDtypeStruct(half, bf16), jax.ShapeDtypeStruct(half, f32)),
        in_specs=[vmem] * 2,
        out_specs=[vmem] * 2,
        compiler_params=params(4),
        cost_estimate=brief,
        name="add_step",
    )(kept, got)


def spread_kernel(k0_ref, g0_ref, k1_ref, g1_ref, own_ref, *sent_refs):
    rows, cols = own_ref.shape[0], k0_ref.shape[1]
    for head, (kept_ref, got_ref) in enumerate(((k0_ref, g0_ref), (k1_ref, g1_ref))):
        total = kept_ref[...] + got_ref[...].astype(f32)
        part = slice(head * cols, head * cols + cols)
        own_ref[:, part] = total[:rows]
        for at, sent_ref in enumerate(sent_refs):
            sent_ref[:, part] = total[(at + 1) * rows : (at + 2) * rows].astype(bf16)


def spread(k0, g0, k1, g1):
    shape = (k0.shape[0] // 4, 2 * k0.shape[1])
    kinds = (f32, bf16, bf16, bf16)
    return pl.pallas_call(
        spread_kernel,
        out_shape=tuple(jax.ShapeDtypeStruct(shape, kind) for kind in kinds),
        in_specs=[vmem] * 4,
        out_specs=[vmem] * 4,
        compiler_params=params(4),
        cost_estimate=brief,
        name="spread",
    )(k0, g0, k1, g1)


def rescale_kernel(start_ref, own_ref, a_ref, b_ref, c_ref, out_ref):
    heads, cols = start_ref.shape[0], start_ref.shape[3]
    size = cols // 3
    for head in range(heads):
        for block in range(3):
            part = slice(head * cols + block * size, head * cols + block * size + size)
            grad = own_ref[:, part]
            for got_ref in (a_ref, b_ref, c_ref):
                grad = grad + got_ref[:, part].astype(f32)
            start = start_ref[head, 0, :, block * size : block * size + size].astype(f32)
            update = start - grad
            before = jnp.sqrt(jnp.mean(start * start, axis=-1, keepdims=True) + eps)
            after = lax.rsqrt(jnp.mean(update * update, axis=-1, keepdims=True) + eps)
            out_ref[:, part] = (update * before * after).astype(bf16)


def rescale(start, own, got):
    return pl.pallas_call(
        rescale_kernel,
        out_shape=jax.ShapeDtypeStruct(own.shape, bf16),
        in_specs=[vmem] * 5,
        out_specs=vmem,
        compiler_params=params(4),
        cost_estimate=brief,
        name="rescale",
    )(start, own, *got)


def query_kernel(t_ref, s0_ref, s1_ref, w_ref, q0_ref, q1_ref):
    count = t_ref.shape[0]
    size = q0_ref.shape[1]
    for head, (s_ref, q_ref) in enumerate(((s0_ref, q0_ref), (s1_ref, q1_ref))):
        for side, rows_ref in enumerate((t_ref, s_ref)):
            q = nn(rows_ref[...], w_ref[:, head * size : head * size + size])
            unit = q * lax.rsqrt(jnp.mean(q * q, axis=-1, keepdims=True) + eps)
            q_ref[side * count : side * count + count, :] = unit.astype(bf16)


def target_queries(target, shared, weight):
    count, width = target.shape
    out = jax.ShapeDtypeStruct((2 * count, width // 2), bf16)
    return pl.pallas_call(
        query_kernel,
        out_shape=(out, out),
        in_specs=[vmem] * 4,
        out_specs=[vmem] * 2,
        compiler_params=params(8),
        cost_estimate=brief,
        name="target_queries",
    )(target, *shared, weight)


def apply_rows(q, w_ref):
    size = q.shape[1]
    act_a = nt(q, w_ref[:, :size])
    act_b = nt(q, w_ref[:, size : 2 * size])
    hidden = (act_a / (1.0 + jnp.exp(-act_a)) * act_b).astype(bf16)
    return nn(hidden, w_ref[:, 2 * size :])


def first_kernel(q_ref, w_ref, out_ref):
    out_ref[...] = apply_rows(q_ref[...], w_ref)


def apply_first(queries, weights):
    return pl.pallas_call(
        first_kernel,
        out_shape=jax.ShapeDtypeStruct((queries.shape[0], weights.shape[1] // 3), f32),
        in_specs=[vmem] * 2,
        out_specs=vmem,
        compiler_params=params(8),
        cost_estimate=brief,
        name="apply_first",
    )(queries, weights)


def last_kernel(q_ref, w_ref, sum_ref, mine_ref, theirs_ref):
    count = mine_ref.shape[0]
    total = sum_ref[...] + apply_rows(q_ref[...], w_ref)
    mine_ref[...] = total[:count]
    theirs_ref[...] = total[count:].astype(bf16)


def apply_last(queries, weights, total):
    half = (total.shape[0] // 2, total.shape[1])
    return pl.pallas_call(
        last_kernel,
        out_shape=(jax.ShapeDtypeStruct(half, f32), jax.ShapeDtypeStruct(half, bf16)),
        in_specs=[vmem] * 3,
        out_specs=[vmem] * 2,
        compiler_params=params(8),
        cost_estimate=brief,
        name="apply_last",
    )(queries, weights, total)


def merge_kernel(used_ref, target_ref, w_ref, m0_ref, m1_ref, r0_ref, r1_ref, out_ref):
    size = m0_ref.shape[1]
    total = target_ref[...].astype(f32)
    for head, (mine, theirs) in enumerate(((m0_ref, r0_ref), (m1_ref, r1_ref))):
        fout = mine[...] + theirs[...].astype(f32)
        unit = (fout * lax.rsqrt(jnp.mean(fout * fout, axis=-1, keepdims=True) + eps)).astype(bf16)
        total = total + nn(unit, w_ref[head * size : head * size + size, :])
    live = lax.broadcasted_iota(jnp.int32, total.shape, 0) < used_ref[0]
    out_ref[...] = jnp.where(live, total, 0.0).astype(bf16)


def merge(used, target, weight, mine, theirs):
    return pl.pallas_call(
        merge_kernel,
        out_shape=jax.ShapeDtypeStruct(target.shape, bf16),
        in_specs=[smem] + [vmem] * 6,
        out_specs=vmem,
        compiler_params=params(8),
        cost_estimate=brief,
        name="merge",
    )(used, target, weight, *mine, *theirs)


def body(
    tokens,
    attn_gain,
    qkv_weight,
    head_temp,
    out_weight,
    kv_weight,
    rate_weight,
    fast_weights,
    target,
    query_weight,
    merge_weight,
    image_lengths,
    target_counts,
):
    tok_rows, width = tokens.shape
    devices = lax.axis_size("tok")
    place = lax.axis_index("tok")
    parity = place % 2
    head_dim = width // head_temp.shape[0]
    fast_hidden, fast_cols = fast_weights.shape
    fast_heads = rate_weight.shape[1]
    rows = fast_hidden // devices
    image_ids = jnp.arange(image_lengths.shape[0], dtype=jnp.int32)
    length = jnp.sum(jnp.where(image_ids == place // 2, image_lengths, 0))
    valid = jnp.stack([length - parity * tok_rows, length - (1 - parity) * tok_rows]).astype(jnp.int32)

    moves = []
    for masks in halve_masks:
        span = [0]
        for mask in (24, 8) + masks[::-1]:
            span = span + [mask ^ at for at in span]
        moves.append(span)
    index = place ^ jnp.array(moves, dtype=jnp.int32)
    gain = attn_gain[None, :]
    rate = rate_weight.T
    sums = jax.ShapeDtypeStruct((tok_rows, 2 * width), f32)

    arrived = swap(tokens, image_mask)
    shared = [swap(target, mask) for mask in share_masks]
    q0, k0, v0 = project_qkv(0, valid, head_temp, tokens, gain, qkv_weight)
    a0 = stage(first_stage, [head_temp], [q0, k0, v0], sums, "attend_first")
    start = gather_rows(index, fast_weights.reshape(devices, rows, fast_cols))
    arrived, shared, a0, start = lax.optimization_barrier((arrived, shared, a0, start))
    weights = start.reshape(fast_heads, len(moves[0]) * rows, fast_cols // fast_heads)

    q1, k1, v1 = project_qkv(1, valid, head_temp, arrived, gain, qkv_weight)
    attn = stage(
        last_stage,
        [valid, head_temp],
        [q0, k0, v0, q1, k1, v1, a0],
        jax.ShapeDtypeStruct((2 * tok_rows, width), bf16),
        "attend_last",
    )
    factor = rate_base / (tok_rows * devices)
    tokens_out, after, keys, pushes = first_pushes(
        factor, valid, attn, tokens, arrived, out_weight, kv_weight, rate
    )
    made = [(keys, pushes)]
    sent = [gradient(weights, keys, pushes, 0, 1, bf16)]
    after, sent[0] = lax.optimization_barrier((after, sent[0]))
    got = [swap(sent[0], halve_masks[0][0])]
    made.append(next_pushes(factor, valid, after, kv_weight, rate, 1))
    sent.append(gradient(weights, *made[1], 1, 1, bf16))
    made[0], made[1], sent[1] = lax.optimization_barrier((made[0], made[1], sent[1]))
    got.append(swap(sent[1], halve_masks[1][0]))
    kept = [gradient(weights, *made[head], head, 0, f32) for head in range(fast_heads)]
    queries = target_queries(target, shared, query_weight)
    for head in range(fast_heads):
        away, kept[head] = add_step(kept[head], got[head])
        got[head] = swap(away, halve_masks[head][1])
    kept[1], queries = lax.optimization_barrier((kept[1], queries))
    own, *pieces = spread(kept[0], got[0], kept[1], got[1])
    fresh = rescale(start, own, [swap(piece, mask) for piece, mask in zip(pieces, ring_masks)])

    ring = [fresh] + [swap(fresh, mask) for mask in ring_masks]
    mine, theirs = [], []
    for head in range(fast_heads):
        part = slice(head * (fast_cols // fast_heads), (head + 1) * (fast_cols // fast_heads))
        held = jnp.concatenate([block[:, part] for block in ring], axis=0)
        held = jnp.concatenate([held, swap(held, double_masks[head][0])], axis=0)
        last = swap(held, double_masks[head][1])
        total = apply_first(queries[head], held)
        kept_sum, sent_sum = apply_last(queries[head], last, total)
        mine.append(kept_sum)
        theirs.append(swap(sent_sum, share_masks[head]))
    target_out = merge(target_counts, target, merge_weight, mine, theirs)
    return (tokens_out, fresh, target_out)


def solution(mesh):
    placed = (
        P(("rep", "tok"), None),
        P(),
        P(),
        P(),
        P(),
        P(),
        P(),
        P(),
        P(("rep", "tok"), None),
        P(),
        P(),
        P("rep"),
        P(("rep", "tok")),
    )
    return jax.shard_map(
        body,
        mesh=mesh,
        in_specs=placed,
        out_specs=(P(("rep", "tok"), None), P(("rep", "tok"), None), P(("rep", "tok"), None)),
        check_vma=False,
    )
```

```python
import functools
import math

import jax
import jax.numpy as jnp
from jax import lax
from jax.experimental import pallas as pl
from jax.experimental.pallas import tpu as pltpu
from jax.sharding import PartitionSpec as P

eps = 1e-06
rate_base = 4.0
safe_temp = 60.0
bf16 = jnp.bfloat16
f32 = jnp.float32

image_mask = 1
halve_masks = ((3, 4), (4, 3))
ring_masks = (24, 8, 16)
double_masks = ((1, 3), (4, 1))
share_masks = (4, 3)


def swap(value, mask):
    pairs = [(source, source ^ mask) for source in range(lax.axis_size("tok"))]
    return lax.ppermute(value, "tok", pairs)


def params(mib):
    return pltpu.CompilerParams(vmem_limit_bytes=mib * 2**20)


brief = pl.CostEstimate(flops=1, transcendentals=0, bytes_accessed=1)


def nn(a, b):
    return lax.dot_general(a, b, (((1,), (0,)), ((), ())), preferred_element_type=f32)


def nt(a, b):
    return lax.dot_general(a, b, (((1,), (1,)), ((), ())), preferred_element_type=f32)


def whole(shape):
    return pl.BlockSpec(shape, lambda *_: (0,) * len(shape))


smem = pl.BlockSpec(memory_space=pltpu.SMEM)
vmem = pl.BlockSpec(memory_space=pltpu.VMEM)


def gather_kernel(index_ref, rows_ref, out_ref):
    head = pl.program_id(0)
    for block in range(index_ref.shape[1]):
        out_ref[head, block] = rows_ref[index_ref[head, block]]


def gather_rows(index, rows):
    heads, blocks = index.shape
    count, height, width = rows.shape
    cols = width // heads
    return pl.pallas_call(
        gather_kernel,
        grid=(heads,),
        out_shape=jax.ShapeDtypeStruct((heads, blocks, height, cols), rows.dtype),
        in_specs=[smem, pl.BlockSpec((count, height, cols), lambda i: (0, 0, i))],
        out_specs=vmem,
        compiler_params=params(12),
        cost_estimate=brief,
        name="gather_rows",
    )(index, rows)


def qkv_kernel(side, valid_ref, temp_ref, tok_ref, gain_ref, w_ref, q_ref, k_ref, v_ref, normed):
    x = tok_ref[...].astype(f32)
    unit = x * lax.rsqrt(jnp.mean(x * x, axis=-1, keepdims=True) + eps)
    normed[...] = (unit * gain_ref[...].astype(f32)).astype(bf16)
    count, width = normed.shape
    cols = 256
    low = lax.broadcasted_iota(jnp.int32, (count, 128), 1) < 64
    live = lax.broadcasted_iota(jnp.int32, (count, 128), 0) < valid_ref[side]
    one = jnp.where(live, 1.0, 0.0)

    def unit_heads(t):
        square = t * t
        first = jnp.sum(jnp.where(low, square, 0.0), axis=-1, keepdims=True)
        second = jnp.sum(jnp.where(low, 0.0, square), axis=-1, keepdims=True)
        inv = [lax.rsqrt(total * (1.0 / 64.0) + eps) for total in (first, second)]
        return (t * jnp.where(low, inv[0], inv[1])).astype(bf16).astype(f32)

    for group in range(0, width, cols):
        rows = normed[...]
        query, key, value = (nn(rows, w_ref[:, at + group : at + group + cols]) for at in (0, width, 2 * width))
        query = query.astype(bf16).astype(f32)
        key = key.astype(bf16).astype(f32)
        for tile in range(0, cols, 128):
            part = slice(tile, tile + 128)
            head = (group + tile) // 64
            even = slice(head * 128, head * 128 + 128)
            odd = slice(head * 128 + 128, head * 128 + 256)
            scale = jnp.where(low, temp_ref[head], temp_ref[head + 1]) * (math.log2(math.e) / 64.0)
            q = unit_heads(query[:, part]) * scale
            q_high = q.astype(bf16).astype(f32)
            moved = pltpu.roll(q - q_high, 64, 1)
            q_ref[:, even] = jnp.where(low, q_high, moved).astype(bf16)
            q_ref[:, odd] = jnp.where(low, moved, q_high).astype(bf16)
            k = unit_heads(key[:, part])
            moved = pltpu.roll(k, 64, 1)
            k_ref[:, even] = jnp.where(low, k, moved).astype(bf16)
            k_ref[:, odd] = jnp.where(low, moved, k).astype(bf16)
            shown = jnp.where(live, value[:, part], 0.0)
            v_ref[:, even] = jnp.where(low, shown, one).astype(bf16)
            v_ref[:, odd] = jnp.where(low, one, shown).astype(bf16)


def project_qkv(side, valid, temps, tokens, gain, weight):
    count, width = tokens.shape
    out = jax.ShapeDtypeStruct((count, 2 * width), bf16)
    return pl.pallas_call(
        functools.partial(qkv_kernel, side),
        out_shape=(out, out, out),
        in_specs=[smem, smem] + [vmem] * 3,
        out_specs=[vmem] * 3,
        scratch_shapes=[pltpu.VMEM((count, width), bf16)],
        compiler_params=params(8),
        cost_estimate=brief,
        name="project_qkv",
    )(valid, temps, tokens, gain, weight)


def weighted(q, keys, values, lanes):
    total = None
    for k_ref, v_ref in zip(keys, values):
        part = nn(jnp.exp2(nt(q, k_ref[:, lanes])).astype(bf16), v_ref[:, lanes])
        total = part if total is None else total + part
    return total


def finish(sums, out_ref, start, pair):
    count = sums[0].shape[0]
    low = lax.broadcasted_iota(jnp.int32, (count, 128), 1) < 64
    top = jnp.where(low, sums[0], sums[1])
    bottom = pltpu.roll(jnp.where(low, sums[1], sums[0]), 64, 1)
    out_ref[start : start + count, pl.ds(pl.multiple_of(pair * 128, 128), 128)] = (top / bottom).astype(bf16)


def pairs_of_heads(temp_ref, width, plain, other=None):
    def step(pair, _):
        lanes = [pl.ds(pl.multiple_of(pair * 256 + head * 128, 128), 128) for head in range(2)]
        safe = jnp.maximum(temp_ref[2 * pair], temp_ref[2 * pair + 1]) <= safe_temp
        pl.when(safe)(functools.partial(plain, pair, lanes))
        if other is not None:
            pl.when(jnp.logical_not(safe))(functools.partial(other, pair, lanes))
        return 0

    lax.fori_loop(0, width // 256, step, 0)


def first_stage(temp_ref, q0, k0, v0, a0):
    def plain(pair, heads):
        for lanes in heads:
            a0[:, lanes] = weighted(q0[:, lanes], [k0], [v0], lanes)

    pairs_of_heads(temp_ref, q0.shape[1], plain)


def last_stage(valid_ref, temp_ref, q0, k0, v0, q1, k1, v1, a0, out_ref):
    count = q0.shape[0]
    keys, values = [k0, k1], [v0, v1]

    def plain(pair, heads):
        finish([a0[:, lanes] + weighted(q0[:, lanes], [k1], [v1], lanes) for lanes in heads], out_ref, 0, pair)
        finish([weighted(q1[:, lanes], keys, values, lanes) for lanes in heads], out_ref, count, pair)

    def other(pair, heads):
        for q_ref, start in zip((q0, q1), (0, count)):
            for first in range(0, count, 256):
                sums = []
                for lanes in heads:
                    scores = []
                    for at, k_ref in enumerate(keys):
                        score = nt(q_ref[first : first + 256, lanes], k_ref[:, lanes])
                        spot = lax.broadcasted_iota(jnp.int32, score.shape, 1)
                        scores.append(jnp.where(spot < valid_ref[at], score, -1e30))
                    tops = [jnp.max(score, axis=-1, keepdims=True) for score in scores]
                    top = functools.reduce(jnp.maximum, tops)
                    total = 0.0
                    for score, v_ref in zip(scores, values):
                        total = total + nn(jnp.exp2(score - top).astype(bf16), v_ref[:, lanes])
                    sums.append(total)
                finish(sums, out_ref, start + first, pair)

    pairs_of_heads(temp_ref, q0.shape[1], plain, other)


def stage(kernel, scalars, arrays, outs, name):
    return pl.pallas_call(
        kernel,
        out_shape=outs,
        in_specs=[smem] * len(scalars) + [vmem] * len(arrays),
        out_specs=jax.tree.map(lambda out: vmem, outs),
        compiler_params=params(8),
        cost_estimate=brief,
        name=name,
    )(*scalars, *arrays)


def push_rows(scale, shown, after, wkv_ref, r_ref, head, key_ref, push_ref, rows):
    size = key_ref.shape[1]
    width = wkv_ref.shape[1] // 2
    exact, pieces = r_ref[...], []
    for _ in range(3):
        pieces.append(exact.astype(bf16).astype(f32))
        exact = exact - pieces[-1]
    heads = exact.shape[0]
    parts = nt(after, jnp.concatenate(pieces, axis=0).astype(bf16))
    high = sum(parts[:, at * heads + head : at * heads + head + 1] for at in range(3)) + 1.0
    soft = jnp.maximum(high, 0.0) + jnp.log1p(jnp.exp(-jnp.abs(high)))
    spot = lax.broadcasted_iota(jnp.int32, high.shape, 0)
    rate = jnp.where(spot < shown, soft * scale, 0.0)
    key = nn(after, wkv_ref[:, head * size : head * size + size])
    key_ref[rows, :] = (key * lax.rsqrt(jnp.mean(key * key, axis=-1, keepdims=True) + eps)).astype(bf16)
    value = nn(after, wkv_ref[:, width + head * size : width + head * size + size])
    push_ref[rows, :] = (-rate * value).astype(bf16)


def out_kernel(scale, valid_ref, attn_ref, t0, t1, wo_ref, wkv_ref, r_ref, out_ref, after_ref, key_ref, push_ref):
    count = t0.shape[0]
    for side, tok_ref in enumerate((t0, t1)):
        rows = slice(side * count, side * count + count)
        after = (tok_ref[...].astype(f32) + nn(attn_ref[rows, :], wo_ref[...])).astype(bf16)
        after_ref[rows, :] = after
        if side == 0:
            out_ref[...] = after
        push_rows(scale, valid_ref[side], after, wkv_ref, r_ref, 0, key_ref, push_ref, rows)


def again_kernel(scale, head, valid_ref, after_ref, wkv_ref, r_ref, key_ref, push_ref):
    half = after_ref.shape[0] // 2
    for side in range(2):
        rows = slice(side * half, side * half + half)
        push_rows(scale, valid_ref[side], after_ref[rows, :], wkv_ref, r_ref, head, key_ref, push_ref, rows)


def first_pushes(scale, valid, attn, t0, t1, wo, wkv, rate):
    count, width = t0.shape
    both = jax.ShapeDtypeStruct((2 * count, width // rate.shape[0]), bf16)
    return pl.pallas_call(
        functools.partial(out_kernel, scale),
        out_shape=(
            jax.ShapeDtypeStruct((count, width), bf16),
            jax.ShapeDtypeStruct((2 * count, width), bf16),
            both,
            both,
        ),
        in_specs=[smem] + [vmem] * 6,
        out_specs=[vmem] * 4,
        compiler_params=params(12),
        cost_estimate=brief,
        name="first_pushes",
    )(valid, attn, t0, t1, wo, wkv, rate)


def next_pushes(scale, valid, after, wkv, rate, head):
    rows, width = after.shape
    both = jax.ShapeDtypeStruct((rows, width // rate.shape[0]), bf16)
    return pl.pallas_call(
        functools.partial(again_kernel, scale, head),
        out_shape=(both, both),
        in_specs=[smem] + [vmem] * 3,
        out_specs=[vmem] * 2,
        compiler_params=params(12),
        cost_estimate=brief,
        name="next_pushes",
    )(valid, after, wkv, rate)


def grad_kernel(head, half, w_ref, key_ref, push_ref, out_ref):
    count, size = out_ref.shape[0], key_ref.shape[1]
    key, push = key_ref[...], push_ref[...]
    w = w_ref[head, half * count : half * count + count, :]
    act_a = nt(w[:, :size], key)
    act_b = nt(w[:, size : 2 * size], key)
    back = nt(w[:, 2 * size :], push)
    sigma = 1.0 / (1.0 + jnp.exp(-act_a))
    silu = act_a * sigma
    hidden = (silu * act_b).astype(bf16)
    grad_a = (back * act_b * sigma * (1.0 + act_a * (1.0 - sigma))).astype(bf16)
    grad_b = (back * silu).astype(bf16)
    out_ref[:, :size] = nn(grad_a, key).astype(out_ref.dtype)
    out_ref[:, size : 2 * size] = nn(grad_b, key).astype(out_ref.dtype)
    out_ref[:, 2 * size :] = nn(hidden, push).astype(out_ref.dtype)


def gradient(weights, keys, pushes, head, half, kind):
    _, rows, cols = weights.shape
    return pl.pallas_call(
        functools.partial(grad_kernel, head, half),
        out_shape=jax.ShapeDtypeStruct((rows // 2, cols), kind),
        in_specs=[vmem] * 3,
        out_specs=vmem,
        compiler_params=params(12),
        cost_estimate=brief,
        name="gradient",
    )(weights, keys, pushes)


def add_kernel(kept_ref, got_ref, sent_ref, keep_ref):
    half = keep_ref.shape[0]
    sent_ref[...] = (kept_ref[half:, :] + got_ref[half:, :].astype(f32)).astype(bf16)
    keep_ref[...] = kept_ref[:half, :] + got_ref[:half, :].astype(f32)


def add_step(kept, got):
    half = (kept.shape[0] // 2, kept.shape[1])
    return pl.pallas_call(
        add_kernel,
        out_shape=(jax.ShapeDtypeStruct(half, bf16), jax.ShapeDtypeStruct(half, f32)),
        in_specs=[vmem] * 2,
        out_specs=[vmem] * 2,
        compiler_params=params(4),
        cost_estimate=brief,
        name="add_step",
    )(kept, got)


def spread_kernel(k0_ref, g0_ref, k1_ref, g1_ref, own_ref, *sent_refs):
    rows, cols = own_ref.shape[0], k0_ref.shape[1]
    for head, (kept_ref, got_ref) in enumerate(((k0_ref, g0_ref), (k1_ref, g1_ref))):
        total = kept_ref[...] + got_ref[...].astype(f32)
        part = slice(head * cols, head * cols + cols)
        own_ref[:, part] = total[:rows]
        for at, sent_ref in enumerate(sent_refs):
            sent_ref[:, part] = total[(at + 1) * rows : (at + 2) * rows].astype(bf16)


def spread(k0, g0, k1, g1):
    shape = (k0.shape[0] // 4, 2 * k0.shape[1])
    kinds = (f32, bf16, bf16, bf16)
    return pl.pallas_call(
        spread_kernel,
        out_shape=tuple(jax.ShapeDtypeStruct(shape, kind) for kind in kinds),
        in_specs=[vmem] * 4,
        out_specs=[vmem] * 4,
        compiler_params=params(4),
        cost_estimate=brief,
        name="spread",
    )(k0, g0, k1, g1)


def rescale_kernel(start_ref, own_ref, a_ref, b_ref, c_ref, out_ref, sent_ref):
    heads, cols = start_ref.shape[0], start_ref.shape[3]
    size = cols // 3
    for head in range(heads):
        for block in range(3):
            part = slice(head * cols + block * size, head * cols + block * size + size)
            grad = own_ref[:, part]
            for got_ref in (a_ref, b_ref, c_ref):
                grad = grad + got_ref[:, part].astype(f32)
            start = start_ref[head, 0, :, block * size : block * size + size].astype(f32)
            update = start - grad
            before = jnp.sqrt(jnp.mean(start * start, axis=-1, keepdims=True) + eps)
            after = lax.rsqrt(jnp.mean(update * update, axis=-1, keepdims=True) + eps)
            fresh = (update * before * after).astype(bf16)
            out_ref[:, part] = fresh
            sent_ref[:, part] = fresh


def rescale(start, own, got):
    out = jax.ShapeDtypeStruct(own.shape, bf16)
    return pl.pallas_call(
        rescale_kernel,
        out_shape=(out, out),
        in_specs=[vmem] * 5,
        out_specs=[vmem] * 2,
        compiler_params=params(4),
        cost_estimate=brief,
        name="rescale",
    )(start, own, *got)


def collect_kernel(a_ref, b_ref, c_ref, d_ref, h0_ref, h1_ref):
    cols = h0_ref.shape[2]
    for at, got_ref in enumerate((a_ref, b_ref, c_ref, d_ref)):
        h0_ref[at] = got_ref[:, :cols]
        h1_ref[at] = got_ref[:, cols:]


def collect(blocks):
    rows, cols = blocks[0].shape
    out = jax.ShapeDtypeStruct((len(blocks), rows, cols // 2), bf16)
    held = pl.pallas_call(
        collect_kernel,
        out_shape=(out, out),
        in_specs=[vmem] * 4,
        out_specs=[vmem] * 2,
        compiler_params=params(4),
        cost_estimate=brief,
        name="collect",
    )(*blocks)
    return [part.reshape(len(blocks) * rows, cols // 2) for part in held]


def query_kernel(t_ref, s0_ref, s1_ref, w_ref, q0_ref, q1_ref):
    count = t_ref.shape[0]
    size = q0_ref.shape[1]
    for head, (s_ref, q_ref) in enumerate(((s0_ref, q0_ref), (s1_ref, q1_ref))):
        for side, rows_ref in enumerate((t_ref, s_ref)):
            q = nn(rows_ref[...], w_ref[:, head * size : head * size + size])
            unit = q * lax.rsqrt(jnp.mean(q * q, axis=-1, keepdims=True) + eps)
            q_ref[side * count : side * count + count, :] = unit.astype(bf16)


def target_queries(target, shared, weight):
    count, width = target.shape
    out = jax.ShapeDtypeStruct((2 * count, width // 2), bf16)
    return pl.pallas_call(
        query_kernel,
        out_shape=(out, out),
        in_specs=[vmem] * 4,
        out_specs=[vmem] * 2,
        compiler_params=params(8),
        cost_estimate=brief,
        name="target_queries",
    )(target, *shared, weight)


def apply_rows(q, w_ref):
    size = q.shape[1]
    act_a = nt(q, w_ref[:, :size])
    act_b = nt(q, w_ref[:, size : 2 * size])
    hidden = (act_a / (1.0 + jnp.exp(-act_a)) * act_b).astype(bf16)
    return nn(hidden, w_ref[:, 2 * size :])


def first_kernel(q_ref, w_ref, out_ref):
    out_ref[...] = apply_rows(q_ref[...], w_ref)


def apply_first(queries, weights):
    return pl.pallas_call(
        first_kernel,
        out_shape=jax.ShapeDtypeStruct((queries.shape[0], weights.shape[1] // 3), f32),
        in_specs=[vmem] * 2,
        out_specs=vmem,
        compiler_params=params(8),
        cost_estimate=brief,
        name="apply_first",
    )(queries, weights)


def last_kernel(q_ref, w_ref, sum_ref, mine_ref, theirs_ref):
    count = mine_ref.shape[0]
    total = sum_ref[...] + apply_rows(q_ref[...], w_ref)
    mine_ref[...] = total[:count]
    theirs_ref[...] = total[count:].astype(bf16)


def apply_last(queries, weights, total):
    half = (total.shape[0] // 2, total.shape[1])
    return pl.pallas_call(
        last_kernel,
        out_shape=(jax.ShapeDtypeStruct(half, f32), jax.ShapeDtypeStruct(half, bf16)),
        in_specs=[vmem] * 3,
        out_specs=[vmem] * 2,
        compiler_params=params(8),
        cost_estimate=brief,
        name="apply_last",
    )(queries, weights, total)


def merge_kernel(target_ref, w_ref, mine_ref, theirs_ref, out_ref):
    size = mine_ref.shape[1]
    fout = mine_ref[...] + theirs_ref[...].astype(f32)
    unit = (fout * lax.rsqrt(jnp.mean(fout * fout, axis=-1, keepdims=True) + eps)).astype(bf16)
    out_ref[...] = target_ref[...].astype(f32) + nn(unit, w_ref[:size, :])


def merge_first(target, weight, mine, theirs):
    return pl.pallas_call(
        merge_kernel,
        out_shape=jax.ShapeDtypeStruct(target.shape, f32),
        in_specs=[vmem] * 4,
        out_specs=vmem,
        compiler_params=params(8),
        cost_estimate=brief,
        name="merge_first",
    )(target, weight, mine, theirs)


def merge_last_kernel(used_ref, sum_ref, w_ref, mine_ref, theirs_ref, out_ref):
    size = mine_ref.shape[1]
    fout = mine_ref[...] + theirs_ref[...].astype(f32)
    unit = (fout * lax.rsqrt(jnp.mean(fout * fout, axis=-1, keepdims=True) + eps)).astype(bf16)
    total = sum_ref[...] + nn(unit, w_ref[size:, :])
    live = lax.broadcasted_iota(jnp.int32, total.shape, 0) < used_ref[0]
    out_ref[...] = jnp.where(live, total, 0.0).astype(bf16)


def merge_last(used, total, weight, mine, theirs):
    return pl.pallas_call(
        merge_last_kernel,
        out_shape=jax.ShapeDtypeStruct(total.shape, bf16),
        in_specs=[smem] + [vmem] * 4,
        out_specs=vmem,
        compiler_params=params(8),
        cost_estimate=brief,
        name="merge_last",
    )(used, total, weight, mine, theirs)


def body(
    tokens,
    attn_gain,
    qkv_weight,
    head_temp,
    out_weight,
    kv_weight,
    rate_weight,
    fast_weights,
    target,
    query_weight,
    merge_weight,
    image_lengths,
    target_counts,
):
    tok_rows, width = tokens.shape
    devices = lax.axis_size("tok")
    place = lax.axis_index("tok")
    parity = place % 2
    head_dim = width // head_temp.shape[0]
    fast_hidden, fast_cols = fast_weights.shape
    fast_heads = rate_weight.shape[1]
    rows = fast_hidden // devices
    image_ids = jnp.arange(image_lengths.shape[0], dtype=jnp.int32)
    length = jnp.sum(jnp.where(image_ids == place // 2, image_lengths, 0))
    valid = jnp.stack([length - parity * tok_rows, length - (1 - parity) * tok_rows]).astype(jnp.int32)

    moves = []
    for masks in halve_masks:
        span = [0]
        for mask in (24, 8) + masks[::-1]:
            span = span + [mask ^ at for at in span]
        moves.append(span)
    index = place ^ jnp.array(moves, dtype=jnp.int32)
    gain = attn_gain[None, :]
    rate = rate_weight.T
    sums = jax.ShapeDtypeStruct((tok_rows, 2 * width), f32)

    arrived = swap(tokens, image_mask)
    q0, k0, v0 = project_qkv(0, valid, head_temp, tokens, gain, qkv_weight)
    a0 = stage(first_stage, [head_temp], [q0, k0, v0], sums, "attend_first")
    index, target_sent, a0 = lax.optimization_barrier((index, target, a0))
    shared = [swap(target_sent, mask) for mask in share_masks]
    start = gather_rows(index, fast_weights.reshape(devices, rows, fast_cols))
    arrived, a0, start = lax.optimization_barrier((arrived, a0, start))
    weights = start.reshape(fast_heads, len(moves[0]) * rows, fast_cols // fast_heads)

    q1, k1, v1 = project_qkv(1, valid, head_temp, arrived, gain, qkv_weight)
    attn = stage(
        last_stage,
        [valid, head_temp],
        [q0, k0, v0, q1, k1, v1, a0],
        jax.ShapeDtypeStruct((2 * tok_rows, width), bf16),
        "attend_last",
    )
    attn, shared = lax.optimization_barrier((attn, shared))
    factor = rate_base / (tok_rows * devices)
    tokens_out, after, keys, pushes = first_pushes(
        factor, valid, attn, tokens, arrived, out_weight, kv_weight, rate
    )
    made = [(keys, pushes)]
    sent = [gradient(weights, keys, pushes, 0, 1, bf16)]
    after, sent[0] = lax.optimization_barrier((after, sent[0]))
    got = [swap(sent[0], halve_masks[0][0])]
    made.append(next_pushes(factor, valid, after, kv_weight, rate, 1))
    sent.append(gradient(weights, *made[1], 1, 1, bf16))
    made[0], made[1], sent[1] = lax.optimization_barrier((made[0], made[1], sent[1]))
    got.append(swap(sent[1], halve_masks[1][0]))
    kept = [gradient(weights, *made[head], head, 0, f32) for head in range(fast_heads)]
    queries = target_queries(target, shared, query_weight)
    for head in range(fast_heads):
        away, kept[head] = add_step(kept[head], got[head])
        got[head] = swap(away, halve_masks[head][1])
    kept[1], queries = lax.optimization_barrier((kept[1], queries))
    own, *pieces = spread(kept[0], got[0], kept[1], got[1])
    fresh, spare = rescale(start, own, [swap(piece, mask) for piece, mask in zip(pieces, ring_masks)])

    collected = collect([spare] + [swap(spare, mask) for mask in ring_masks])
    mine, theirs = [], []
    for head, held in enumerate(collected):
        held = jnp.concatenate([held, swap(held, double_masks[head][0])], axis=0)
        last = swap(held, double_masks[head][1])
        total = apply_first(queries[head], held)
        kept_sum, sent_sum = apply_last(queries[head], last, total)
        mine.append(kept_sum)
        theirs.append(swap(sent_sum, share_masks[head]))
    target_sum = merge_first(target, merge_weight, mine[0], theirs[0])
    target_out = merge_last(target_counts, target_sum, merge_weight, mine[1], theirs[1])
    return (tokens_out, fresh, target_out)


def solution(mesh):
    placed = (
        P(("rep", "tok"), None),
        P(),
        P(),
        P(),
        P(),
        P(),
        P(),
        P(),
        P(("rep", "tok"), None),
        P(),
        P(),
        P("rep"),
        P(("rep", "tok")),
    )
    return jax.shard_map(
        body,
        mesh=mesh,
        in_specs=placed,
        out_specs=(P(("rep", "tok"), None), P(("rep", "tok"), None), P(("rep", "tok"), None)),
        check_vma=False,
    )
```

```python
import functools
import math

import jax
import jax.numpy as jnp
from jax import lax
from jax.experimental import pallas as pl
from jax.experimental.pallas import tpu as pltpu
from jax.sharding import PartitionSpec as P

eps = 1e-06
rate_base = 4.0
safe_temp = 60.0
bf16 = jnp.bfloat16
f32 = jnp.float32

image_mask = 1
halve_masks = ((8, 24), (24, 8))
sum_masks = (3, 4, 7)
ring_masks = (24, 8, 16)
double_masks = ((1, 3), (4, 1))
share_masks = (4, 3)


def swap(value, mask):
    pairs = [(source, source ^ mask) for source in range(lax.axis_size("tok"))]
    return lax.ppermute(value, "tok", pairs)


def params(mib):
    return pltpu.CompilerParams(vmem_limit_bytes=mib * 2**20)


brief = pl.CostEstimate(flops=1, transcendentals=0, bytes_accessed=1)


def nn(a, b):
    return lax.dot_general(a, b, (((1,), (0,)), ((), ())), preferred_element_type=f32)


def nt(a, b):
    return lax.dot_general(a, b, (((1,), (1,)), ((), ())), preferred_element_type=f32)


def whole(shape):
    return pl.BlockSpec(shape, lambda *_: (0,) * len(shape))


smem = pl.BlockSpec(memory_space=pltpu.SMEM)
vmem = pl.BlockSpec(memory_space=pltpu.VMEM)


def valid_rows(lengths_ref, count):
    place = lax.axis_index("tok")
    length = lengths_ref[lax.shift_right_logical(place, 1)]
    parity = lax.bitwise_and(place, 1)
    return length - parity * count, length - (1 - parity) * count


def gather_kernel(moves, rows_ref, out_ref):
    place = lax.axis_index("tok")
    cols = out_ref.shape[-1]
    for head, span in enumerate(moves):
        for block, mask in enumerate(span):
            out_ref[head, block] = rows_ref[lax.bitwise_xor(place, mask), :, head * cols : head * cols + cols]


def gather_rows(moves, rows):
    _, height, width = rows.shape
    heads = len(moves)
    return pl.pallas_call(
        functools.partial(gather_kernel, moves),
        out_shape=jax.ShapeDtypeStruct((heads, len(moves[0]), height, width // heads), rows.dtype),
        in_specs=[vmem],
        out_specs=vmem,
        compiler_params=params(4),
        cost_estimate=brief,
        name="gather_rows",
    )(rows)


def qkv_kernel(side, lengths_ref, temp_ref, gain_ref, tok_hbm, w_hbm, q_ref, k_ref, v_ref, tok_ref, w_ref, normed, sems):
    count, width = normed.shape
    cols = 256
    copies = [pltpu.make_async_copy(tok_hbm, tok_ref, sems.at[0])]
    for group in range(width // cols):
        for part in range(3):
            lanes = slice(part * width + group * cols, part * width + group * cols + cols)
            at = 3 * group + part
            copies.append(pltpu.make_async_copy(w_hbm.at[:, lanes], w_ref.at[at], sems.at[1 + at]))
    for copy in copies:
        copy.start()
    copies[0].wait()
    x = tok_ref[...].astype(f32)
    unit = x * lax.rsqrt(jnp.mean(x * x, axis=-1, keepdims=True) + eps)
    normed[...] = (unit * gain_ref[...].astype(f32)).astype(bf16)
    shown_rows = valid_rows(lengths_ref, count)[side]
    low = lax.broadcasted_iota(jnp.int32, (count, 128), 1) < 64
    live = lax.broadcasted_iota(jnp.int32, (count, 128), 0) < shown_rows
    one = jnp.where(live, 1.0, 0.0)

    def unit_heads(t):
        square = t * t
        first = jnp.sum(jnp.where(low, square, 0.0), axis=-1, keepdims=True)
        second = jnp.sum(jnp.where(low, 0.0, square), axis=-1, keepdims=True)
        inv = [lax.rsqrt(total * (1.0 / 64.0) + eps) for total in (first, second)]
        return (t * jnp.where(low, inv[0], inv[1])).astype(bf16).astype(f32)

    for group in range(0, width, cols):
        rows = normed[...]
        first = 3 * (group // cols)
        for copy in copies[1 + first : 4 + first]:
            copy.wait()
        query, key, value = (nn(rows, w_ref[at]) for at in range(first, first + 3))
        query = query.astype(bf16).astype(f32)
        key = key.astype(bf16).astype(f32)
        for tile in range(0, cols, 128):
            part = slice(tile, tile + 128)
            head = (group + tile) // 64
            even = slice(head * 128, head * 128 + 128)
            odd = slice(head * 128 + 128, head * 128 + 256)
            scale = jnp.where(low, temp_ref[head], temp_ref[head + 1]) * (math.log2(math.e) / 64.0)
            q = unit_heads(query[:, part]) * scale
            q_high = q.astype(bf16).astype(f32)
            moved = pltpu.roll(q - q_high, 64, 1)
            q_ref[:, even] = jnp.where(low, q_high, moved).astype(bf16)
            q_ref[:, odd] = jnp.where(low, moved, q_high).astype(bf16)
            k = unit_heads(key[:, part])
            moved = pltpu.roll(k, 64, 1)
            k_ref[:, even] = jnp.where(low, k, moved).astype(bf16)
            k_ref[:, odd] = jnp.where(low, moved, k).astype(bf16)
            shown = jnp.where(live, value[:, part], 0.0)
            v_ref[:, even] = jnp.where(low, shown, one).astype(bf16)
            v_ref[:, odd] = jnp.where(low, one, shown).astype(bf16)


def project_qkv(side, lengths, temps, tokens, gain, weight):
    count, width = tokens.shape
    blocks = 3 * width // 256
    out = jax.ShapeDtypeStruct((count, 2 * width), bf16)
    hbm = pl.BlockSpec(memory_space=pltpu.HBM)
    return pl.pallas_call(
        functools.partial(qkv_kernel, side),
        out_shape=(out, out, out),
        in_specs=[smem, smem, vmem, hbm, hbm],
        out_specs=[vmem] * 3,
        scratch_shapes=[
            pltpu.VMEM((count, width), bf16),
            pltpu.VMEM((blocks, width, 256), bf16),
            pltpu.VMEM((count, width), bf16),
            pltpu.SemaphoreType.DMA((1 + blocks,)),
        ],
        compiler_params=params((47, 46)[side]),
        cost_estimate=brief,
        name="project_qkv",
    )(lengths, temps, gain, tokens, weight)


def weighted(q, keys, values, lanes):
    total = None
    for k_ref, v_ref in zip(keys, values):
        part = nn(jnp.exp2(nt(q, k_ref[:, lanes])).astype(bf16), v_ref[:, lanes])
        total = part if total is None else total + part
    return total


def finish(sums, out_ref, start, pair):
    count = sums[0].shape[0]
    low = lax.broadcasted_iota(jnp.int32, (count, 128), 1) < 64
    top = jnp.where(low, sums[0], sums[1])
    bottom = pltpu.roll(jnp.where(low, sums[1], sums[0]), 64, 1)
    out_ref[start : start + count, pl.ds(pl.multiple_of(pair * 128, 128), 128)] = (top / bottom).astype(bf16)


def pairs_of_heads(temp_ref, width, plain, other=None):
    def step(pair, _):
        lanes = [pl.ds(pl.multiple_of(pair * 256 + head * 128, 128), 128) for head in range(2)]
        safe = jnp.maximum(temp_ref[2 * pair], temp_ref[2 * pair + 1]) <= safe_temp
        pl.when(safe)(functools.partial(plain, pair, lanes))
        if other is not None:
            pl.when(jnp.logical_not(safe))(functools.partial(other, pair, lanes))
        return 0

    lax.fori_loop(0, width // 256, step, 0)


def first_stage(temp_ref, q0, k0, v0, a0):
    def plain(pair, heads):
        for lanes in heads:
            a0[:, lanes] = weighted(q0[:, lanes], [k0], [v0], lanes)

    pairs_of_heads(temp_ref, q0.shape[1], plain)


def last_stage(lengths_ref, temp_ref, q0, k0, v0, q1, k1, v1, a0, out_ref):
    count = q0.shape[0]
    keys, values = [k0, k1], [v0, v1]
    valid = valid_rows(lengths_ref, count)

    def plain(pair, heads):
        finish([a0[:, lanes] + weighted(q0[:, lanes], [k1], [v1], lanes) for lanes in heads], out_ref, 0, pair)
        finish([weighted(q1[:, lanes], keys, values, lanes) for lanes in heads], out_ref, count, pair)

    def other(pair, heads):
        for q_ref, start in zip((q0, q1), (0, count)):
            for first in range(0, count, 256):
                sums = []
                for lanes in heads:
                    scores = []
                    for at, k_ref in enumerate(keys):
                        score = nt(q_ref[first : first + 256, lanes], k_ref[:, lanes])
                        spot = lax.broadcasted_iota(jnp.int32, score.shape, 1)
                        scores.append(jnp.where(spot < valid[at], score, -1e30))
                    tops = [jnp.max(score, axis=-1, keepdims=True) for score in scores]
                    top = functools.reduce(jnp.maximum, tops)
                    total = 0.0
                    for score, v_ref in zip(scores, values):
                        total = total + nn(jnp.exp2(score - top).astype(bf16), v_ref[:, lanes])
                    sums.append(total)
                finish(sums, out_ref, start + first, pair)

    pairs_of_heads(temp_ref, q0.shape[1], plain, other)


def stage(kernel, scalars, arrays, outs, name):
    return pl.pallas_call(
        kernel,
        out_shape=outs,
        in_specs=[smem] * len(scalars) + [vmem] * len(arrays),
        out_specs=jax.tree.map(lambda out: vmem, outs),
        compiler_params=params(8),
        cost_estimate=brief,
        name=name,
    )(*scalars, *arrays)


def push_rows(scale, shown, after, wkv_ref, r_ref, head, key_ref, push_ref, rows):
    size = key_ref.shape[1]
    width = wkv_ref.shape[1] // 2
    exact, pieces = r_ref[...], []
    for _ in range(3):
        pieces.append(exact.astype(bf16).astype(f32))
        exact = exact - pieces[-1]
    heads = exact.shape[0]
    parts = nt(after, jnp.concatenate(pieces, axis=0).astype(bf16))
    high = sum(parts[:, at * heads + head : at * heads + head + 1] for at in range(3)) + 1.0
    soft = jnp.maximum(high, 0.0) + jnp.log1p(jnp.exp(-jnp.abs(high)))
    spot = lax.broadcasted_iota(jnp.int32, high.shape, 0)
    rate = jnp.where(spot < shown, soft * scale, 0.0)
    key = nn(after, wkv_ref[:, head * size : head * size + size])
    key_ref[rows, :] = (key * lax.rsqrt(jnp.mean(key * key, axis=-1, keepdims=True) + eps)).astype(bf16)
    value = nn(after, wkv_ref[:, width + head * size : width + head * size + size])
    push_ref[rows, :] = (-rate * value).astype(bf16)


def out_kernel(scale, lengths_ref, attn_ref, t0, t1, wo_ref, wkv_ref, r_ref, out_ref, after_ref, key_ref, push_ref):
    count = t0.shape[0]
    valid = valid_rows(lengths_ref, count)
    for side, tok_ref in enumerate((t0, t1)):
        rows = slice(side * count, side * count + count)
        after = (tok_ref[...].astype(f32) + nn(attn_ref[rows, :], wo_ref[...])).astype(bf16)
        after_ref[rows, :] = after
        if side == 0:
            out_ref[...] = after
        push_rows(scale, valid[side], after, wkv_ref, r_ref, 0, key_ref, push_ref, rows)


def again_kernel(scale, head, lengths_ref, after_ref, wkv_ref, r_ref, key_ref, push_ref):
    half = after_ref.shape[0] // 2
    valid = valid_rows(lengths_ref, half)
    for side in range(2):
        rows = slice(side * half, side * half + half)
        push_rows(scale, valid[side], after_ref[rows, :], wkv_ref, r_ref, head, key_ref, push_ref, rows)


def first_pushes(scale, lengths, attn, t0, t1, wo, wkv, rate):
    count, width = t0.shape
    both = jax.ShapeDtypeStruct((2 * count, width // rate.shape[0]), bf16)
    return pl.pallas_call(
        functools.partial(out_kernel, scale),
        out_shape=(
            jax.ShapeDtypeStruct((count, width), bf16),
            jax.ShapeDtypeStruct((2 * count, width), bf16),
            both,
            both,
        ),
        in_specs=[smem] + [vmem] * 6,
        out_specs=[vmem] * 4,
        compiler_params=params(12),
        cost_estimate=brief,
        name="first_pushes",
    )(lengths, attn, t0, t1, wo, wkv, rate)


def next_pushes(scale, lengths, after, wkv, rate, head):
    rows, width = after.shape
    both = jax.ShapeDtypeStruct((rows, width // rate.shape[0]), bf16)
    return pl.pallas_call(
        functools.partial(again_kernel, scale, head),
        out_shape=(both, both),
        in_specs=[smem] + [vmem] * 3,
        out_specs=[vmem] * 2,
        compiler_params=params(12),
        cost_estimate=brief,
        name="next_pushes",
    )(lengths, after, wkv, rate)


def grad_kernel(head, half, w_ref, key_ref, push_ref, out_ref):
    count, size = out_ref.shape[0], key_ref.shape[1]
    key, push = key_ref[...], push_ref[...]
    w = w_ref[head, half * count : half * count + count, :]
    act_a = nt(w[:, :size], key)
    act_b = nt(w[:, size : 2 * size], key)
    back = nt(w[:, 2 * size :], push)
    sigma = 1.0 / (1.0 + jnp.exp(-act_a))
    silu = act_a * sigma
    hidden = (silu * act_b).astype(bf16)
    grad_a = (back * act_b * sigma * (1.0 + act_a * (1.0 - sigma))).astype(bf16)
    grad_b = (back * silu).astype(bf16)
    out_ref[:, :size] = nn(grad_a, key).astype(out_ref.dtype)
    out_ref[:, size : 2 * size] = nn(grad_b, key).astype(out_ref.dtype)
    out_ref[:, 2 * size :] = nn(hidden, push).astype(out_ref.dtype)


def gradient(weights, keys, pushes, head, half, kind):
    _, rows, cols = weights.shape
    return pl.pallas_call(
        functools.partial(grad_kernel, head, half),
        out_shape=jax.ShapeDtypeStruct((rows // 2, cols), kind),
        in_specs=[vmem] * 3,
        out_specs=vmem,
        compiler_params=params(12),
        cost_estimate=brief,
        name="gradient",
    )(weights, keys, pushes)


def add_kernel(kept_ref, got_ref, sent_ref, keep_ref):
    half = keep_ref.shape[0]
    sent_ref[...] = (kept_ref[half:, :] + got_ref[half:, :].astype(f32)).astype(bf16)
    keep_ref[...] = kept_ref[:half, :] + got_ref[:half, :].astype(f32)


def add_step(kept, got):
    half = (kept.shape[0] // 2, kept.shape[1])
    return pl.pallas_call(
        add_kernel,
        out_shape=(jax.ShapeDtypeStruct(half, bf16), jax.ShapeDtypeStruct(half, f32)),
        in_specs=[vmem] * 2,
        out_specs=[vmem] * 2,
        compiler_params=params(4),
        cost_estimate=brief,
        name="add_step",
    )(kept, got)


def spread_kernel(k0_ref, g0_ref, k1_ref, g1_ref, own_ref, *sent_refs):
    rows, cols = own_ref.shape[0], k0_ref.shape[1]
    for head, (kept_ref, got_ref) in enumerate(((k0_ref, g0_ref), (k1_ref, g1_ref))):
        total = kept_ref[...] + got_ref[...].astype(f32)
        part = slice(head * cols, head * cols + cols)
        own_ref[:, part] = total[:rows]
        for at, sent_ref in enumerate(sent_refs):
            sent_ref[:, part] = total[(at + 1) * rows : (at + 2) * rows].astype(bf16)


def spread(k0, g0, k1, g1):
    shape = (k0.shape[0] // 4, 2 * k0.shape[1])
    kinds = (f32, bf16, bf16, bf16)
    return pl.pallas_call(
        spread_kernel,
        out_shape=tuple(jax.ShapeDtypeStruct(shape, kind) for kind in kinds),
        in_specs=[vmem] * 4,
        out_specs=[vmem] * 4,
        compiler_params=params(4),
        cost_estimate=brief,
        name="spread",
    )(k0, g0, k1, g1)


def rescale_kernel(start_ref, own_ref, a_ref, b_ref, c_ref, out_ref, sent_ref):
    heads, cols = start_ref.shape[0], start_ref.shape[3]
    size = cols // 3
    for head in range(heads):
        for block in range(3):
            part = slice(head * cols + block * size, head * cols + block * size + size)
            grad = own_ref[:, part]
            for got_ref in (a_ref, b_ref, c_ref):
                grad = grad + got_ref[:, part].astype(f32)
            start = start_ref[head, 0, :, block * size : block * size + size].astype(f32)
            update = start - grad
            before = jnp.sqrt(jnp.mean(start * start, axis=-1, keepdims=True) + eps)
            after = lax.rsqrt(jnp.mean(update * update, axis=-1, keepdims=True) + eps)
            fresh = (update * before * after).astype(bf16)
            out_ref[:, part] = fresh
            sent_ref[:, part] = fresh


def rescale(start, own, got):
    out = jax.ShapeDtypeStruct(own.shape, bf16)
    return pl.pallas_call(
        rescale_kernel,
        out_shape=(out, out),
        in_specs=[vmem] * 5,
        out_specs=[vmem] * 2,
        compiler_params=params(4),
        cost_estimate=brief,
        name="rescale",
    )(start, own, *got)


def collect_kernel(a_ref, b_ref, c_ref, d_ref, h0_ref, h1_ref):
    cols = h0_ref.shape[2]
    for at, got_ref in enumerate((a_ref, b_ref, c_ref, d_ref)):
        h0_ref[at] = got_ref[:, :cols]
        h1_ref[at] = got_ref[:, cols:]


def collect(blocks):
    rows, cols = blocks[0].shape
    out = jax.ShapeDtypeStruct((len(blocks), rows, cols // 2), bf16)
    held = pl.pallas_call(
        collect_kernel,
        out_shape=(out, out),
        in_specs=[vmem] * 4,
        out_specs=[vmem] * 2,
        compiler_params=params(4),
        cost_estimate=brief,
        name="collect",
    )(*blocks)
    return [part.reshape(len(blocks) * rows, cols // 2) for part in held]


def query_kernel(t_ref, s0_ref, s1_ref, w_ref, q0_ref, q1_ref):
    count = t_ref.shape[0]
    size = q0_ref.shape[1]
    for head, (s_ref, q_ref) in enumerate(((s0_ref, q0_ref), (s1_ref, q1_ref))):
        for side, rows_ref in enumerate((t_ref, s_ref)):
            q = nn(rows_ref[...], w_ref[:, head * size : head * size + size])
            unit = q * lax.rsqrt(jnp.mean(q * q, axis=-1, keepdims=True) + eps)
            q_ref[side * count : side * count + count, :] = unit.astype(bf16)


def target_queries(target, shared, weight):
    count, width = target.shape
    out = jax.ShapeDtypeStruct((2 * count, width // 2), bf16)
    return pl.pallas_call(
        query_kernel,
        out_shape=(out, out),
        in_specs=[vmem] * 4,
        out_specs=[vmem] * 2,
        compiler_params=params(8),
        cost_estimate=brief,
        name="target_queries",
    )(target, *shared, weight)


def apply_rows(q, w_ref):
    size = q.shape[1]
    act_a = nt(q, w_ref[:, :size])
    act_b = nt(q, w_ref[:, size : 2 * size])
    hidden = (act_a / (1.0 + jnp.exp(-act_a)) * act_b).astype(bf16)
    return nn(hidden, w_ref[:, 2 * size :])


def first_kernel(q_ref, w_ref, out_ref):
    out_ref[...] = apply_rows(q_ref[...], w_ref)


def apply_first(queries, weights):
    return pl.pallas_call(
        first_kernel,
        out_shape=jax.ShapeDtypeStruct((queries.shape[0], weights.shape[1] // 3), f32),
        in_specs=[vmem] * 2,
        out_specs=vmem,
        compiler_params=params(8),
        cost_estimate=brief,
        name="apply_first",
    )(queries, weights)


def last_kernel(q_ref, w_ref, sum_ref, mine_ref, theirs_ref):
    count = mine_ref.shape[0]
    total = sum_ref[...] + apply_rows(q_ref[...], w_ref)
    mine_ref[...] = total[:count]
    theirs_ref[...] = total[count:].astype(bf16)


def apply_last(queries, weights, total):
    half = (total.shape[0] // 2, total.shape[1])
    return pl.pallas_call(
        last_kernel,
        out_shape=(jax.ShapeDtypeStruct(half, f32), jax.ShapeDtypeStruct(half, bf16)),
        in_specs=[vmem] * 3,
        out_specs=[vmem] * 2,
        compiler_params=params(8),
        cost_estimate=brief,
        name="apply_last",
    )(queries, weights, total)


def merge_kernel(target_ref, w_ref, mine_ref, theirs_ref, out_ref):
    size = mine_ref.shape[1]
    fout = mine_ref[...] + theirs_ref[...].astype(f32)
    unit = (fout * lax.rsqrt(jnp.mean(fout * fout, axis=-1, keepdims=True) + eps)).astype(bf16)
    out_ref[...] = target_ref[...].astype(f32) + nn(unit, w_ref[:size, :])


def merge_first(target, weight, mine, theirs):
    return pl.pallas_call(
        merge_kernel,
        out_shape=jax.ShapeDtypeStruct(target.shape, f32),
        in_specs=[vmem] * 4,
        out_specs=vmem,
        compiler_params=params(8),
        cost_estimate=brief,
        name="merge_first",
    )(target, weight, mine, theirs)


def merge_last_kernel(used_ref, sum_ref, w_ref, mine_ref, theirs_ref, out_ref):
    size = mine_ref.shape[1]
    fout = mine_ref[...] + theirs_ref[...].astype(f32)
    unit = (fout * lax.rsqrt(jnp.mean(fout * fout, axis=-1, keepdims=True) + eps)).astype(bf16)
    total = sum_ref[...] + nn(unit, w_ref[size:, :])
    live = lax.broadcasted_iota(jnp.int32, total.shape, 0) < used_ref[0]
    out_ref[...] = jnp.where(live, total, 0.0).astype(bf16)


def merge_last(used, total, weight, mine, theirs):
    return pl.pallas_call(
        merge_last_kernel,
        out_shape=jax.ShapeDtypeStruct(total.shape, bf16),
        in_specs=[smem] + [vmem] * 4,
        out_specs=vmem,
        compiler_params=params(8),
        cost_estimate=brief,
        name="merge_last",
    )(used, total, weight, mine, theirs)


def body(
    tokens,
    attn_gain,
    qkv_weight,
    head_temp,
    out_weight,
    kv_weight,
    rate_weight,
    fast_weights,
    target,
    query_weight,
    merge_weight,
    image_lengths,
    target_counts,
):
    tok_rows, width = tokens.shape
    devices = lax.axis_size("tok")
    fast_hidden, fast_cols = fast_weights.shape
    fast_heads = rate_weight.shape[1]
    rows = fast_hidden // devices
    moves = []
    for masks in halve_masks:
        span = [0]
        for mask in sum_masks[:2] + masks[::-1]:
            span = span + [mask ^ at for at in span]
        moves.append(span)
    gain = attn_gain[None, :]
    rate = rate_weight.T
    sums = jax.ShapeDtypeStruct((tok_rows, 2 * width), f32)

    arrived = swap(tokens, image_mask)
    q0, k0, v0 = project_qkv(0, image_lengths, head_temp, tokens, gain, qkv_weight)
    a0 = stage(first_stage, [head_temp], [q0, k0, v0], sums, "attend_first")
    fast_blocks, a0 = lax.optimization_barrier((fast_weights.reshape(devices, rows, fast_cols), a0))
    start = gather_rows(moves, fast_blocks)
    arrived, a0, start = lax.optimization_barrier((arrived, a0, start))
    weights = start.reshape(fast_heads, len(moves[0]) * rows, fast_cols // fast_heads)

    q1, k1, v1 = project_qkv(1, image_lengths, head_temp, arrived, gain, qkv_weight)
    attn = stage(
        last_stage,
        [image_lengths, head_temp],
        [q0, k0, v0, q1, k1, v1, a0],
        jax.ShapeDtypeStruct((2 * tok_rows, width), bf16),
        "attend_last",
    )
    factor = rate_base / (tok_rows * devices)
    tokens_out, after, keys, pushes = first_pushes(
        factor, image_lengths, attn, tokens, arrived, out_weight, kv_weight, rate
    )
    made = [(keys, pushes)]
    sent = [gradient(weights, keys, pushes, 0, 1, bf16)]
    after, sent[0] = lax.optimization_barrier((after, sent[0]))
    got = [swap(sent[0], halve_masks[0][0])]
    made.append(next_pushes(factor, image_lengths, after, kv_weight, rate, 1))
    sent.append(gradient(weights, *made[1], 1, 1, bf16))
    made[0], made[1], sent[1], given = lax.optimization_barrier((made[0], made[1], sent[1], target))
    got.append(swap(sent[1], halve_masks[1][0]))
    shared = [swap(given, mask) for mask in share_masks]
    kept = [gradient(weights, *made[head], head, 0, f32) for head in range(fast_heads)]
    queries = target_queries(target, shared, query_weight)
    for head in range(fast_heads):
        away, kept[head] = add_step(kept[head], got[head])
        got[head] = swap(away, halve_masks[head][1])
    kept[1], queries = lax.optimization_barrier((kept[1], queries))
    own, *pieces = spread(kept[0], got[0], kept[1], got[1])
    fresh, spare = rescale(start, own, [swap(piece, mask) for piece, mask in zip(pieces, sum_masks)])

    collected = collect([spare] + [swap(spare, mask) for mask in ring_masks])
    mine, theirs = [], []
    for head, held in enumerate(collected):
        held = jnp.concatenate([held, swap(held, double_masks[head][0])], axis=0)
        last = swap(held, double_masks[head][1])
        total = apply_first(queries[head], held)
        kept_sum, sent_sum = apply_last(queries[head], last, total)
        mine.append(kept_sum)
        theirs.append(swap(sent_sum, share_masks[head]))
    target_sum = merge_first(target, merge_weight, mine[0], theirs[0])
    target_out = merge_last(target_counts, target_sum, merge_weight, mine[1], theirs[1])
    return (tokens_out, fresh, target_out)


def solution(mesh):
    placed = (
        P(("rep", "tok"), None),
        P(),
        P(),
        P(),
        P(),
        P(),
        P(),
        P(),
        P(("rep", "tok"), None),
        P(),
        P(),
        P("rep"),
        P(("rep", "tok")),
    )
    return jax.shard_map(
        body,
        mesh=mesh,
        in_specs=placed,
        out_specs=(P(("rep", "tok"), None), P(("rep", "tok"), None), P(("rep", "tok"), None)),
        check_vma=False,
    )
```

```python
import functools
import math

import jax
import jax.numpy as jnp
from jax import lax
from jax.experimental import pallas as pl
from jax.experimental.pallas import tpu as pltpu
from jax.sharding import PartitionSpec as P

eps = 1e-06
rate_base = 4.0
safe_temp = 60.0
bf16 = jnp.bfloat16
f32 = jnp.float32

image_mask = (1, 1)
halve_masks = (((3, 8), (4, 24)), ((4, 24), (3, 8)))
ring_masks = ((24, 3), (8, 4), (16, 7))
double_masks = (((3, 1), (4, 24)), ((4, 24), (1, 8)))
share_masks = ((1, 8), (3, 1))


def swap(value, masks):
    reps, places = lax.axis_size("rep"), lax.axis_size("tok")
    pairs = [
        (place * reps + rep, (place ^ masks[rep % 2]) * reps + rep) for place in range(places) for rep in range(reps)
    ]
    return lax.ppermute(value, ("tok", "rep"), pairs)


def params(mib):
    return pltpu.CompilerParams(vmem_limit_bytes=mib * 2**20)


brief = pl.CostEstimate(flops=1, transcendentals=0, bytes_accessed=1)


def nn(a, b):
    return lax.dot_general(a, b, (((1,), (0,)), ((), ())), preferred_element_type=f32)


def nt(a, b):
    return lax.dot_general(a, b, (((1,), (1,)), ((), ())), preferred_element_type=f32)


def whole(shape):
    return pl.BlockSpec(shape, lambda *_: (0,) * len(shape))


smem = pl.BlockSpec(memory_space=pltpu.SMEM)
vmem = pl.BlockSpec(memory_space=pltpu.VMEM)


def valid_rows(lengths_ref, count):
    place = lax.axis_index("tok")
    length = lengths_ref[lax.shift_right_logical(place, 1)]
    parity = lax.bitwise_and(place, 1)
    return length - parity * count, length - (1 - parity) * count


def gather_kernel(moves, rows_ref, out_ref):
    place = lax.axis_index("tok")
    core = lax.bitwise_and(lax.axis_index("rep"), 1)
    cols = out_ref.shape[-1]
    for head, span in enumerate(moves):
        for block, (mask, other) in enumerate(span):
            owner = lax.bitwise_xor(place, mask + core * (other - mask))
            out_ref[head, block] = rows_ref[owner, :, head * cols : head * cols + cols]


def gather_rows(moves, rows):
    _, height, width = rows.shape
    heads = len(moves)
    return pl.pallas_call(
        functools.partial(gather_kernel, moves),
        out_shape=jax.ShapeDtypeStruct((heads, len(moves[0]), height, width // heads), rows.dtype),
        in_specs=[vmem],
        out_specs=vmem,
        compiler_params=params(4),
        cost_estimate=brief,
        name="gather_rows",
    )(rows)


def qkv_kernel(side, lengths_ref, temp_ref, gain_ref, tok_ref, w_ref, q_ref, k_ref, v_ref, normed):
    count, width = normed.shape
    cols = 256
    x = tok_ref[...].astype(f32)
    unit = x * lax.rsqrt(jnp.mean(x * x, axis=-1, keepdims=True) + eps)
    normed[...] = (unit * gain_ref[...].astype(f32)).astype(bf16)
    shown_rows = valid_rows(lengths_ref, count)[side]
    low = lax.broadcasted_iota(jnp.int32, (count, 128), 1) < 64
    live = lax.broadcasted_iota(jnp.int32, (count, 128), 0) < shown_rows
    one = jnp.where(live, 1.0, 0.0)

    def unit_heads(t):
        square = t * t
        first = jnp.sum(jnp.where(low, square, 0.0), axis=-1, keepdims=True)
        second = jnp.sum(jnp.where(low, 0.0, square), axis=-1, keepdims=True)
        inv = [lax.rsqrt(total * (1.0 / 64.0) + eps) for total in (first, second)]
        return (t * jnp.where(low, inv[0], inv[1])).astype(bf16).astype(f32)

    for group in range(0, width, cols):
        rows = normed[...]
        query, key, value = (nn(rows, w_ref[:, at + group : at + group + cols]) for at in (0, width, 2 * width))
        query = query.astype(bf16).astype(f32)
        key = key.astype(bf16).astype(f32)
        for tile in range(0, cols, 128):
            part = slice(tile, tile + 128)
            head = (group + tile) // 64
            even = slice(head * 128, head * 128 + 128)
            odd = slice(head * 128 + 128, head * 128 + 256)
            scale = jnp.where(low, temp_ref[head], temp_ref[head + 1]) * (math.log2(math.e) / 64.0)
            q = unit_heads(query[:, part]) * scale
            q_high = q.astype(bf16).astype(f32)
            moved = pltpu.roll(q - q_high, 64, 1)
            q_ref[:, even] = jnp.where(low, q_high, moved).astype(bf16)
            q_ref[:, odd] = jnp.where(low, moved, q_high).astype(bf16)
            k = unit_heads(key[:, part])
            moved = pltpu.roll(k, 64, 1)
            k_ref[:, even] = jnp.where(low, k, moved).astype(bf16)
            k_ref[:, odd] = jnp.where(low, moved, k).astype(bf16)
            shown = jnp.where(live, value[:, part], 0.0)
            v_ref[:, even] = jnp.where(low, shown, one).astype(bf16)
            v_ref[:, odd] = jnp.where(low, one, shown).astype(bf16)


def project_qkv(side, lengths, temps, tokens, gain, weight):
    count, width = tokens.shape
    out = jax.ShapeDtypeStruct((count, 2 * width), bf16)
    return pl.pallas_call(
        functools.partial(qkv_kernel, side),
        out_shape=(out, out, out),
        in_specs=[smem, smem] + [vmem] * 3,
        out_specs=[vmem] * 3,
        scratch_shapes=[pltpu.VMEM((count, width), bf16)],
        compiler_params=params(8),
        cost_estimate=brief,
        name="project_qkv",
    )(lengths, temps, gain, tokens, weight)


def weighted(q, keys, values, lanes):
    total = None
    for k_ref, v_ref in zip(keys, values):
        part = nn(jnp.exp2(nt(q, k_ref[:, lanes])).astype(bf16), v_ref[:, lanes])
        total = part if total is None else total + part
    return total


def finish(sums, out_ref, start, pair):
    count = sums[0].shape[0]
    low = lax.broadcasted_iota(jnp.int32, (count, 128), 1) < 64
    top = jnp.where(low, sums[0], sums[1])
    bottom = pltpu.roll(jnp.where(low, sums[1], sums[0]), 64, 1)
    out_ref[start : start + count, pl.ds(pl.multiple_of(pair * 128, 128), 128)] = (top / bottom).astype(bf16)


def pairs_of_heads(temp_ref, width, plain, other=None):
    def step(pair, _):
        lanes = [pl.ds(pl.multiple_of(pair * 256 + head * 128, 128), 128) for head in range(2)]
        safe = jnp.maximum(temp_ref[2 * pair], temp_ref[2 * pair + 1]) <= safe_temp
        pl.when(safe)(functools.partial(plain, pair, lanes))
        if other is not None:
            pl.when(jnp.logical_not(safe))(functools.partial(other, pair, lanes))
        return 0

    lax.fori_loop(0, width // 256, step, 0)


def first_stage(temp_ref, q0, k0, v0, a0):
    def plain(pair, heads):
        for lanes in heads:
            a0[:, lanes] = weighted(q0[:, lanes], [k0], [v0], lanes)

    pairs_of_heads(temp_ref, q0.shape[1], plain)


def last_stage(lengths_ref, temp_ref, q0, k0, v0, q1, k1, v1, a0, out_ref):
    count = q0.shape[0]
    keys, values = [k0, k1], [v0, v1]
    valid = valid_rows(lengths_ref, count)

    def plain(pair, heads):
        finish([a0[:, lanes] + weighted(q0[:, lanes], [k1], [v1], lanes) for lanes in heads], out_ref, 0, pair)
        finish([weighted(q1[:, lanes], keys, values, lanes) for lanes in heads], out_ref, count, pair)

    def other(pair, heads):
        for q_ref, start in zip((q0, q1), (0, count)):
            for first in range(0, count, 256):
                sums = []
                for lanes in heads:
                    scores = []
                    for at, k_ref in enumerate(keys):
                        score = nt(q_ref[first : first + 256, lanes], k_ref[:, lanes])
                        spot = lax.broadcasted_iota(jnp.int32, score.shape, 1)
                        scores.append(jnp.where(spot < valid[at], score, -1e30))
                    tops = [jnp.max(score, axis=-1, keepdims=True) for score in scores]
                    top = functools.reduce(jnp.maximum, tops)
                    total = 0.0
                    for score, v_ref in zip(scores, values):
                        total = total + nn(jnp.exp2(score - top).astype(bf16), v_ref[:, lanes])
                    sums.append(total)
                finish(sums, out_ref, start + first, pair)

    pairs_of_heads(temp_ref, q0.shape[1], plain, other)


def stage(kernel, scalars, arrays, outs, name):
    return pl.pallas_call(
        kernel,
        out_shape=outs,
        in_specs=[smem] * len(scalars) + [vmem] * len(arrays),
        out_specs=jax.tree.map(lambda out: vmem, outs),
        compiler_params=params(8),
        cost_estimate=brief,
        name=name,
    )(*scalars, *arrays)


def push_rows(scale, shown, after, wkv_ref, r_ref, head, key_ref, push_ref, rows):
    size = key_ref.shape[1]
    width = wkv_ref.shape[1] // 2
    exact, pieces = r_ref[...], []
    for _ in range(3):
        pieces.append(exact.astype(bf16).astype(f32))
        exact = exact - pieces[-1]
    heads = exact.shape[0]
    parts = nt(after, jnp.concatenate(pieces, axis=0).astype(bf16))
    high = sum(parts[:, at * heads + head : at * heads + head + 1] for at in range(3)) + 1.0
    soft = jnp.maximum(high, 0.0) + jnp.log1p(jnp.exp(-jnp.abs(high)))
    spot = lax.broadcasted_iota(jnp.int32, high.shape, 0)
    rate = jnp.where(spot < shown, soft * scale, 0.0)
    key = nn(after, wkv_ref[:, head * size : head * size + size])
    key_ref[rows, :] = (key * lax.rsqrt(jnp.mean(key * key, axis=-1, keepdims=True) + eps)).astype(bf16)
    value = nn(after, wkv_ref[:, width + head * size : width + head * size + size])
    push_ref[rows, :] = (-rate * value).astype(bf16)


def out_kernel(scale, lengths_ref, attn_ref, t0, t1, wo_ref, wkv_ref, r_ref, out_ref, after_ref, key_ref, push_ref):
    count = t0.shape[0]
    valid = valid_rows(lengths_ref, count)
    for side, tok_ref in enumerate((t0, t1)):
        rows = slice(side * count, side * count + count)
        after = (tok_ref[...].astype(f32) + nn(attn_ref[rows, :], wo_ref[...])).astype(bf16)
        after_ref[rows, :] = after
        if side == 0:
            out_ref[...] = after
        push_rows(scale, valid[side], after, wkv_ref, r_ref, 0, key_ref, push_ref, rows)


def again_kernel(scale, head, lengths_ref, after_ref, wkv_ref, r_ref, key_ref, push_ref):
    half = after_ref.shape[0] // 2
    valid = valid_rows(lengths_ref, half)
    for side in range(2):
        rows = slice(side * half, side * half + half)
        push_rows(scale, valid[side], after_ref[rows, :], wkv_ref, r_ref, head, key_ref, push_ref, rows)


def first_pushes(scale, lengths, attn, t0, t1, wo, wkv, rate):
    count, width = t0.shape
    both = jax.ShapeDtypeStruct((2 * count, width // rate.shape[0]), bf16)
    return pl.pallas_call(
        functools.partial(out_kernel, scale),
        out_shape=(
            jax.ShapeDtypeStruct((count, width), bf16),
            jax.ShapeDtypeStruct((2 * count, width), bf16),
            both,
            both,
        ),
        in_specs=[smem] + [vmem] * 6,
        out_specs=[vmem] * 4,
        compiler_params=params(12),
        cost_estimate=brief,
        name="first_pushes",
    )(lengths, attn, t0, t1, wo, wkv, rate)


def next_pushes(scale, lengths, after, wkv, rate, head):
    rows, width = after.shape
    both = jax.ShapeDtypeStruct((rows, width // rate.shape[0]), bf16)
    return pl.pallas_call(
        functools.partial(again_kernel, scale, head),
        out_shape=(both, both),
        in_specs=[smem] + [vmem] * 3,
        out_specs=[vmem] * 2,
        compiler_params=params(12),
        cost_estimate=brief,
        name="next_pushes",
    )(lengths, after, wkv, rate)


def grad_kernel(head, half, w_ref, key_ref, push_ref, out_ref):
    count, size = out_ref.shape[0], key_ref.shape[1]
    key, push = key_ref[...], push_ref[...]
    w = w_ref[head, half * count : half * count + count, :]
    act_a = nt(w[:, :size], key)
    act_b = nt(w[:, size : 2 * size], key)
    back = nt(w[:, 2 * size :], push)
    sigma = 1.0 / (1.0 + jnp.exp(-act_a))
    silu = act_a * sigma
    hidden = (silu * act_b).astype(bf16)
    grad_a = (back * act_b * sigma * (1.0 + act_a * (1.0 - sigma))).astype(bf16)
    grad_b = (back * silu).astype(bf16)
    out_ref[:, :size] = nn(grad_a, key).astype(out_ref.dtype)
    out_ref[:, size : 2 * size] = nn(grad_b, key).astype(out_ref.dtype)
    out_ref[:, 2 * size :] = nn(hidden, push).astype(out_ref.dtype)


def gradient(weights, keys, pushes, head, half, kind):
    _, rows, cols = weights.shape
    return pl.pallas_call(
        functools.partial(grad_kernel, head, half),
        out_shape=jax.ShapeDtypeStruct((rows // 2, cols), kind),
        in_specs=[vmem] * 3,
        out_specs=vmem,
        compiler_params=params(12),
        cost_estimate=brief,
        name="gradient",
    )(weights, keys, pushes)


def add_kernel(kept_ref, got_ref, sent_ref, keep_ref):
    half = keep_ref.shape[0]
    sent_ref[...] = (kept_ref[half:, :] + got_ref[half:, :].astype(f32)).astype(bf16)
    keep_ref[...] = kept_ref[:half, :] + got_ref[:half, :].astype(f32)


def add_step(kept, got):
    half = (kept.shape[0] // 2, kept.shape[1])
    return pl.pallas_call(
        add_kernel,
        out_shape=(jax.ShapeDtypeStruct(half, bf16), jax.ShapeDtypeStruct(half, f32)),
        in_specs=[vmem] * 2,
        out_specs=[vmem] * 2,
        compiler_params=params(4),
        cost_estimate=brief,
        name="add_step",
    )(kept, got)


def spread_kernel(k0_ref, g0_ref, k1_ref, g1_ref, own_ref, *sent_refs):
    rows, cols = own_ref.shape[0], k0_ref.shape[1]
    for head, (kept_ref, got_ref) in enumerate(((k0_ref, g0_ref), (k1_ref, g1_ref))):
        total = kept_ref[...] + got_ref[...].astype(f32)
        part = slice(head * cols, head * cols + cols)
        own_ref[:, part] = total[:rows]
        for at, sent_ref in enumerate(sent_refs):
            sent_ref[:, part] = total[(at + 1) * rows : (at + 2) * rows].astype(bf16)


def spread(k0, g0, k1, g1):
    shape = (k0.shape[0] // 4, 2 * k0.shape[1])
    kinds = (f32, bf16, bf16, bf16)
    return pl.pallas_call(
        spread_kernel,
        out_shape=tuple(jax.ShapeDtypeStruct(shape, kind) for kind in kinds),
        in_specs=[vmem] * 4,
        out_specs=[vmem] * 4,
        compiler_params=params(4),
        cost_estimate=brief,
        name="spread",
    )(k0, g0, k1, g1)


def rescale_kernel(start_ref, own_ref, a_ref, b_ref, c_ref, out_ref, sent_ref):
    heads, cols = start_ref.shape[0], start_ref.shape[3]
    size = cols // 3
    for head in range(heads):
        for block in range(3):
            part = slice(head * cols + block * size, head * cols + block * size + size)
            grad = own_ref[:, part]
            for got_ref in (a_ref, b_ref, c_ref):
                grad = grad + got_ref[:, part].astype(f32)
            start = start_ref[head, 0, :, block * size : block * size + size].astype(f32)
            update = start - grad
            before = jnp.sqrt(jnp.mean(start * start, axis=-1, keepdims=True) + eps)
            after = lax.rsqrt(jnp.mean(update * update, axis=-1, keepdims=True) + eps)
            fresh = (update * before * after).astype(bf16)
            out_ref[:, part] = fresh
            sent_ref[:, part] = fresh


def rescale(start, own, got):
    out = jax.ShapeDtypeStruct(own.shape, bf16)
    return pl.pallas_call(
        rescale_kernel,
        out_shape=(out, out),
        in_specs=[vmem] * 5,
        out_specs=[vmem] * 2,
        compiler_params=params(4),
        cost_estimate=brief,
        name="rescale",
    )(start, own, *got)


def collect_kernel(a_ref, b_ref, c_ref, d_ref, h0_ref, h1_ref):
    cols = h0_ref.shape[2]
    for at, got_ref in enumerate((a_ref, b_ref, c_ref, d_ref)):
        h0_ref[at] = got_ref[:, :cols]
        h1_ref[at] = got_ref[:, cols:]


def collect(blocks):
    rows, cols = blocks[0].shape
    out = jax.ShapeDtypeStruct((len(blocks), rows, cols // 2), bf16)
    held = pl.pallas_call(
        collect_kernel,
        out_shape=(out, out),
        in_specs=[vmem] * 4,
        out_specs=[vmem] * 2,
        compiler_params=params(4),
        cost_estimate=brief,
        name="collect",
    )(*blocks)
    return [part.reshape(len(blocks) * rows, cols // 2) for part in held]


def query_kernel(t_ref, s0_ref, s1_ref, w_ref, q0_ref, q1_ref):
    count = t_ref.shape[0]
    size = q0_ref.shape[1]
    for head, (s_ref, q_ref) in enumerate(((s0_ref, q0_ref), (s1_ref, q1_ref))):
        for side, rows_ref in enumerate((t_ref, s_ref)):
            q = nn(rows_ref[...], w_ref[:, head * size : head * size + size])
            unit = q * lax.rsqrt(jnp.mean(q * q, axis=-1, keepdims=True) + eps)
            q_ref[side * count : side * count + count, :] = unit.astype(bf16)


def target_queries(target, shared, weight):
    count, width = target.shape
    out = jax.ShapeDtypeStruct((2 * count, width // 2), bf16)
    return pl.pallas_call(
        query_kernel,
        out_shape=(out, out),
        in_specs=[vmem] * 4,
        out_specs=[vmem] * 2,
        compiler_params=params(8),
        cost_estimate=brief,
        name="target_queries",
    )(target, *shared, weight)


def apply_rows(q, w_ref):
    size = q.shape[1]
    act_a = nt(q, w_ref[:, :size])
    act_b = nt(q, w_ref[:, size : 2 * size])
    hidden = (act_a / (1.0 + jnp.exp(-act_a)) * act_b).astype(bf16)
    return nn(hidden, w_ref[:, 2 * size :])


def first_kernel(q_ref, w_ref, out_ref):
    out_ref[...] = apply_rows(q_ref[...], w_ref)


def apply_first(queries, weights):
    return pl.pallas_call(
        first_kernel,
        out_shape=jax.ShapeDtypeStruct((queries.shape[0], weights.shape[1] // 3), f32),
        in_specs=[vmem] * 2,
        out_specs=vmem,
        compiler_params=params(8),
        cost_estimate=brief,
        name="apply_first",
    )(queries, weights)


def last_kernel(q_ref, w_ref, sum_ref, mine_ref, theirs_ref):
    count = mine_ref.shape[0]
    total = sum_ref[...] + apply_rows(q_ref[...], w_ref)
    mine_ref[...] = total[:count]
    theirs_ref[...] = total[count:].astype(bf16)


def apply_last(queries, weights, total):
    half = (total.shape[0] // 2, total.shape[1])
    return pl.pallas_call(
        last_kernel,
        out_shape=(jax.ShapeDtypeStruct(half, f32), jax.ShapeDtypeStruct(half, bf16)),
        in_specs=[vmem] * 3,
        out_specs=[vmem] * 2,
        compiler_params=params(8),
        cost_estimate=brief,
        name="apply_last",
    )(queries, weights, total)


def merge_kernel(target_ref, w_ref, mine_ref, theirs_ref, out_ref):
    size = mine_ref.shape[1]
    fout = mine_ref[...] + theirs_ref[...].astype(f32)
    unit = (fout * lax.rsqrt(jnp.mean(fout * fout, axis=-1, keepdims=True) + eps)).astype(bf16)
    out_ref[...] = target_ref[...].astype(f32) + nn(unit, w_ref[:size, :])


def merge_first(target, weight, mine, theirs):
    return pl.pallas_call(
        merge_kernel,
        out_shape=jax.ShapeDtypeStruct(target.shape, f32),
        in_specs=[vmem] * 4,
        out_specs=vmem,
        compiler_params=params(8),
        cost_estimate=brief,
        name="merge_first",
    )(target, weight, mine, theirs)


def merge_last_kernel(used_ref, sum_ref, w_ref, mine_ref, theirs_ref, out_ref):
    size = mine_ref.shape[1]
    fout = mine_ref[...] + theirs_ref[...].astype(f32)
    unit = (fout * lax.rsqrt(jnp.mean(fout * fout, axis=-1, keepdims=True) + eps)).astype(bf16)
    total = sum_ref[...] + nn(unit, w_ref[size:, :])
    live = lax.broadcasted_iota(jnp.int32, total.shape, 0) < used_ref[0]
    out_ref[...] = jnp.where(live, total, 0.0).astype(bf16)


def merge_last(used, total, weight, mine, theirs):
    return pl.pallas_call(
        merge_last_kernel,
        out_shape=jax.ShapeDtypeStruct(total.shape, bf16),
        in_specs=[smem] + [vmem] * 4,
        out_specs=vmem,
        compiler_params=params(8),
        cost_estimate=brief,
        name="merge_last",
    )(used, total, weight, mine, theirs)


def body(
    tokens,
    attn_gain,
    qkv_weight,
    head_temp,
    out_weight,
    kv_weight,
    rate_weight,
    fast_weights,
    target,
    query_weight,
    merge_weight,
    image_lengths,
    target_counts,
):
    tok_rows, width = tokens.shape
    devices = lax.axis_size("tok")
    fast_hidden, fast_cols = fast_weights.shape
    fast_heads = rate_weight.shape[1]
    rows = fast_hidden // devices
    moves = []
    for masks in halve_masks:
        span = [(0, 0)]
        for first, second in ring_masks[:2] + masks[::-1]:
            span = span + [(first ^ at, second ^ to) for at, to in span]
        moves.append(span)
    gain = attn_gain[None, :]
    rate = rate_weight.T
    sums = jax.ShapeDtypeStruct((tok_rows, 2 * width), f32)

    arrived = swap(tokens, image_mask)
    q0, k0, v0 = project_qkv(0, image_lengths, head_temp, tokens, gain, qkv_weight)
    a0 = stage(first_stage, [head_temp], [q0, k0, v0], sums, "attend_first")
    fast_blocks = fast_weights.reshape(devices, rows, fast_cols)
    fast_blocks, given, a0 = lax.optimization_barrier((fast_blocks, target, a0))
    shared = [swap(given, masks) for masks in share_masks]
    start = gather_rows(moves, fast_blocks)
    arrived, a0, start = lax.optimization_barrier((arrived, a0, start))
    weights = start.reshape(fast_heads, len(moves[0]) * rows, fast_cols // fast_heads)

    q1, k1, v1 = project_qkv(1, image_lengths, head_temp, arrived, gain, qkv_weight)
    attn = stage(
        last_stage,
        [image_lengths, head_temp],
        [q0, k0, v0, q1, k1, v1, a0],
        jax.ShapeDtypeStruct((2 * tok_rows, width), bf16),
        "attend_last",
    )
    attn, shared = lax.optimization_barrier((attn, shared))
    factor = rate_base / (tok_rows * devices)
    tokens_out, after, keys, pushes = first_pushes(
        factor, image_lengths, attn, tokens, arrived, out_weight, kv_weight, rate
    )
    made = [(keys, pushes)]
    sent = [gradient(weights, keys, pushes, 0, 1, bf16)]
    after, sent[0] = lax.optimization_barrier((after, sent[0]))
    got = [swap(sent[0], halve_masks[0][0])]
    made.append(next_pushes(factor, image_lengths, after, kv_weight, rate, 1))
    sent.append(gradient(weights, *made[1], 1, 1, bf16))
    made[0], made[1], sent[1] = lax.optimization_barrier((made[0], made[1], sent[1]))
    got.append(swap(sent[1], halve_masks[1][0]))
    kept = [gradient(weights, *made[head], head, 0, f32) for head in range(fast_heads)]
    for head in range(fast_heads):
        away, kept[head] = add_step(kept[head], got[head])
        got[head] = swap(away, halve_masks[head][1])
    queries = target_queries(target, shared, query_weight)
    kept[1], queries = lax.optimization_barrier((kept[1], queries))
    own, *pieces = spread(kept[0], got[0], kept[1], got[1])
    fresh, spare = rescale(start, own, [swap(piece, masks) for piece, masks in zip(pieces, ring_masks)])

    collected = collect([spare] + [swap(spare, mask) for mask in ring_masks])
    mine, theirs = [], []
    for head, held in enumerate(collected):
        held = jnp.concatenate([held, swap(held, double_masks[head][0])], axis=0)
        last = swap(held, double_masks[head][1])
        total = apply_first(queries[head], held)
        kept_sum, sent_sum = apply_last(queries[head], last, total)
        mine.append(kept_sum)
        theirs.append(swap(sent_sum, share_masks[head]))
    target_sum = merge_first(target, merge_weight, mine[0], theirs[0])
    target_out = merge_last(target_counts, target_sum, merge_weight, mine[1], theirs[1])
    return (tokens_out, fresh, target_out)


def solution(mesh):
    placed = (
        P(("rep", "tok"), None),
        P(),
        P(),
        P(),
        P(),
        P(),
        P(),
        P(),
        P(("rep", "tok"), None),
        P(),
        P(),
        P("rep"),
        P(("rep", "tok")),
    )
    return jax.shard_map(
        body,
        mesh=mesh,
        in_specs=placed,
        out_specs=(P(("rep", "tok"), None), P(("rep", "tok"), None), P(("rep", "tok"), None)),
        check_vma=False,
    )
```

```python
import functools
import math

import jax
import jax.numpy as jnp
from jax import lax
from jax.experimental import pallas as pl
from jax.experimental.pallas import tpu as pltpu
from jax.sharding import PartitionSpec as P

eps = 1e-06
rate_base = 4.0
safe_temp = 60.0
bf16 = jnp.bfloat16
f32 = jnp.float32

image_mask = (1, 1)
halve_masks = (((3, 8), (4, 24)), ((4, 24), (3, 8)))
ring_masks = ((24, 3), (8, 4), (16, 7))
double_masks = halve_masks
share_mask = (1, 1)


def swap(value, masks):
    reps, places = lax.axis_size("rep"), lax.axis_size("tok")
    pairs = [
        (place * reps + rep, (place ^ masks[rep % 2]) * reps + rep) for place in range(places) for rep in range(reps)
    ]
    return lax.ppermute(value, ("tok", "rep"), pairs)


def params(mib):
    return pltpu.CompilerParams(vmem_limit_bytes=mib * 2**20)


brief = pl.CostEstimate(flops=1, transcendentals=0, bytes_accessed=1)


def nn(a, b):
    return lax.dot_general(a, b, (((1,), (0,)), ((), ())), preferred_element_type=f32)


def nt(a, b):
    return lax.dot_general(a, b, (((1,), (1,)), ((), ())), preferred_element_type=f32)


def whole(shape):
    return pl.BlockSpec(shape, lambda *_: (0,) * len(shape))


smem = pl.BlockSpec(memory_space=pltpu.SMEM)
vmem = pl.BlockSpec(memory_space=pltpu.VMEM)


def valid_rows(lengths_ref, count):
    place = lax.axis_index("tok")
    length = lengths_ref[lax.shift_right_logical(place, 1)]
    parity = lax.bitwise_and(place, 1)
    return length - parity * count, length - (1 - parity) * count


def gather_kernel(moves, rows_ref, out_ref):
    place = lax.axis_index("tok")
    core = lax.bitwise_and(lax.axis_index("rep"), 1)
    cols = out_ref.shape[-1]
    for head, span in enumerate(moves):
        for block, (mask, other) in enumerate(span):
            owner = lax.bitwise_xor(place, mask + core * (other - mask))
            out_ref[head, block] = rows_ref[owner, :, head * cols : head * cols + cols]


def gather_rows(moves, rows):
    _, height, width = rows.shape
    heads = len(moves)
    return pl.pallas_call(
        functools.partial(gather_kernel, moves),
        out_shape=jax.ShapeDtypeStruct((heads, len(moves[0]), height, width // heads), rows.dtype),
        in_specs=[vmem],
        out_specs=vmem,
        compiler_params=params(4),
        cost_estimate=brief,
        name="gather_rows",
    )(rows)


def qkv_kernel(side, lengths_ref, temp_ref, gain_ref, tok_ref, w_ref, q_ref, k_ref, v_ref, normed):
    count, width = normed.shape
    cols = 256
    x = tok_ref[...].astype(f32)
    unit = x * lax.rsqrt(jnp.mean(x * x, axis=-1, keepdims=True) + eps)
    normed[...] = (unit * gain_ref[...].astype(f32)).astype(bf16)
    shown_rows = valid_rows(lengths_ref, count)[side]
    low = lax.broadcasted_iota(jnp.int32, (count, 128), 1) < 64
    live = lax.broadcasted_iota(jnp.int32, (count, 128), 0) < shown_rows
    one = jnp.where(live, 1.0, 0.0)

    def unit_heads(t):
        square = t * t
        first = jnp.sum(jnp.where(low, square, 0.0), axis=-1, keepdims=True)
        second = jnp.sum(jnp.where(low, 0.0, square), axis=-1, keepdims=True)
        inv = [lax.rsqrt(total * (1.0 / 64.0) + eps) for total in (first, second)]
        return (t * jnp.where(low, inv[0], inv[1])).astype(bf16).astype(f32)

    for group in range(0, width, cols):
        rows = normed[...]
        query, key, value = (nn(rows, w_ref[:, at + group : at + group + cols]) for at in (0, width, 2 * width))
        query = query.astype(bf16).astype(f32)
        key = key.astype(bf16).astype(f32)
        for tile in range(0, cols, 128):
            part = slice(tile, tile + 128)
            head = (group + tile) // 64
            even = slice(head * 128, head * 128 + 128)
            odd = slice(head * 128 + 128, head * 128 + 256)
            scale = jnp.where(low, temp_ref[head], temp_ref[head + 1]) * (math.log2(math.e) / 64.0)
            q = unit_heads(query[:, part]) * scale
            q_high = q.astype(bf16).astype(f32)
            moved = pltpu.roll(q - q_high, 64, 1)
            q_ref[:, even] = jnp.where(low, q_high, moved).astype(bf16)
            q_ref[:, odd] = jnp.where(low, moved, q_high).astype(bf16)
            k = unit_heads(key[:, part])
            moved = pltpu.roll(k, 64, 1)
            k_ref[:, even] = jnp.where(low, k, moved).astype(bf16)
            k_ref[:, odd] = jnp.where(low, moved, k).astype(bf16)
            shown = jnp.where(live, value[:, part], 0.0)
            v_ref[:, even] = jnp.where(low, shown, one).astype(bf16)
            v_ref[:, odd] = jnp.where(low, one, shown).astype(bf16)


def project_qkv(side, lengths, temps, tokens, gain, weight):
    count, width = tokens.shape
    out = jax.ShapeDtypeStruct((count, 2 * width), bf16)
    return pl.pallas_call(
        functools.partial(qkv_kernel, side),
        out_shape=(out, out, out),
        in_specs=[smem, smem] + [vmem] * 3,
        out_specs=[vmem] * 3,
        scratch_shapes=[pltpu.VMEM((count, width), bf16)],
        compiler_params=params(8),
        cost_estimate=brief,
        name="project_qkv",
    )(lengths, temps, gain, tokens, weight)


def weighted(q, keys, values, lanes):
    total = None
    for k_ref, v_ref in zip(keys, values):
        part = nn(jnp.exp2(nt(q, k_ref[:, lanes])).astype(bf16), v_ref[:, lanes])
        total = part if total is None else total + part
    return total


def finish(sums, out_ref, start, pair):
    count = sums[0].shape[0]
    low = lax.broadcasted_iota(jnp.int32, (count, 128), 1) < 64
    top = jnp.where(low, sums[0], sums[1])
    bottom = pltpu.roll(jnp.where(low, sums[1], sums[0]), 64, 1)
    out_ref[start : start + count, pl.ds(pl.multiple_of(pair * 128, 128), 128)] = (top / bottom).astype(bf16)


def pairs_of_heads(temp_ref, width, plain, other=None):
    def step(pair, _):
        lanes = [pl.ds(pl.multiple_of(pair * 256 + head * 128, 128), 128) for head in range(2)]
        safe = jnp.maximum(temp_ref[2 * pair], temp_ref[2 * pair + 1]) <= safe_temp
        pl.when(safe)(functools.partial(plain, pair, lanes))
        if other is not None:
            pl.when(jnp.logical_not(safe))(functools.partial(other, pair, lanes))
        return 0

    lax.fori_loop(0, width // 256, step, 0)


def first_stage(temp_ref, q0, k0, v0, a0):
    def plain(pair, heads):
        for lanes in heads:
            a0[:, lanes] = weighted(q0[:, lanes], [k0], [v0], lanes)

    pairs_of_heads(temp_ref, q0.shape[1], plain)


def last_stage(lengths_ref, temp_ref, q0, k0, v0, q1, k1, v1, a0, out_ref):
    count = q0.shape[0]
    keys, values = [k0, k1], [v0, v1]
    valid = valid_rows(lengths_ref, count)

    def plain(pair, heads):
        finish([a0[:, lanes] + weighted(q0[:, lanes], [k1], [v1], lanes) for lanes in heads], out_ref, 0, pair)
        finish([weighted(q1[:, lanes], keys, values, lanes) for lanes in heads], out_ref, count, pair)

    def other(pair, heads):
        for q_ref, start in zip((q0, q1), (0, count)):
            for first in range(0, count, 256):
                sums = []
                for lanes in heads:
                    scores = []
                    for at, k_ref in enumerate(keys):
                        score = nt(q_ref[first : first + 256, lanes], k_ref[:, lanes])
                        spot = lax.broadcasted_iota(jnp.int32, score.shape, 1)
                        scores.append(jnp.where(spot < valid[at], score, -1e30))
                    tops = [jnp.max(score, axis=-1, keepdims=True) for score in scores]
                    top = functools.reduce(jnp.maximum, tops)
                    total = 0.0
                    for score, v_ref in zip(scores, values):
                        total = total + nn(jnp.exp2(score - top).astype(bf16), v_ref[:, lanes])
                    sums.append(total)
                finish(sums, out_ref, start + first, pair)

    pairs_of_heads(temp_ref, q0.shape[1], plain, other)


def stage(kernel, scalars, arrays, outs, name):
    return pl.pallas_call(
        kernel,
        out_shape=outs,
        in_specs=[smem] * len(scalars) + [vmem] * len(arrays),
        out_specs=jax.tree.map(lambda out: vmem, outs),
        compiler_params=params(8),
        cost_estimate=brief,
        name=name,
    )(*scalars, *arrays)


def push_rows(scale, shown, after, wkv_ref, r_ref, head, key_ref, push_ref, rows):
    size = key_ref.shape[1]
    width = wkv_ref.shape[1] // 2
    exact, pieces = r_ref[...], []
    for _ in range(3):
        pieces.append(exact.astype(bf16).astype(f32))
        exact = exact - pieces[-1]
    heads = exact.shape[0]
    parts = nt(after, jnp.concatenate(pieces, axis=0).astype(bf16))
    high = sum(parts[:, at * heads + head : at * heads + head + 1] for at in range(3)) + 1.0
    soft = jnp.maximum(high, 0.0) + jnp.log1p(jnp.exp(-jnp.abs(high)))
    spot = lax.broadcasted_iota(jnp.int32, high.shape, 0)
    rate = jnp.where(spot < shown, soft * scale, 0.0)
    key = nn(after, wkv_ref[:, head * size : head * size + size])
    key_ref[rows, :] = (key * lax.rsqrt(jnp.mean(key * key, axis=-1, keepdims=True) + eps)).astype(bf16)
    value = nn(after, wkv_ref[:, width + head * size : width + head * size + size])
    push_ref[rows, :] = (-rate * value).astype(bf16)


def out_kernel(scale, lengths_ref, attn_ref, t0, t1, wo_ref, wkv_ref, r_ref, out_ref, after_ref, key_ref, push_ref):
    count = t0.shape[0]
    valid = valid_rows(lengths_ref, count)
    for side, tok_ref in enumerate((t0, t1)):
        rows = slice(side * count, side * count + count)
        after = (tok_ref[...].astype(f32) + nn(attn_ref[rows, :], wo_ref[...])).astype(bf16)
        after_ref[rows, :] = after
        if side == 0:
            out_ref[...] = after
        push_rows(scale, valid[side], after, wkv_ref, r_ref, 0, key_ref, push_ref, rows)


def again_kernel(scale, head, lengths_ref, after_ref, wkv_ref, r_ref, key_ref, push_ref):
    half = after_ref.shape[0] // 2
    valid = valid_rows(lengths_ref, half)
    for side in range(2):
        rows = slice(side * half, side * half + half)
        push_rows(scale, valid[side], after_ref[rows, :], wkv_ref, r_ref, head, key_ref, push_ref, rows)


def first_pushes(scale, lengths, attn, t0, t1, wo, wkv, rate):
    count, width = t0.shape
    both = jax.ShapeDtypeStruct((2 * count, width // rate.shape[0]), bf16)
    return pl.pallas_call(
        functools.partial(out_kernel, scale),
        out_shape=(
            jax.ShapeDtypeStruct((count, width), bf16),
            jax.ShapeDtypeStruct((2 * count, width), bf16),
            both,
            both,
        ),
        in_specs=[smem] + [vmem] * 6,
        out_specs=[vmem] * 4,
        compiler_params=params(12),
        cost_estimate=brief,
        name="first_pushes",
    )(lengths, attn, t0, t1, wo, wkv, rate)


def next_pushes(scale, lengths, after, wkv, rate, head):
    rows, width = after.shape
    both = jax.ShapeDtypeStruct((rows, width // rate.shape[0]), bf16)
    return pl.pallas_call(
        functools.partial(again_kernel, scale, head),
        out_shape=(both, both),
        in_specs=[smem] + [vmem] * 3,
        out_specs=[vmem] * 2,
        compiler_params=params(12),
        cost_estimate=brief,
        name="next_pushes",
    )(lengths, after, wkv, rate)


def grad_kernel(head, half, w_ref, key_ref, push_ref, out_ref):
    count, size = out_ref.shape[0], key_ref.shape[1]
    key, push = key_ref[...], push_ref[...]
    w = w_ref[head, half * count : half * count + count, :]
    act_a = nt(w[:, :size], key)
    act_b = nt(w[:, size : 2 * size], key)
    back = nt(w[:, 2 * size :], push)
    sigma = 1.0 / (1.0 + jnp.exp(-act_a))
    silu = act_a * sigma
    hidden = (silu * act_b).astype(bf16)
    grad_a = (back * act_b * sigma * (1.0 + act_a * (1.0 - sigma))).astype(bf16)
    grad_b = (back * silu).astype(bf16)
    out_ref[:, :size] = nn(grad_a, key).astype(out_ref.dtype)
    out_ref[:, size : 2 * size] = nn(grad_b, key).astype(out_ref.dtype)
    out_ref[:, 2 * size :] = nn(hidden, push).astype(out_ref.dtype)


def gradient(weights, keys, pushes, head, half, kind):
    _, rows, cols = weights.shape
    return pl.pallas_call(
        functools.partial(grad_kernel, head, half),
        out_shape=jax.ShapeDtypeStruct((rows // 2, cols), kind),
        in_specs=[vmem] * 3,
        out_specs=vmem,
        compiler_params=params(12),
        cost_estimate=brief,
        name="gradient",
    )(weights, keys, pushes)


def add_kernel(kept_ref, got_ref, sent_ref, keep_ref):
    half = keep_ref.shape[0]
    sent_ref[...] = (kept_ref[half:, :] + got_ref[half:, :].astype(f32)).astype(bf16)
    keep_ref[...] = kept_ref[:half, :] + got_ref[:half, :].astype(f32)


def add_step(kept, got):
    half = (kept.shape[0] // 2, kept.shape[1])
    return pl.pallas_call(
        add_kernel,
        out_shape=(jax.ShapeDtypeStruct(half, bf16), jax.ShapeDtypeStruct(half, f32)),
        in_specs=[vmem] * 2,
        out_specs=[vmem] * 2,
        compiler_params=params(4),
        cost_estimate=brief,
        name="add_step",
    )(kept, got)


def spread_kernel(k0_ref, g0_ref, k1_ref, g1_ref, own_ref, *sent_refs):
    rows, cols = own_ref.shape[0], k0_ref.shape[1]
    for head, (kept_ref, got_ref) in enumerate(((k0_ref, g0_ref), (k1_ref, g1_ref))):
        total = kept_ref[...] + got_ref[...].astype(f32)
        part = slice(head * cols, head * cols + cols)
        own_ref[:, part] = total[:rows]
        for at, sent_ref in enumerate(sent_refs):
            sent_ref[:, part] = total[(at + 1) * rows : (at + 2) * rows].astype(bf16)


def spread(k0, g0, k1, g1):
    shape = (k0.shape[0] // 4, 2 * k0.shape[1])
    kinds = (f32, bf16, bf16, bf16)
    return pl.pallas_call(
        spread_kernel,
        out_shape=tuple(jax.ShapeDtypeStruct(shape, kind) for kind in kinds),
        in_specs=[vmem] * 4,
        out_specs=[vmem] * 4,
        compiler_params=params(4),
        cost_estimate=brief,
        name="spread",
    )(k0, g0, k1, g1)


def rescale_kernel(start_ref, own_ref, a_ref, b_ref, c_ref, out_ref, sent_ref):
    heads, cols = start_ref.shape[0], start_ref.shape[3]
    size = cols // 3
    for head in range(heads):
        for block in range(3):
            part = slice(head * cols + block * size, head * cols + block * size + size)
            grad = own_ref[:, part]
            for got_ref in (a_ref, b_ref, c_ref):
                grad = grad + got_ref[:, part].astype(f32)
            start = start_ref[head, 0, :, block * size : block * size + size].astype(f32)
            update = start - grad
            before = jnp.sqrt(jnp.mean(start * start, axis=-1, keepdims=True) + eps)
            after = lax.rsqrt(jnp.mean(update * update, axis=-1, keepdims=True) + eps)
            fresh = (update * before * after).astype(bf16)
            out_ref[:, part] = fresh
            sent_ref[:, part] = fresh


def rescale(start, own, got):
    out = jax.ShapeDtypeStruct(own.shape, bf16)
    return pl.pallas_call(
        rescale_kernel,
        out_shape=(out, out),
        in_specs=[vmem] * 5,
        out_specs=[vmem] * 2,
        compiler_params=params(4),
        cost_estimate=brief,
        name="rescale",
    )(start, own, *got)


def collect_kernel(a_ref, b_ref, c_ref, d_ref, h0_ref, h1_ref):
    cols = h0_ref.shape[2]
    for at, got_ref in enumerate((a_ref, b_ref, c_ref, d_ref)):
        h0_ref[at] = got_ref[:, :cols]
        h1_ref[at] = got_ref[:, cols:]


def collect(blocks):
    rows, cols = blocks[0].shape
    out = jax.ShapeDtypeStruct((len(blocks), rows, cols // 2), bf16)
    held = pl.pallas_call(
        collect_kernel,
        out_shape=(out, out),
        in_specs=[vmem] * 4,
        out_specs=[vmem] * 2,
        compiler_params=params(4),
        cost_estimate=brief,
        name="collect",
    )(*blocks)
    return [part.reshape(len(blocks) * rows, cols // 2) for part in held]


def query_kernel(t_ref, s_ref, w_ref, q0_ref, q1_ref):
    count = t_ref.shape[0]
    size = q0_ref.shape[1]
    for side, rows_ref in enumerate((t_ref, s_ref)):
        tq = nn(rows_ref[...], w_ref[...])
        for head, q_ref in enumerate((q0_ref, q1_ref)):
            q = tq[:, head * size : head * size + size]
            unit = q * lax.rsqrt(jnp.mean(q * q, axis=-1, keepdims=True) + eps)
            q_ref[side * count : side * count + count, :] = unit.astype(bf16)


def target_queries(target, shared, weight):
    count, width = target.shape
    out = jax.ShapeDtypeStruct((2 * count, width // 2), bf16)
    return pl.pallas_call(
        query_kernel,
        out_shape=(out, out),
        in_specs=[vmem] * 3,
        out_specs=[vmem] * 2,
        compiler_params=params(8),
        cost_estimate=brief,
        name="target_queries",
    )(target, shared, weight)


def apply_rows(q, w_ref):
    size = q.shape[1]
    act_a = nt(q, w_ref[:, :size])
    act_b = nt(q, w_ref[:, size : 2 * size])
    hidden = (act_a / (1.0 + jnp.exp(-act_a)) * act_b).astype(bf16)
    return nn(hidden, w_ref[:, 2 * size :])


def first_kernel(q_ref, w_ref, out_ref):
    out_ref[...] = apply_rows(q_ref[...], w_ref)


def apply_first(queries, weights):
    return pl.pallas_call(
        first_kernel,
        out_shape=jax.ShapeDtypeStruct((queries.shape[0], weights.shape[1] // 3), f32),
        in_specs=[vmem] * 2,
        out_specs=vmem,
        compiler_params=params(8),
        cost_estimate=brief,
        name="apply_first",
    )(queries, weights)


def last_kernel(q_ref, w_ref, sum_ref, mine_ref, theirs_ref):
    count = mine_ref.shape[0]
    total = sum_ref[...] + apply_rows(q_ref[...], w_ref)
    mine_ref[...] = total[:count]
    theirs_ref[...] = total[count:].astype(bf16)


def apply_last(queries, weights, total):
    half = (total.shape[0] // 2, total.shape[1])
    return pl.pallas_call(
        last_kernel,
        out_shape=(jax.ShapeDtypeStruct(half, f32), jax.ShapeDtypeStruct(half, bf16)),
        in_specs=[vmem] * 3,
        out_specs=[vmem] * 2,
        compiler_params=params(8),
        cost_estimate=brief,
        name="apply_last",
    )(queries, weights, total)


def merge_kernel(target_ref, w_ref, mine_ref, theirs_ref, out_ref):
    size = mine_ref.shape[1]
    fout = mine_ref[...] + theirs_ref[...].astype(f32)
    unit = (fout * lax.rsqrt(jnp.mean(fout * fout, axis=-1, keepdims=True) + eps)).astype(bf16)
    out_ref[...] = target_ref[...].astype(f32) + nn(unit, w_ref[:size, :])


def merge_first(target, weight, mine, theirs):
    return pl.pallas_call(
        merge_kernel,
        out_shape=jax.ShapeDtypeStruct(target.shape, f32),
        in_specs=[vmem] * 4,
        out_specs=vmem,
        compiler_params=params(8),
        cost_estimate=brief,
        name="merge_first",
    )(target, weight, mine, theirs)


def merge_last_kernel(used_ref, sum_ref, w_ref, mine_ref, theirs_ref, out_ref):
    size = mine_ref.shape[1]
    fout = mine_ref[...] + theirs_ref[...].astype(f32)
    unit = (fout * lax.rsqrt(jnp.mean(fout * fout, axis=-1, keepdims=True) + eps)).astype(bf16)
    total = sum_ref[...] + nn(unit, w_ref[size:, :])
    live = lax.broadcasted_iota(jnp.int32, total.shape, 0) < used_ref[0]
    out_ref[...] = jnp.where(live, total, 0.0).astype(bf16)


def merge_last(used, total, weight, mine, theirs):
    return pl.pallas_call(
        merge_last_kernel,
        out_shape=jax.ShapeDtypeStruct(total.shape, bf16),
        in_specs=[smem] + [vmem] * 4,
        out_specs=vmem,
        compiler_params=params(8),
        cost_estimate=brief,
        name="merge_last",
    )(used, total, weight, mine, theirs)


def body(
    tokens,
    attn_gain,
    qkv_weight,
    head_temp,
    out_weight,
    kv_weight,
    rate_weight,
    fast_weights,
    target,
    query_weight,
    merge_weight,
    image_lengths,
    target_counts,
):
    tok_rows, width = tokens.shape
    devices = lax.axis_size("tok")
    fast_hidden, fast_cols = fast_weights.shape
    fast_heads = rate_weight.shape[1]
    rows = fast_hidden // devices
    moves = []
    for masks in halve_masks:
        span = [(0, 0)]
        for first, second in ring_masks[:2] + masks[::-1]:
            span = span + [(first ^ at, second ^ to) for at, to in span]
        moves.append(span)
    gain = attn_gain[None, :]
    rate = rate_weight.T
    sums = jax.ShapeDtypeStruct((tok_rows, 2 * width), f32)

    arrived = swap(tokens, image_mask)
    q0, k0, v0 = project_qkv(0, image_lengths, head_temp, tokens, gain, qkv_weight)
    a0 = stage(first_stage, [head_temp], [q0, k0, v0], sums, "attend_first")
    fast_blocks = fast_weights.reshape(devices, rows, fast_cols)
    fast_blocks, a0 = lax.optimization_barrier((fast_blocks, a0))
    start = gather_rows(moves, fast_blocks)
    arrived, a0, start = lax.optimization_barrier((arrived, a0, start))
    weights = start.reshape(fast_heads, len(moves[0]) * rows, fast_cols // fast_heads)

    q1, k1, v1 = project_qkv(1, image_lengths, head_temp, arrived, gain, qkv_weight)
    attn = stage(
        last_stage,
        [image_lengths, head_temp],
        [q0, k0, v0, q1, k1, v1, a0],
        jax.ShapeDtypeStruct((2 * tok_rows, width), bf16),
        "attend_last",
    )
    factor = rate_base / (tok_rows * devices)
    tokens_out, after, keys, pushes = first_pushes(
        factor, image_lengths, attn, tokens, arrived, out_weight, kv_weight, rate
    )
    made = [(keys, pushes)]
    sent = [gradient(weights, keys, pushes, 0, 1, bf16)]
    after, sent[0] = lax.optimization_barrier((after, sent[0]))
    got = [swap(sent[0], halve_masks[0][0])]
    made.append(next_pushes(factor, image_lengths, after, kv_weight, rate, 1))
    sent.append(gradient(weights, *made[1], 1, 1, bf16))
    made[1], sent[1], given = lax.optimization_barrier((made[1], sent[1], target))
    got.append(swap(sent[1], halve_masks[1][0]))
    shared = swap(given, share_mask)
    got[0], made[0], made[1] = lax.optimization_barrier((got[0], made[0], made[1]))
    kept = []
    for head in range(fast_heads):
        away, keep = add_step(gradient(weights, *made[head], head, 0, f32), got[head])
        if head == 0:
            away, made[1] = lax.optimization_barrier((away, made[1]))
        kept.append(keep)
        got[head] = swap(away, halve_masks[head][1])
    queries = target_queries(target, shared, query_weight)
    kept[1], queries = lax.optimization_barrier((kept[1], queries))
    own, *pieces = spread(kept[0], got[0], kept[1], got[1])
    fresh, spare = rescale(start, own, [swap(piece, masks) for piece, masks in zip(pieces, ring_masks)])

    collected = collect([spare] + [swap(spare, mask) for mask in ring_masks])
    mine, theirs = [], []
    for head, held in enumerate(collected):
        held = jnp.concatenate([held, swap(held, double_masks[head][0])], axis=0)
        last = swap(held, double_masks[head][1])
        total = apply_first(queries[head], held)
        kept_sum, sent_sum = apply_last(queries[head], last, total)
        mine.append(kept_sum)
        theirs.append(swap(sent_sum, share_mask))
    target_sum = merge_first(target, merge_weight, mine[0], theirs[0])
    target_out = merge_last(target_counts, target_sum, merge_weight, mine[1], theirs[1])
    return (tokens_out, fresh, target_out)


def solution(mesh):
    placed = (
        P(("rep", "tok"), None),
        P(),
        P(),
        P(),
        P(),
        P(),
        P(),
        P(),
        P(("rep", "tok"), None),
        P(),
        P(),
        P("rep"),
        P(("rep", "tok")),
    )
    return jax.shard_map(
        body,
        mesh=mesh,
        in_specs=placed,
        out_specs=(P(("rep", "tok"), None), P(("rep", "tok"), None), P(("rep", "tok"), None)),
        check_vma=False,
    )
```

```python
import functools
import math

import jax
import jax.numpy as jnp
from jax import lax
from jax.experimental import pallas as pl
from jax.experimental.pallas import tpu as pltpu
from jax.sharding import PartitionSpec as P

eps = 1e-06
rate_base = 4.0
safe_temp = 60.0
bf16 = jnp.bfloat16
f32 = jnp.float32

image_mask = (1, 1)
halve_masks = (((3, 8), (4, 24)), ((4, 24), (3, 8)))
ring_masks = ((24, 3), (8, 4), (16, 7))
double_masks = halve_masks
share_mask = (1, 1)


def swap(value, masks):
    reps, places = lax.axis_size("rep"), lax.axis_size("tok")
    pairs = [
        (place * reps + rep, (place ^ masks[rep % 2]) * reps + rep) for place in range(places) for rep in range(reps)
    ]
    return lax.ppermute(value, ("tok", "rep"), pairs)


def params(mib):
    return pltpu.CompilerParams(vmem_limit_bytes=mib * 2**20)


brief = pl.CostEstimate(flops=1, transcendentals=0, bytes_accessed=1)


def nn(a, b):
    return lax.dot_general(a, b, (((1,), (0,)), ((), ())), preferred_element_type=f32)


def nt(a, b):
    return lax.dot_general(a, b, (((1,), (1,)), ((), ())), preferred_element_type=f32)


def whole(shape):
    return pl.BlockSpec(shape, lambda *_: (0,) * len(shape))


smem = pl.BlockSpec(memory_space=pltpu.SMEM)
vmem = pl.BlockSpec(memory_space=pltpu.VMEM)


def valid_rows(lengths_ref, count):
    place = lax.axis_index("tok")
    length = lengths_ref[lax.shift_right_logical(place, 1)]
    parity = lax.bitwise_and(place, 1)
    return length - parity * count, length - (1 - parity) * count


def gather_kernel(moves, rows_ref, out_ref):
    place = lax.axis_index("tok")
    core = lax.bitwise_and(lax.axis_index("rep"), 1)
    cols = out_ref.shape[-1]
    for head, span in enumerate(moves):
        for block, (mask, other) in enumerate(span):
            owner = lax.bitwise_xor(place, mask + core * (other - mask))
            out_ref[head, block] = rows_ref[owner, :, head * cols : head * cols + cols]


def gather_rows(moves, rows):
    _, height, width = rows.shape
    heads = len(moves)
    return pl.pallas_call(
        functools.partial(gather_kernel, moves),
        out_shape=jax.ShapeDtypeStruct((heads, len(moves[0]), height, width // heads), rows.dtype),
        in_specs=[vmem],
        out_specs=vmem,
        compiler_params=params(4),
        cost_estimate=brief,
        name="gather_rows",
    )(rows)


def qkv_kernel(side, lengths_ref, temp_ref, gain_ref, tok_ref, w_ref, q_ref, k_ref, v_ref, normed):
    count, width = normed.shape
    cols = 256
    x = tok_ref[...].astype(f32)
    unit = x * lax.rsqrt(jnp.mean(x * x, axis=-1, keepdims=True) + eps)
    normed[...] = (unit * gain_ref[...].astype(f32)).astype(bf16)
    shown_rows = valid_rows(lengths_ref, count)[side]
    low = lax.broadcasted_iota(jnp.int32, (count, 128), 1) < 64
    live = lax.broadcasted_iota(jnp.int32, (count, 128), 0) < shown_rows
    one = jnp.where(live, 1.0, 0.0)

    def unit_heads(t):
        square = t * t
        first = jnp.sum(jnp.where(low, square, 0.0), axis=-1, keepdims=True)
        second = jnp.sum(jnp.where(low, 0.0, square), axis=-1, keepdims=True)
        inv = [lax.rsqrt(total * (1.0 / 64.0) + eps) for total in (first, second)]
        return (t * jnp.where(low, inv[0], inv[1])).astype(bf16).astype(f32)

    for group in range(0, width, cols):
        rows = normed[...]
        query, key, value = (nn(rows, w_ref[:, at + group : at + group + cols]) for at in (0, width, 2 * width))
        query = query.astype(bf16).astype(f32)
        key = key.astype(bf16).astype(f32)
        for tile in range(0, cols, 128):
            part = slice(tile, tile + 128)
            head = (group + tile) // 64
            even = slice(head * 128, head * 128 + 128)
            odd = slice(head * 128 + 128, head * 128 + 256)
            scale = jnp.where(low, temp_ref[head], temp_ref[head + 1]) * (math.log2(math.e) / 64.0)
            q = unit_heads(query[:, part]) * scale
            q_high = q.astype(bf16).astype(f32)
            moved = pltpu.roll(q - q_high, 64, 1)
            q_ref[:, even] = jnp.where(low, q_high, moved).astype(bf16)
            q_ref[:, odd] = jnp.where(low, moved, q_high).astype(bf16)
            k = unit_heads(key[:, part])
            moved = pltpu.roll(k, 64, 1)
            k_ref[:, even] = jnp.where(low, k, moved).astype(bf16)
            k_ref[:, odd] = jnp.where(low, moved, k).astype(bf16)
            shown = jnp.where(live, value[:, part], 0.0)
            v_ref[:, even] = jnp.where(low, shown, one).astype(bf16)
            v_ref[:, odd] = jnp.where(low, one, shown).astype(bf16)


def project_qkv(side, lengths, temps, tokens, gain, weight):
    count, width = tokens.shape
    out = jax.ShapeDtypeStruct((count, 2 * width), bf16)
    return pl.pallas_call(
        functools.partial(qkv_kernel, side),
        out_shape=(out, out, out),
        in_specs=[smem, smem] + [vmem] * 3,
        out_specs=[vmem] * 3,
        scratch_shapes=[pltpu.VMEM((count, width), bf16)],
        compiler_params=params(8),
        cost_estimate=brief,
        name="project_qkv",
    )(lengths, temps, gain, tokens, weight)


def weighted(q, keys, values, lanes):
    total = None
    for k_ref, v_ref in zip(keys, values):
        part = nn(jnp.exp2(nt(q, k_ref[:, lanes])).astype(bf16), v_ref[:, lanes])
        total = part if total is None else total + part
    return total


def finish(sums, out_ref, start, pair):
    count = sums[0].shape[0]
    low = lax.broadcasted_iota(jnp.int32, (count, 128), 1) < 64
    top = jnp.where(low, sums[0], sums[1])
    bottom = pltpu.roll(jnp.where(low, sums[1], sums[0]), 64, 1)
    out_ref[pl.ds(start, count), pl.ds(pl.multiple_of(pair * 128, 128), 128)] = (top / bottom).astype(bf16)


def pairs_of_heads(temp_ref, width, plain, other=None):
    def lanes_of(pair):
        return [pl.ds(pl.multiple_of(pair * 256 + head * 128, 128), 128) for head in range(2)]

    def is_safe(pair):
        return jnp.maximum(temp_ref[2 * pair], temp_ref[2 * pair + 1]) <= safe_temp

    def two_pairs(step, _):
        first, second = 2 * step, 2 * step + 1
        both = jnp.logical_and(is_safe(first), is_safe(second))

        @pl.when(both)
        def _():
            plain(first, lanes_of(first))
            plain(second, lanes_of(second))

        @pl.when(jnp.logical_not(both))
        def _():
            def one_pair(pair, _):
                if other is not None:
                    other(pair, lanes_of(pair))
                return 0

            lax.fori_loop(first, first + 2, one_pair, 0)

        return 0

    lax.fori_loop(0, width // 512, two_pairs, 0)


def first_stage(temp_ref, q0, k0, v0, a0):
    def plain(pair, heads):
        for lanes in heads:
            a0[:, lanes] = weighted(q0[:, lanes], [k0], [v0], lanes)

    pairs_of_heads(temp_ref, q0.shape[1], plain)


def last_stage(lengths_ref, temp_ref, q0, k0, v0, q1, k1, v1, a0, out_ref):
    count = q0.shape[0]
    keys, values = [k0, k1], [v0, v1]
    valid = valid_rows(lengths_ref, count)

    def plain(pair, heads):
        finish([a0[:, lanes] + weighted(q0[:, lanes], [k1], [v1], lanes) for lanes in heads], out_ref, 0, pair)
        finish([weighted(q1[:, lanes], keys, values, lanes) for lanes in heads], out_ref, count, pair)

    def other(pair, heads):
        block = 128
        for q_ref, start in zip((q0, q1), (0, count)):

            def some_rows(step, _):
                first = pl.multiple_of(step * block, block)
                sums = []
                for lanes in heads:
                    scores = []
                    for at, k_ref in enumerate(keys):
                        score = nt(q_ref[pl.ds(first, block), lanes], k_ref[:, lanes])
                        spot = lax.broadcasted_iota(jnp.int32, score.shape, 1)
                        scores.append(jnp.where(spot < valid[at], score, -1e30))
                    tops = [jnp.max(score, axis=-1, keepdims=True) for score in scores]
                    top = functools.reduce(jnp.maximum, tops)
                    total = 0.0
                    for score, v_ref in zip(scores, values):
                        total = total + nn(jnp.exp2(score - top).astype(bf16), v_ref[:, lanes])
                    sums.append(total)
                finish(sums, out_ref, pl.multiple_of(start + first, block), pair)
                return 0

            lax.fori_loop(0, count // block, some_rows, 0)

    pairs_of_heads(temp_ref, q0.shape[1], plain, other)


def stage(kernel, scalars, arrays, outs, name):
    return pl.pallas_call(
        kernel,
        out_shape=outs,
        in_specs=[smem] * len(scalars) + [vmem] * len(arrays),
        out_specs=jax.tree.map(lambda out: vmem, outs),
        compiler_params=params(8),
        cost_estimate=brief,
        name=name,
    )(*scalars, *arrays)


def push_rows(scale, shown, after, wkv_ref, r_ref, head, key_ref, push_ref, rows):
    size = key_ref.shape[1]
    width = wkv_ref.shape[1] // 2
    exact, pieces = r_ref[...], []
    for _ in range(3):
        pieces.append(exact.astype(bf16).astype(f32))
        exact = exact - pieces[-1]
    heads = exact.shape[0]
    parts = nt(after, jnp.concatenate(pieces, axis=0).astype(bf16))
    high = sum(parts[:, at * heads + head : at * heads + head + 1] for at in range(3)) + 1.0
    soft = jnp.maximum(high, 0.0) + jnp.log1p(jnp.exp(-jnp.abs(high)))
    spot = lax.broadcasted_iota(jnp.int32, high.shape, 0)
    rate = jnp.where(spot < shown, soft * scale, 0.0)
    key = nn(after, wkv_ref[:, head * size : head * size + size])
    key_ref[rows, :] = (key * lax.rsqrt(jnp.mean(key * key, axis=-1, keepdims=True) + eps)).astype(bf16)
    value = nn(after, wkv_ref[:, width + head * size : width + head * size + size])
    push_ref[rows, :] = (-rate * value).astype(bf16)


def out_kernel(scale, lengths_ref, attn_ref, t0, t1, wo_ref, wkv_ref, r_ref, out_ref, after_ref, key_ref, push_ref):
    count = t0.shape[0]
    valid = valid_rows(lengths_ref, count)
    for side, tok_ref in enumerate((t0, t1)):
        rows = slice(side * count, side * count + count)
        after = (tok_ref[...].astype(f32) + nn(attn_ref[rows, :], wo_ref[...])).astype(bf16)
        after_ref[rows, :] = after
        if side == 0:
            out_ref[...] = after
        push_rows(scale, valid[side], after, wkv_ref, r_ref, 0, key_ref, push_ref, rows)


def again_kernel(scale, head, lengths_ref, after_ref, wkv_ref, r_ref, key_ref, push_ref):
    half = after_ref.shape[0] // 2
    valid = valid_rows(lengths_ref, half)
    for side in range(2):
        rows = slice(side * half, side * half + half)
        push_rows(scale, valid[side], after_ref[rows, :], wkv_ref, r_ref, head, key_ref, push_ref, rows)


def first_pushes(scale, lengths, attn, t0, t1, wo, wkv, rate):
    count, width = t0.shape
    both = jax.ShapeDtypeStruct((2 * count, width // rate.shape[0]), bf16)
    return pl.pallas_call(
        functools.partial(out_kernel, scale),
        out_shape=(
            jax.ShapeDtypeStruct((count, width), bf16),
            jax.ShapeDtypeStruct((2 * count, width), bf16),
            both,
            both,
        ),
        in_specs=[smem] + [vmem] * 6,
        out_specs=[vmem] * 4,
        compiler_params=params(12),
        cost_estimate=brief,
        name="first_pushes",
    )(lengths, attn, t0, t1, wo, wkv, rate)


def next_pushes(scale, lengths, after, wkv, rate, head):
    rows, width = after.shape
    both = jax.ShapeDtypeStruct((rows, width // rate.shape[0]), bf16)
    return pl.pallas_call(
        functools.partial(again_kernel, scale, head),
        out_shape=(both, both),
        in_specs=[smem] + [vmem] * 3,
        out_specs=[vmem] * 2,
        compiler_params=params(12),
        cost_estimate=brief,
        name="next_pushes",
    )(lengths, after, wkv, rate)


def grad_kernel(head, half, w_ref, key_ref, push_ref, out_ref):
    count, size = out_ref.shape[0], key_ref.shape[1]
    key, push = key_ref[...], push_ref[...]
    w = w_ref[head, half * count : half * count + count, :]
    act_a = nt(w[:, :size], key)
    act_b = nt(w[:, size : 2 * size], key)
    back = nt(w[:, 2 * size :], push)
    sigma = 1.0 / (1.0 + jnp.exp(-act_a))
    silu = act_a * sigma
    hidden = (silu * act_b).astype(bf16)
    grad_a = (back * act_b * sigma * (1.0 + act_a * (1.0 - sigma))).astype(bf16)
    grad_b = (back * silu).astype(bf16)
    out_ref[:, :size] = nn(grad_a, key).astype(out_ref.dtype)
    out_ref[:, size : 2 * size] = nn(grad_b, key).astype(out_ref.dtype)
    out_ref[:, 2 * size :] = nn(hidden, push).astype(out_ref.dtype)


def gradient(weights, keys, pushes, head, half, kind):
    _, rows, cols = weights.shape
    return pl.pallas_call(
        functools.partial(grad_kernel, head, half),
        out_shape=jax.ShapeDtypeStruct((rows // 2, cols), kind),
        in_specs=[vmem] * 3,
        out_specs=vmem,
        compiler_params=params(12),
        cost_estimate=brief,
        name="gradient",
    )(weights, keys, pushes)


def add_kernel(kept_ref, got_ref, sent_ref, keep_ref):
    half = keep_ref.shape[0]
    sent_ref[...] = (kept_ref[half:, :] + got_ref[half:, :].astype(f32)).astype(bf16)
    keep_ref[...] = kept_ref[:half, :] + got_ref[:half, :].astype(f32)


def add_step(kept, got):
    half = (kept.shape[0] // 2, kept.shape[1])
    return pl.pallas_call(
        add_kernel,
        out_shape=(jax.ShapeDtypeStruct(half, bf16), jax.ShapeDtypeStruct(half, f32)),
        in_specs=[vmem] * 2,
        out_specs=[vmem] * 2,
        compiler_params=params(4),
        cost_estimate=brief,
        name="add_step",
    )(kept, got)


def spread_kernel(k0_ref, g0_ref, k1_ref, g1_ref, own_ref, *sent_refs):
    rows, cols = own_ref.shape[0], k0_ref.shape[1]
    for head, (kept_ref, got_ref) in enumerate(((k0_ref, g0_ref), (k1_ref, g1_ref))):
        total = kept_ref[...] + got_ref[...].astype(f32)
        part = slice(head * cols, head * cols + cols)
        own_ref[:, part] = total[:rows]
        for at, sent_ref in enumerate(sent_refs):
            sent_ref[:, part] = total[(at + 1) * rows : (at + 2) * rows].astype(bf16)


def spread(k0, g0, k1, g1):
    shape = (k0.shape[0] // 4, 2 * k0.shape[1])
    kinds = (f32, bf16, bf16, bf16)
    return pl.pallas_call(
        spread_kernel,
        out_shape=tuple(jax.ShapeDtypeStruct(shape, kind) for kind in kinds),
        in_specs=[vmem] * 4,
        out_specs=[vmem] * 4,
        compiler_params=params(4),
        cost_estimate=brief,
        name="spread",
    )(k0, g0, k1, g1)


def rescale_kernel(start_ref, own_ref, a_ref, b_ref, c_ref, out_ref, sent_ref):
    heads, cols = start_ref.shape[0], start_ref.shape[3]
    size = cols // 3
    for head in range(heads):
        for block in range(3):
            part = slice(head * cols + block * size, head * cols + block * size + size)
            grad = own_ref[:, part]
            for got_ref in (a_ref, b_ref, c_ref):
                grad = grad + got_ref[:, part].astype(f32)
            start = start_ref[head, 0, :, block * size : block * size + size].astype(f32)
            update = start - grad
            before = jnp.sqrt(jnp.mean(start * start, axis=-1, keepdims=True) + eps)
            after = lax.rsqrt(jnp.mean(update * update, axis=-1, keepdims=True) + eps)
            fresh = (update * before * after).astype(bf16)
            out_ref[:, part] = fresh
            sent_ref[:, part] = fresh


def rescale(start, own, got):
    out = jax.ShapeDtypeStruct(own.shape, bf16)
    return pl.pallas_call(
        rescale_kernel,
        out_shape=(out, out),
        in_specs=[vmem] * 5,
        out_specs=[vmem] * 2,
        compiler_params=params(4),
        cost_estimate=brief,
        name="rescale",
    )(start, own, *got)


def collect_kernel(a_ref, b_ref, c_ref, d_ref, h0_ref, h1_ref):
    cols = h0_ref.shape[2]
    for at, got_ref in enumerate((a_ref, b_ref, c_ref, d_ref)):
        h0_ref[at] = got_ref[:, :cols]
        h1_ref[at] = got_ref[:, cols:]


def collect(blocks):
    rows, cols = blocks[0].shape
    out = jax.ShapeDtypeStruct((len(blocks), rows, cols // 2), bf16)
    held = pl.pallas_call(
        collect_kernel,
        out_shape=(out, out),
        in_specs=[vmem] * 4,
        out_specs=[vmem] * 2,
        compiler_params=params(4),
        cost_estimate=brief,
        name="collect",
    )(*blocks)
    return [part.reshape(len(blocks) * rows, cols // 2) for part in held]


def query_kernel(t_ref, s_ref, w_ref, q0_ref, q1_ref):
    count = t_ref.shape[0]
    size = q0_ref.shape[1]
    for side, rows_ref in enumerate((t_ref, s_ref)):
        tq = nn(rows_ref[...], w_ref[...])
        for head, q_ref in enumerate((q0_ref, q1_ref)):
            q = tq[:, head * size : head * size + size]
            unit = q * lax.rsqrt(jnp.mean(q * q, axis=-1, keepdims=True) + eps)
            q_ref[side * count : side * count + count, :] = unit.astype(bf16)


def target_queries(target, shared, weight):
    count, width = target.shape
    out = jax.ShapeDtypeStruct((2 * count, width // 2), bf16)
    return pl.pallas_call(
        query_kernel,
        out_shape=(out, out),
        in_specs=[vmem] * 3,
        out_specs=[vmem] * 2,
        compiler_params=params(8),
        cost_estimate=brief,
        name="target_queries",
    )(target, shared, weight)


def apply_rows(q, w_ref):
    size = q.shape[1]
    act_a = nt(q, w_ref[:, :size])
    act_b = nt(q, w_ref[:, size : 2 * size])
    hidden = (act_a / (1.0 + jnp.exp(-act_a)) * act_b).astype(bf16)
    return nn(hidden, w_ref[:, 2 * size :])


def first_kernel(q_ref, w_ref, out_ref):
    out_ref[...] = apply_rows(q_ref[...], w_ref)


def apply_first(queries, weights):
    return pl.pallas_call(
        first_kernel,
        out_shape=jax.ShapeDtypeStruct((queries.shape[0], weights.shape[1] // 3), f32),
        in_specs=[vmem] * 2,
        out_specs=vmem,
        compiler_params=params(8),
        cost_estimate=brief,
        name="apply_first",
    )(queries, weights)


def last_kernel(q_ref, w_ref, sum_ref, mine_ref, theirs_ref):
    count = mine_ref.shape[0]
    total = sum_ref[...] + apply_rows(q_ref[...], w_ref)
    mine_ref[...] = total[:count]
    theirs_ref[...] = total[count:].astype(bf16)


def apply_last(queries, weights, total):
    half = (total.shape[0] // 2, total.shape[1])
    return pl.pallas_call(
        last_kernel,
        out_shape=(jax.ShapeDtypeStruct(half, f32), jax.ShapeDtypeStruct(half, bf16)),
        in_specs=[vmem] * 3,
        out_specs=[vmem] * 2,
        compiler_params=params(8),
        cost_estimate=brief,
        name="apply_last",
    )(queries, weights, total)


def merge_kernel(target_ref, w_ref, mine_ref, theirs_ref, out_ref):
    size = mine_ref.shape[1]
    fout = mine_ref[...] + theirs_ref[...].astype(f32)
    unit = (fout * lax.rsqrt(jnp.mean(fout * fout, axis=-1, keepdims=True) + eps)).astype(bf16)
    out_ref[...] = target_ref[...].astype(f32) + nn(unit, w_ref[:size, :])


def merge_first(target, weight, mine, theirs):
    return pl.pallas_call(
        merge_kernel,
        out_shape=jax.ShapeDtypeStruct(target.shape, f32),
        in_specs=[vmem] * 4,
        out_specs=vmem,
        compiler_params=params(8),
        cost_estimate=brief,
        name="merge_first",
    )(target, weight, mine, theirs)


def merge_last_kernel(used_ref, sum_ref, w_ref, mine_ref, theirs_ref, out_ref):
    size = mine_ref.shape[1]
    fout = mine_ref[...] + theirs_ref[...].astype(f32)
    unit = (fout * lax.rsqrt(jnp.mean(fout * fout, axis=-1, keepdims=True) + eps)).astype(bf16)
    total = sum_ref[...] + nn(unit, w_ref[size:, :])
    live = lax.broadcasted_iota(jnp.int32, total.shape, 0) < used_ref[0]
    out_ref[...] = jnp.where(live, total, 0.0).astype(bf16)


def merge_last(used, total, weight, mine, theirs):
    return pl.pallas_call(
        merge_last_kernel,
        out_shape=jax.ShapeDtypeStruct(total.shape, bf16),
        in_specs=[smem] + [vmem] * 4,
        out_specs=vmem,
        compiler_params=params(8),
        cost_estimate=brief,
        name="merge_last",
    )(used, total, weight, mine, theirs)


def body(
    tokens,
    attn_gain,
    qkv_weight,
    head_temp,
    out_weight,
    kv_weight,
    rate_weight,
    fast_weights,
    target,
    query_weight,
    merge_weight,
    image_lengths,
    target_counts,
):
    tok_rows, width = tokens.shape
    devices = lax.axis_size("tok")
    fast_hidden, fast_cols = fast_weights.shape
    fast_heads = rate_weight.shape[1]
    rows = fast_hidden // devices
    moves = []
    for masks in halve_masks:
        span = [(0, 0)]
        for first, second in ring_masks[:2] + masks[::-1]:
            span = span + [(first ^ at, second ^ to) for at, to in span]
        moves.append(span)
    gain = attn_gain[None, :]
    rate = rate_weight.T
    sums = jax.ShapeDtypeStruct((tok_rows, 2 * width), f32)

    arrived = swap(tokens, image_mask)
    q0, k0, v0 = project_qkv(0, image_lengths, head_temp, tokens, gain, qkv_weight)
    a0 = stage(first_stage, [head_temp], [q0, k0, v0], sums, "attend_first")
    fast_blocks = fast_weights.reshape(devices, rows, fast_cols)
    fast_blocks, a0 = lax.optimization_barrier((fast_blocks, a0))
    start = gather_rows(moves, fast_blocks)
    arrived, a0, start = lax.optimization_barrier((arrived, a0, start))
    weights = start.reshape(fast_heads, len(moves[0]) * rows, fast_cols // fast_heads)

    q1, k1, v1 = project_qkv(1, image_lengths, head_temp, arrived, gain, qkv_weight)
    attn = stage(
        last_stage,
        [image_lengths, head_temp],
        [q0, k0, v0, q1, k1, v1, a0],
        jax.ShapeDtypeStruct((2 * tok_rows, width), bf16),
        "attend_last",
    )
    factor = rate_base / (tok_rows * devices)
    tokens_out, after, keys, pushes = first_pushes(
        factor, image_lengths, attn, tokens, arrived, out_weight, kv_weight, rate
    )
    made = [(keys, pushes)]
    sent = [gradient(weights, keys, pushes, 0, 1, bf16)]
    after, sent[0] = lax.optimization_barrier((after, sent[0]))
    got = [swap(sent[0], halve_masks[0][0])]
    made.append(next_pushes(factor, image_lengths, after, kv_weight, rate, 1))
    sent.append(gradient(weights, *made[1], 1, 1, bf16))
    made[1], sent[1], given = lax.optimization_barrier((made[1], sent[1], target))
    got.append(swap(sent[1], halve_masks[1][0]))
    shared = swap(given, share_mask)
    got[0], made[0], made[1] = lax.optimization_barrier((got[0], made[0], made[1]))
    kept = []
    for head in range(fast_heads):
        away, keep = add_step(gradient(weights, *made[head], head, 0, f32), got[head])
        if head == 0:
            away, made[1] = lax.optimization_barrier((away, made[1]))
        kept.append(keep)
        got[head] = swap(away, halve_masks[head][1])
    queries = target_queries(target, shared, query_weight)
    kept[1], queries = lax.optimization_barrier((kept[1], queries))
    own, *pieces = spread(kept[0], got[0], kept[1], got[1])
    fresh, spare = rescale(start, own, [swap(piece, masks) for piece, masks in zip(pieces, ring_masks)])

    collected = collect([spare] + [swap(spare, mask) for mask in ring_masks])
    mine, theirs = [], []
    for head, held in enumerate(collected):
        held = jnp.concatenate([held, swap(held, double_masks[head][0])], axis=0)
        last = swap(held, double_masks[head][1])
        total = apply_first(queries[head], held)
        kept_sum, sent_sum = apply_last(queries[head], last, total)
        mine.append(kept_sum)
        theirs.append(swap(sent_sum, share_mask))
    target_sum = merge_first(target, merge_weight, mine[0], theirs[0])
    target_out = merge_last(target_counts, target_sum, merge_weight, mine[1], theirs[1])
    return (tokens_out, fresh, target_out)


def solution(mesh):
    placed = (
        P(("rep", "tok"), None),
        P(),
        P(),
        P(),
        P(),
        P(),
        P(),
        P(),
        P(("rep", "tok"), None),
        P(),
        P(),
        P("rep"),
        P(("rep", "tok")),
    )
    return jax.shard_map(
        body,
        mesh=mesh,
        in_specs=placed,
        out_specs=(P(("rep", "tok"), None), P(("rep", "tok"), None), P(("rep", "tok"), None)),
        check_vma=False,
    )
```

```python
import functools
import math

import jax
import jax.numpy as jnp
from jax import lax
from jax.experimental import pallas as pl
from jax.experimental.pallas import tpu as pltpu
from jax.sharding import PartitionSpec as P

eps = 1e-06
rate_base = 4.0
safe_temp = 60.0
bf16 = jnp.bfloat16
f32 = jnp.float32

image_mask = (1, 1)
halve_masks = (((3, 8), (4, 24)), ((4, 24), (3, 8)))
ring_masks = ((24, 3), (8, 4), (16, 7))
double_masks = halve_masks
share_mask = (1, 1)


def swap(value, masks):
    reps, places = lax.axis_size("rep"), lax.axis_size("tok")
    pairs = [
        (place * reps + rep, (place ^ masks[rep % 2]) * reps + rep) for place in range(places) for rep in range(reps)
    ]
    return lax.ppermute(value, ("tok", "rep"), pairs)


def params(mib):
    return pltpu.CompilerParams(vmem_limit_bytes=mib * 2**20)


brief = pl.CostEstimate(flops=1, transcendentals=0, bytes_accessed=1)


def nn(a, b):
    return lax.dot_general(a, b, (((1,), (0,)), ((), ())), preferred_element_type=f32)


def nt(a, b):
    return lax.dot_general(a, b, (((1,), (1,)), ((), ())), preferred_element_type=f32)


def whole(shape):
    return pl.BlockSpec(shape, lambda *_: (0,) * len(shape))


smem = pl.BlockSpec(memory_space=pltpu.SMEM)
vmem = pl.BlockSpec(memory_space=pltpu.VMEM)


def valid_rows(lengths_ref, count):
    place = lax.axis_index("tok")
    length = lengths_ref[lax.shift_right_logical(place, 1)]
    parity = lax.bitwise_and(place, 1)
    return length - parity * count, length - (1 - parity) * count


def gather_kernel(moves, rows_ref, out_ref):
    place = lax.axis_index("tok")
    core = lax.bitwise_and(lax.axis_index("rep"), 1)
    cols = out_ref.shape[-1]
    for head, span in enumerate(moves):
        for block, (mask, other) in enumerate(span):
            owner = lax.bitwise_xor(place, mask + core * (other - mask))
            out_ref[head, block] = rows_ref[owner, :, head * cols : head * cols + cols]


def gather_rows(moves, rows):
    _, height, width = rows.shape
    heads = len(moves)
    return pl.pallas_call(
        functools.partial(gather_kernel, moves),
        out_shape=jax.ShapeDtypeStruct((heads, len(moves[0]), height, width // heads), rows.dtype),
        in_specs=[vmem],
        out_specs=vmem,
        compiler_params=params(4),
        cost_estimate=brief,
        name="gather_rows",
    )(rows)


def qkv_kernel(side, lengths_ref, temp_ref, gain_ref, tok_ref, w_ref, q_ref, k_ref, v_ref, normed):
    count, width = normed.shape
    cols = 256
    x = tok_ref[...].astype(f32)
    unit = x * lax.rsqrt(jnp.mean(x * x, axis=-1, keepdims=True) + eps)
    normed[...] = (unit * gain_ref[...].astype(f32)).astype(bf16)
    shown_rows = valid_rows(lengths_ref, count)[side]
    low = lax.broadcasted_iota(jnp.int32, (count, 128), 1) < 64
    live = lax.broadcasted_iota(jnp.int32, (count, 128), 0) < shown_rows
    one = jnp.where(live, 1.0, 0.0)

    def unit_heads(t):
        square = t * t
        first = jnp.sum(jnp.where(low, square, 0.0), axis=-1, keepdims=True)
        second = jnp.sum(jnp.where(low, 0.0, square), axis=-1, keepdims=True)
        inv = [lax.rsqrt(total * (1.0 / 64.0) + eps) for total in (first, second)]
        return (t * jnp.where(low, inv[0], inv[1])).astype(bf16).astype(f32)

    for group in range(0, width, cols):
        rows = normed[...]
        query, key, value = (nn(rows, w_ref[:, at + group : at + group + cols]) for at in (0, width, 2 * width))
        query = query.astype(bf16).astype(f32)
        key = key.astype(bf16).astype(f32)
        for tile in range(0, cols, 128):
            part = slice(tile, tile + 128)
            head = (group + tile) // 64
            even = slice(head * 128, head * 128 + 128)
            odd = slice(head * 128 + 128, head * 128 + 256)
            scale = jnp.where(low, temp_ref[head], temp_ref[head + 1]) * (math.log2(math.e) / 64.0)
            q = unit_heads(query[:, part]) * scale
            q_high = q.astype(bf16).astype(f32)
            moved = pltpu.roll(q - q_high, 64, 1)
            q_ref[:, even] = jnp.where(low, q_high, moved).astype(bf16)
            q_ref[:, odd] = jnp.where(low, moved, q_high).astype(bf16)
            k = unit_heads(key[:, part])
            moved = pltpu.roll(k, 64, 1)
            k_ref[:, even] = jnp.where(low, k, moved).astype(bf16)
            k_ref[:, odd] = jnp.where(low, moved, k).astype(bf16)
            shown = jnp.where(live, value[:, part], 0.0)
            v_ref[:, even] = jnp.where(low, shown, one).astype(bf16)
            v_ref[:, odd] = jnp.where(low, one, shown).astype(bf16)


def project_qkv(side, lengths, temps, tokens, gain, weight):
    count, width = tokens.shape
    out = jax.ShapeDtypeStruct((count, 2 * width), bf16)
    return pl.pallas_call(
        functools.partial(qkv_kernel, side),
        out_shape=(out, out, out),
        in_specs=[smem, smem] + [vmem] * 3,
        out_specs=[vmem] * 3,
        scratch_shapes=[pltpu.VMEM((count, width), bf16)],
        compiler_params=params(8),
        cost_estimate=brief,
        name="project_qkv",
    )(lengths, temps, gain, tokens, weight)


def weighted(q, keys, values, lanes):
    total = None
    for k_ref, v_ref in zip(keys, values):
        part = nn(jnp.exp2(nt(q, k_ref[:, lanes])).astype(bf16), v_ref[:, lanes])
        total = part if total is None else total + part
    return total


def finish(sums, out_ref, start, pair):
    count = sums[0].shape[0]
    low = lax.broadcasted_iota(jnp.int32, (count, 128), 1) < 64
    top = jnp.where(low, sums[0], sums[1])
    bottom = pltpu.roll(jnp.where(low, sums[1], sums[0]), 64, 1)
    out_ref[pl.ds(start, count), pl.ds(pl.multiple_of(pair * 128, 128), 128)] = (top / bottom).astype(bf16)


def pairs_of_heads(temp_ref, width, plain, other=None):
    def lanes_of(pair):
        return [pl.ds(pl.multiple_of(pair * 256 + head * 128, 128), 128) for head in range(2)]

    def is_safe(pair):
        return jnp.maximum(temp_ref[2 * pair], temp_ref[2 * pair + 1]) <= safe_temp

    def two_pairs(step, _):
        first, second = 2 * step, 2 * step + 1
        both = jnp.logical_and(is_safe(first), is_safe(second))

        @pl.when(both)
        def _():
            plain(first, lanes_of(first))
            plain(second, lanes_of(second))

        @pl.when(jnp.logical_not(both))
        def _():
            def one_pair(pair, _):
                if other is not None:
                    other(pair, lanes_of(pair))
                return 0

            lax.fori_loop(first, first + 2, one_pair, 0)

        return 0

    lax.fori_loop(0, width // 512, two_pairs, 0)


def first_stage(temp_ref, q0, k0, v0, a0):
    def plain(pair, heads):
        for lanes in heads:
            a0[:, lanes] = weighted(q0[:, lanes], [k0], [v0], lanes)

    pairs_of_heads(temp_ref, q0.shape[1], plain)


def last_stage(lengths_ref, temp_ref, q0, k0, v0, q1, k1, v1, a0, out_ref):
    count = q0.shape[0]
    keys, values = [k0, k1], [v0, v1]
    valid = valid_rows(lengths_ref, count)

    def plain(pair, heads):
        finish([a0[:, lanes] + weighted(q0[:, lanes], [k1], [v1], lanes) for lanes in heads], out_ref, 0, pair)
        finish([weighted(q1[:, lanes], keys, values, lanes) for lanes in heads], out_ref, count, pair)

    def other(pair, heads):
        block = 128
        for q_ref, start in zip((q0, q1), (0, count)):

            def some_rows(step, _):
                first = pl.multiple_of(step * block, block)
                sums = []
                for lanes in heads:
                    scores = []
                    for at, k_ref in enumerate(keys):
                        score = nt(q_ref[pl.ds(first, block), lanes], k_ref[:, lanes])
                        spot = lax.broadcasted_iota(jnp.int32, score.shape, 1)
                        scores.append(jnp.where(spot < valid[at], score, -1e30))
                    tops = [jnp.max(score, axis=-1, keepdims=True) for score in scores]
                    top = functools.reduce(jnp.maximum, tops)
                    total = 0.0
                    for score, v_ref in zip(scores, values):
                        total = total + nn(jnp.exp2(score - top).astype(bf16), v_ref[:, lanes])
                    sums.append(total)
                finish(sums, out_ref, pl.multiple_of(start + first, block), pair)
                return 0

            lax.fori_loop(0, count // block, some_rows, 0)

    pairs_of_heads(temp_ref, q0.shape[1], plain, other)


def stage(kernel, scalars, arrays, outs, name):
    return pl.pallas_call(
        kernel,
        out_shape=outs,
        in_specs=[smem] * len(scalars) + [vmem] * len(arrays),
        out_specs=jax.tree.map(lambda out: vmem, outs),
        compiler_params=params(8),
        cost_estimate=brief,
        name=name,
    )(*scalars, *arrays)


def push_rows(scale, shown, after, wkv_ref, r_ref, head, key_ref, push_ref, rows):
    size = key_ref.shape[1]
    width = wkv_ref.shape[1] // 2
    exact, pieces = r_ref[...], []
    for _ in range(3):
        pieces.append(exact.astype(bf16).astype(f32))
        exact = exact - pieces[-1]
    heads = exact.shape[0]
    parts = nt(after, jnp.concatenate(pieces, axis=0).astype(bf16))
    high = sum(parts[:, at * heads + head : at * heads + head + 1] for at in range(3)) + 1.0
    soft = jnp.maximum(high, 0.0) + jnp.log1p(jnp.exp(-jnp.abs(high)))
    spot = lax.broadcasted_iota(jnp.int32, high.shape, 0)
    rate = jnp.where(spot < shown, soft * scale, 0.0)
    key = nn(after, wkv_ref[:, head * size : head * size + size])
    key_ref[rows, :] = (key * lax.rsqrt(jnp.mean(key * key, axis=-1, keepdims=True) + eps)).astype(bf16)
    value = nn(after, wkv_ref[:, width + head * size : width + head * size + size])
    push_ref[rows, :] = (-rate * value).astype(bf16)


def out_kernel(scale, lengths_ref, attn_ref, t0, t1, wo_ref, wkv_ref, r_ref, out_ref, after_ref, key_ref, push_ref):
    count = t0.shape[0]
    valid = valid_rows(lengths_ref, count)
    for side, tok_ref in enumerate((t0, t1)):
        rows = slice(side * count, side * count + count)
        after = (tok_ref[...].astype(f32) + nn(attn_ref[rows, :], wo_ref[...])).astype(bf16)
        after_ref[rows, :] = after
        if side == 0:
            out_ref[...] = after
        push_rows(scale, valid[side], after, wkv_ref, r_ref, 0, key_ref, push_ref, rows)


def again_kernel(scale, head, lengths_ref, after_ref, wkv_ref, r_ref, key_ref, push_ref):
    half = after_ref.shape[0] // 2
    valid = valid_rows(lengths_ref, half)
    for side in range(2):
        rows = slice(side * half, side * half + half)
        push_rows(scale, valid[side], after_ref[rows, :], wkv_ref, r_ref, head, key_ref, push_ref, rows)


def first_pushes(scale, lengths, attn, t0, t1, wo, wkv, rate):
    count, width = t0.shape
    both = jax.ShapeDtypeStruct((2 * count, width // rate.shape[0]), bf16)
    return pl.pallas_call(
        functools.partial(out_kernel, scale),
        out_shape=(
            jax.ShapeDtypeStruct((count, width), bf16),
            jax.ShapeDtypeStruct((2 * count, width), bf16),
            both,
            both,
        ),
        in_specs=[smem] + [vmem] * 6,
        out_specs=[vmem] * 4,
        compiler_params=params(12),
        cost_estimate=brief,
        name="first_pushes",
    )(lengths, attn, t0, t1, wo, wkv, rate)


def next_pushes(scale, lengths, after, wkv, rate, head):
    rows, width = after.shape
    both = jax.ShapeDtypeStruct((rows, width // rate.shape[0]), bf16)
    return pl.pallas_call(
        functools.partial(again_kernel, scale, head),
        out_shape=(both, both),
        in_specs=[smem] + [vmem] * 3,
        out_specs=[vmem] * 2,
        compiler_params=params(12),
        cost_estimate=brief,
        name="next_pushes",
    )(lengths, after, wkv, rate)


def grad_kernel(head, half, w_ref, key_ref, push_ref, out_ref):
    count, size = out_ref.shape[0], key_ref.shape[1]
    key, push = key_ref[...], push_ref[...]
    w = w_ref[head, half * count : half * count + count, :]
    act_a = nt(w[:, :size], key)
    act_b = nt(w[:, size : 2 * size], key)
    back = nt(w[:, 2 * size :], push)
    sigma = 1.0 / (1.0 + jnp.exp(-act_a))
    silu = act_a * sigma
    hidden = (silu * act_b).astype(bf16)
    grad_a = (back * act_b * sigma * (1.0 + act_a * (1.0 - sigma))).astype(bf16)
    grad_b = (back * silu).astype(bf16)
    out_ref[:, :size] = nn(grad_a, key).astype(out_ref.dtype)
    out_ref[:, size : 2 * size] = nn(grad_b, key).astype(out_ref.dtype)
    out_ref[:, 2 * size :] = nn(hidden, push).astype(out_ref.dtype)


def gradient(weights, keys, pushes, head, half, kind):
    _, rows, cols = weights.shape
    return pl.pallas_call(
        functools.partial(grad_kernel, head, half),
        out_shape=jax.ShapeDtypeStruct((rows // 2, cols), kind),
        in_specs=[vmem] * 3,
        out_specs=vmem,
        compiler_params=params(12),
        cost_estimate=brief,
        name="gradient",
    )(weights, keys, pushes)


def add_kernel(kept_ref, got_ref, sent_ref, keep_ref):
    half = keep_ref.shape[0]
    sent_ref[...] = (kept_ref[half:, :] + got_ref[half:, :].astype(f32)).astype(bf16)
    keep_ref[...] = kept_ref[:half, :] + got_ref[:half, :].astype(f32)


def add_step(kept, got):
    half = (kept.shape[0] // 2, kept.shape[1])
    return pl.pallas_call(
        add_kernel,
        out_shape=(jax.ShapeDtypeStruct(half, bf16), jax.ShapeDtypeStruct(half, f32)),
        in_specs=[vmem] * 2,
        out_specs=[vmem] * 2,
        compiler_params=params(4),
        cost_estimate=brief,
        name="add_step",
    )(kept, got)


def spread_kernel(k0_ref, g0_ref, k1_ref, g1_ref, own_ref, *sent_refs):
    rows, cols = own_ref.shape[0], k0_ref.shape[1]
    for head, (kept_ref, got_ref) in enumerate(((k0_ref, g0_ref), (k1_ref, g1_ref))):
        total = kept_ref[...] + got_ref[...].astype(f32)
        part = slice(head * cols, head * cols + cols)
        own_ref[:, part] = total[:rows]
        for at, sent_ref in enumerate(sent_refs):
            sent_ref[:, part] = total[(at + 1) * rows : (at + 2) * rows].astype(bf16)


def spread(k0, g0, k1, g1):
    shape = (k0.shape[0] // 4, 2 * k0.shape[1])
    kinds = (f32, bf16, bf16, bf16)
    return pl.pallas_call(
        spread_kernel,
        out_shape=tuple(jax.ShapeDtypeStruct(shape, kind) for kind in kinds),
        in_specs=[vmem] * 4,
        out_specs=[vmem] * 4,
        compiler_params=params(4),
        cost_estimate=brief,
        name="spread",
    )(k0, g0, k1, g1)


def rescale_kernel(start_ref, own_ref, a_ref, b_ref, c_ref, out_ref, sent_ref):
    heads, cols = start_ref.shape[0], start_ref.shape[3]
    size = cols // 3
    for head in range(heads):
        for block in range(3):
            part = slice(head * cols + block * size, head * cols + block * size + size)
            grad = own_ref[:, part]
            for got_ref in (a_ref, b_ref, c_ref):
                grad = grad + got_ref[:, part].astype(f32)
            start = start_ref[head, 0, :, block * size : block * size + size].astype(f32)
            update = start - grad
            before = jnp.sqrt(jnp.mean(start * start, axis=-1, keepdims=True) + eps)
            after = lax.rsqrt(jnp.mean(update * update, axis=-1, keepdims=True) + eps)
            fresh = (update * before * after).astype(bf16)
            out_ref[:, part] = fresh
            sent_ref[:, part] = fresh


def rescale(start, own, got):
    out = jax.ShapeDtypeStruct(own.shape, bf16)
    return pl.pallas_call(
        rescale_kernel,
        out_shape=(out, out),
        in_specs=[vmem] * 5,
        out_specs=[vmem] * 2,
        compiler_params=params(4),
        cost_estimate=brief,
        name="rescale",
    )(start, own, *got)


def collect_kernel(a_ref, b_ref, c_ref, d_ref, h0_ref, h1_ref):
    cols = h0_ref.shape[2]
    for at, got_ref in enumerate((a_ref, b_ref, c_ref, d_ref)):
        h0_ref[at] = got_ref[:, :cols]
        h1_ref[at] = got_ref[:, cols:]


def collect(blocks):
    rows, cols = blocks[0].shape
    out = jax.ShapeDtypeStruct((len(blocks), rows, cols // 2), bf16)
    held = pl.pallas_call(
        collect_kernel,
        out_shape=(out, out),
        in_specs=[vmem] * 4,
        out_specs=[vmem] * 2,
        compiler_params=params(4),
        cost_estimate=brief,
        name="collect",
    )(*blocks)
    return [part.reshape(len(blocks) * rows, cols // 2) for part in held]


def query_kernel(t_ref, s_ref, w_ref, q0_ref, q1_ref):
    count = t_ref.shape[0]
    size = q0_ref.shape[1]
    for side, rows_ref in enumerate((t_ref, s_ref)):
        tq = nn(rows_ref[...], w_ref[...])
        for head, q_ref in enumerate((q0_ref, q1_ref)):
            q = tq[:, head * size : head * size + size]
            unit = q * lax.rsqrt(jnp.mean(q * q, axis=-1, keepdims=True) + eps)
            q_ref[side * count : side * count + count, :] = unit.astype(bf16)


def target_queries(target, shared, weight):
    count, width = target.shape
    out = jax.ShapeDtypeStruct((2 * count, width // 2), bf16)
    return pl.pallas_call(
        query_kernel,
        out_shape=(out, out),
        in_specs=[vmem] * 3,
        out_specs=[vmem] * 2,
        compiler_params=params(8),
        cost_estimate=brief,
        name="target_queries",
    )(target, shared, weight)


def apply_rows(q, w_ref):
    size = q.shape[1]
    act_a = nt(q, w_ref[:, :size])
    act_b = nt(q, w_ref[:, size : 2 * size])
    hidden = (act_a / (1.0 + jnp.exp(-act_a)) * act_b).astype(bf16)
    return nn(hidden, w_ref[:, 2 * size :])


def first_kernel(q_ref, w_ref, out_ref):
    out_ref[...] = apply_rows(q_ref[...], w_ref)


def apply_first(queries, weights):
    return pl.pallas_call(
        first_kernel,
        out_shape=jax.ShapeDtypeStruct((queries.shape[0], weights.shape[1] // 3), f32),
        in_specs=[vmem] * 2,
        out_specs=vmem,
        compiler_params=params(8),
        cost_estimate=brief,
        name="apply_first",
    )(queries, weights)


def last_kernel(q_ref, w_ref, sum_ref, mine_ref, theirs_ref):
    count = mine_ref.shape[0]
    total = sum_ref[...] + apply_rows(q_ref[...], w_ref)
    mine_ref[...] = total[:count]
    theirs_ref[...] = total[count:].astype(bf16)


def apply_last(queries, weights, total):
    half = (total.shape[0] // 2, total.shape[1])
    return pl.pallas_call(
        last_kernel,
        out_shape=(jax.ShapeDtypeStruct(half, f32), jax.ShapeDtypeStruct(half, bf16)),
        in_specs=[vmem] * 3,
        out_specs=[vmem] * 2,
        compiler_params=params(8),
        cost_estimate=brief,
        name="apply_last",
    )(queries, weights, total)


def merge_kernel(target_ref, w_ref, mine_ref, theirs_ref, out_ref):
    size = mine_ref.shape[1]
    fout = mine_ref[...] + theirs_ref[...].astype(f32)
    unit = (fout * lax.rsqrt(jnp.mean(fout * fout, axis=-1, keepdims=True) + eps)).astype(bf16)
    out_ref[...] = target_ref[...].astype(f32) + nn(unit, w_ref[:size, :])


def merge_first(target, weight, mine, theirs):
    return pl.pallas_call(
        merge_kernel,
        out_shape=jax.ShapeDtypeStruct(target.shape, f32),
        in_specs=[vmem] * 4,
        out_specs=vmem,
        compiler_params=params(8),
        cost_estimate=brief,
        name="merge_first",
    )(target, weight, mine, theirs)


def merge_last_kernel(used_ref, sum_ref, w_ref, mine_ref, theirs_ref, out_ref):
    size = mine_ref.shape[1]
    fout = mine_ref[...] + theirs_ref[...].astype(f32)
    unit = (fout * lax.rsqrt(jnp.mean(fout * fout, axis=-1, keepdims=True) + eps)).astype(bf16)
    total = sum_ref[...] + nn(unit, w_ref[size:, :])
    live = lax.broadcasted_iota(jnp.int32, total.shape, 0) < used_ref[0]
    out_ref[...] = jnp.where(live, total, 0.0).astype(bf16)


def merge_last(used, total, weight, mine, theirs):
    return pl.pallas_call(
        merge_last_kernel,
        out_shape=jax.ShapeDtypeStruct(total.shape, bf16),
        in_specs=[smem] + [vmem] * 4,
        out_specs=vmem,
        compiler_params=params(8),
        cost_estimate=brief,
        name="merge_last",
    )(used, total, weight, mine, theirs)


def body(
    tokens,
    attn_gain,
    qkv_weight,
    head_temp,
    out_weight,
    kv_weight,
    rate_weight,
    fast_weights,
    target,
    query_weight,
    merge_weight,
    image_lengths,
    target_counts,
):
    tok_rows, width = tokens.shape
    devices = lax.axis_size("tok")
    fast_hidden, fast_cols = fast_weights.shape
    fast_heads = rate_weight.shape[1]
    rows = fast_hidden // devices
    moves = []
    for masks in halve_masks:
        span = [(0, 0)]
        for first, second in ring_masks[:2] + masks[::-1]:
            span = span + [(first ^ at, second ^ to) for at, to in span]
        moves.append(span)
    gain = attn_gain[None, :]
    rate = rate_weight.T
    sums = jax.ShapeDtypeStruct((tok_rows, 2 * width), f32)

    arrived = swap(tokens, image_mask)
    q0, k0, v0 = project_qkv(0, image_lengths, head_temp, tokens, gain, qkv_weight)
    a0 = stage(first_stage, [head_temp], [q0, k0, v0], sums, "attend_first")
    fast_blocks = fast_weights.reshape(devices, rows, fast_cols)
    fast_blocks, a0 = lax.optimization_barrier((fast_blocks, a0))
    start = gather_rows(moves, fast_blocks)
    arrived, a0, start = lax.optimization_barrier((arrived, a0, start))
    weights = start.reshape(fast_heads, len(moves[0]) * rows, fast_cols // fast_heads)

    q1, k1, v1 = project_qkv(1, image_lengths, head_temp, arrived, gain, qkv_weight)
    attn = stage(
        last_stage,
        [image_lengths, head_temp],
        [q0, k0, v0, q1, k1, v1, a0],
        jax.ShapeDtypeStruct((2 * tok_rows, width), bf16),
        "attend_last",
    )
    factor = rate_base / (tok_rows * devices)
    tokens_out, after, keys, pushes = first_pushes(
        factor, image_lengths, attn, tokens, arrived, out_weight, kv_weight, rate
    )
    made = [(keys, pushes)]
    sent = [gradient(weights, keys, pushes, 0, 1, bf16)]
    after, sent[0] = lax.optimization_barrier((after, sent[0]))
    got = [swap(sent[0], halve_masks[0][0])]
    made.append(next_pushes(factor, image_lengths, after, kv_weight, rate, 1))
    sent.append(gradient(weights, *made[1], 1, 1, bf16))
    made[1], sent[1], given = lax.optimization_barrier((made[1], sent[1], target))
    got.append(swap(sent[1], halve_masks[1][0]))
    shared = swap(given, share_mask)
    got[0], made[0], made[1] = lax.optimization_barrier((got[0], made[0], made[1]))
    kept = []
    for head in range(fast_heads):
        away, keep = add_step(gradient(weights, *made[head], head, 0, f32), got[head])
        if head == 0:
            away, made[1] = lax.optimization_barrier((away, made[1]))
        kept.append(keep)
        got[head] = swap(away, halve_masks[head][1])
    queries = target_queries(target, shared, query_weight)
    kept[1], queries = lax.optimization_barrier((kept[1], queries))
    own, *pieces = spread(kept[0], got[0], kept[1], got[1])
    fresh, spare = rescale(start, own, [swap(piece, masks) for piece, masks in zip(pieces[::-1], ring_masks[::-1])])

    collected = collect([spare] + [swap(spare, mask) for mask in ring_masks[::-1]])
    mine, theirs = [], []
    for head, held in enumerate(collected):
        held = jnp.concatenate([held, swap(held, double_masks[head][0])], axis=0)
        last = swap(held, double_masks[head][1])
        total = apply_first(queries[head], held)
        kept_sum, sent_sum = apply_last(queries[head], last, total)
        mine.append(kept_sum)
        theirs.append(swap(sent_sum, share_mask))
    target_sum = merge_first(target, merge_weight, mine[0], theirs[0])
    target_out = merge_last(target_counts, target_sum, merge_weight, mine[1], theirs[1])
    return (tokens_out, fresh, target_out)


def solution(mesh):
    placed = (
        P(("rep", "tok"), None),
        P(),
        P(),
        P(),
        P(),
        P(),
        P(),
        P(),
        P(("rep", "tok"), None),
        P(),
        P(),
        P("rep"),
        P(("rep", "tok")),
    )
    return jax.shard_map(
        body,
        mesh=mesh,
        in_specs=placed,
        out_specs=(P(("rep", "tok"), None), P(("rep", "tok"), None), P(("rep", "tok"), None)),
        check_vma=False,
    )
```
